32 devices in a mesh: seq: 32 (over z, y, x, core).
Axes of the slice: x: 2, y: 2, z: 4, core: 2. Of those that a mesh axis runs over, the one named last changes fastest.
Arguments:
- hidden: bfloat16 [4096, 768], P('seq'), may hold values from -6 to 6
- condition: float32 [6, 768], replicated, may hold values from -6 to 6
- seq_lengths: int32 [6], replicated, may hold values from 1 to 4032, as said below
- w_mod: bfloat16 [768, 2304], replicated, may hold values from -0.21875 to 0.21875
- b_mod: float32 [2304], replicated, may hold values from -2 to 2
- w_in: bfloat16 [768, 3072], replicated, may hold values from -0.21875 to 0.21875
- conv_w: float32 [2, 4, 1536], replicated, may hold values from -3 to 3
- conv_b: float32 [2, 1536], replicated, may hold values from -0.5 to 0.5
- w_x: bfloat16 [2, 1536, 80], replicated, may hold values from -0.15625 to 0.15625
- w_dt: bfloat16 [2, 48, 1536], replicated, may hold values from -0.875 to 0.875
- dt_bias: float32 [2, 1536], replicated, may hold values from -6.5 to -2.3
- a_log: float32 [2, 16, 1536], replicated, may hold values from -9 to 1
- d_skip: float32 [2, 1536], replicated, may hold values from 0.5 to 1.5
- w_out: bfloat16 [1536, 768], replicated, may hold values from -0.4375 to 0.4375
- grad_out: bfloat16 [4096, 768], P('seq'), may hold values from -6 to 6
Outputs:
- output: bfloat16 [4096, 768], P('seq')
- grad_hidden: float32 [4096, 768], P('seq')
- grad_w_mod: float32 [768, 2304], P('seq')
- grad_b_mod: float32 [2304], P('seq')
- grad_w_in: float32 [768, 3072], P('seq')
- grad_conv_w: float32 [2, 4, 1536], P(None, None, 'seq')
- grad_conv_b: float32 [2, 1536], P(None, 'seq')
- grad_w_x: float32 [2, 1536, 80], P(None, 'seq')
- grad_w_dt: float32 [2, 48, 1536], P(None, None, 'seq')
- grad_dt_bias: float32 [2, 1536], P(None, 'seq')
- grad_a_log: float32 [2, 16, 1536], P(None, None, 'seq')
- grad_d_skip: float32 [2, 1536], P(None, 'seq')
- grad_w_out: float32 [1536, 768], P('seq')
The draws below stay inside these ranges and needn't reach their ends.
Inputs may be any that keep to these rules, and one draw needn't show every extreme that they name: `seq_lengths`: the sequences lie one after another from token 0 and are followed by one or more padding tokens. One of them, which one varies, is a high-resolution image's patch tokens with 4032 tokens; each other one has at most (63) // 5.
All inputs are finite; a program needn't handle non-finite values.
Results may differ from the reference program's by a relative error of at most 0.0097.
Values may be sent and summed in bfloat16 or wider, within the bound.
A program may use at most 192 MiB of HBM per device.

```python
import jax
import jax.numpy as jnp
from jax import lax

D = 768
INNER = 1536
STATE = 16
RANK = 48
KCONV = 4
TOK_DEV = 128
SEQS = 6
TOKENS = 4096
PROJ = 80


def fast_channels(key):
    picks = jax.random.randint(jax.random.fold_in(key, 11), (2, INNER), 0, 2)
    return picks == 1


def draw_seq_lengths(key, part):
    key_short, key_pick = jax.random.split(jax.random.fold_in(key, 7))
    short_most = (TOK_DEV // 2 - 1) // (SEQS - 1)
    shorts = jax.random.randint(key_short, (SEQS,), 1, short_most + 1)
    picked = jax.random.randint(key_pick, (), 0, SEQS)
    longest = TOKENS - TOK_DEV // 2
    return jnp.where(jnp.arange(SEQS) == picked, longest, shorts).astype(jnp.int32)


def draw_dt_bias(key, part):
    fast = fast_channels(key)
    key = jax.random.fold_in(key, 5)
    spread = jax.random.uniform(key, (2, INNER), jnp.float32)
    return jnp.where(fast, -3.0 + 0.7 * spread, -6.5 + spread).astype(jnp.float32)


def draw_a_log(key, part):
    fast = fast_channels(key)
    key = jax.random.fold_in(key, 3)
    spread = jax.random.uniform(key, (2, STATE, INNER), jnp.float32)
    slow_value = jnp.log(jnp.float32(5.0) / jnp.float32(TOKENS)) + jnp.log(jnp.float32(40.0)) * spread
    fast_value = -1.0 + 2.0 * spread
    return jnp.where(fast[:, None, :], fast_value, slow_value).astype(jnp.float32)


def block_scale(own_key, extent, cuts, least, high):
    def one(axis_at, shards_of):
        draws = jax.random.uniform(jax.random.fold_in(jax.random.fold_in(own_key, 6), axis_at), (shards_of,), jnp.float32, least / len(cuts), high / len(cuts))
        return jnp.repeat(jnp.exp(draws), extent[axis_at] // shards_of).reshape((-1,) + (1,) * (len(extent) - axis_at - 1))

    loudness = one(*cuts[0])
    for cut in cuts[1:]:
        loudness = loudness * one(*cut)
    return loudness


def bell_draw(key, shape, scale, most, pieces=(), kind=jnp.bfloat16):
    result = scale * jax.random.normal(key, shape, jnp.float32)
    if pieces:
        result = result * block_scale(key, shape, pieces, -0.22, 0.18)
    return jnp.clip(result, -most, most).astype(kind)


def setup_inputs(seed: int = 0) -> dict:
    splits = jax.random.split(jax.random.key(seed), 16)
    hidden = bell_draw(splits[0], (TOKENS, D), 1.0, 6.0, ((0, 32),))
    condition = bell_draw(splits[1], (SEQS, D), 1.0, 6.0, (), jnp.float32)
    seq_lengths = draw_seq_lengths(jax.random.fold_in(splits[15], 71), 0)
    w_mod = bell_draw(splits[3], (D, 3 * D), D ** -0.5, 0.21875)
    b_mod = bell_draw(splits[4], (3 * D,), 0.3, 2.0, (), jnp.float32)
    w_in = bell_draw(splits[5], (D, 2 * INNER), D ** -0.5, 0.21875)
    conv_w = bell_draw(splits[6], (2, KCONV, INNER), KCONV ** -0.5, 3.0, (), jnp.float32)
    conv_b = jnp.clip(jax.random.uniform(splits[7], (2, INNER), jnp.float32, -0.5, 0.5), -0.5, 0.5)
    w_x = bell_draw(splits[8], (2, INNER, PROJ), INNER ** -0.5, 0.15625)
    w_dt = bell_draw(splits[9], (2, RANK, INNER), RANK ** -0.5, 0.875)
    dt_bias = draw_dt_bias(jax.random.fold_in(splits[15], 71), 0)
    a_log = draw_a_log(jax.random.fold_in(splits[15], 71), 0)
    d_skip = jnp.clip(jax.random.uniform(splits[12], (2, INNER), jnp.float32, 0.5, 1.5), 0.5, 1.5)
    w_out = bell_draw(splits[13], (INNER, D), (INNER // 8) ** -0.5, 0.4375)
    grad_out = bell_draw(splits[14], (TOKENS, D), 1.0, 6.0, ((0, 32),))
    return dict(hidden=hidden, condition=condition, seq_lengths=seq_lengths, w_mod=w_mod, b_mod=b_mod, w_in=w_in, conv_w=conv_w, conv_b=conv_b, w_x=w_x, w_dt=w_dt, dt_bias=dt_bias, a_log=a_log, d_skip=d_skip, w_out=w_out, grad_out=grad_out)


@jax.custom_vjp
def low(v):
    return lax.optimization_barrier(v.astype(jnp.bfloat16)).astype(jnp.float32)

@jax.custom_vjp
def low_back(v):
    return v

def low_keep(v):
    return (low(v), None)

def low_pass(kept, grad):
    return (grad,)

def back_keep(v):
    return (v, None)

def back_low(kept, grad):
    return (low(grad),)
low.defvjp(low_keep, low_pass)
low_back.defvjp(back_keep, back_low)
EPSILON = 1e-06
HIGHEST = lax.Precision.HIGHEST

def matmul(left, right):
    return jnp.dot(left, right, precision=HIGHEST, preferred_element_type=jnp.float32)

def segment_ids(positions, bounds):
    return lax.optimization_barrier(jnp.sum((positions[:, None] >= bounds[None, :]).astype(jnp.int32), axis=1)) - 1

def shifted(values, offset):
    if offset == 0:
        return values
    padding = jnp.zeros((abs(offset), values.shape[1]), values.dtype)
    if offset > 0:
        return jnp.concatenate([values[offset:], padding], axis=0)
    return jnp.concatenate([padding, values[:offset]], axis=0)

def run_scan(step_size, active, in_coef, out_coef, rate, keep):
    length = step_size.shape[0]
    block_len = 64 if length % 64 == 0 else length

    def scan_step(state, row_data):
        step_row, act_row, in_row, out_row, keep_row = row_data
        state = keep_row * jnp.exp(step_row[None, :] * rate) * state + in_row[:, None] * (step_row * act_row)[None, :]
        return (state, lax.optimization_barrier(jnp.sum(out_row[:, None] * state, axis=0)))

    def run_block(state, row_blocks):
        return lax.scan(scan_step, state, row_blocks)
    row_blocks = tuple((r.reshape((length // block_len, block_len) + r.shape[1:]) for r in (step_size, active, in_coef, out_coef, keep)))
    zero_state = jnp.zeros(rate.shape, jnp.float32)
    _, outputs = lax.scan(jax.checkpoint(run_block), zero_state, row_blocks)
    return outputs.reshape(length, rate.shape[1])

def reference(hidden, condition, seq_lengths, w_mod, b_mod, w_in, conv_w, conv_b, w_x, w_dt, dt_bias, a_log, d_skip, w_out, grad_out):
    seq_count = condition.shape[0]
    n_tok = hidden.shape[0]
    model_width = hidden.shape[1]
    inner_width = w_in.shape[1] // 2
    rank_width = w_dt.shape[1]
    states = a_log.shape[1]
    kernel = conv_w.shape[1]
    positions = jnp.arange(n_tok, dtype=jnp.int32)
    bounds = jnp.concatenate([jnp.zeros((1,), jnp.int32), jnp.cumsum(seq_lengths).astype(jnp.int32)])
    segment = segment_ids(positions, bounds)
    keep_forward = (segment_ids(positions - 1, bounds) == segment).astype(jnp.float32)
    keep_reverse = (segment_ids(positions + 1, bounds) == segment).astype(jnp.float32)
    onehot = (segment[:, None] == jnp.arange(seq_count, dtype=jnp.int32)[None, :]).astype(jnp.float32)
    same_seg = {}
    for offset in range(-(kernel - 1), kernel):
        same_seg[offset] = (segment_ids(positions + offset, bounds) == segment).astype(jnp.float32)[:, None]
    cond_act = low(jax.nn.silu(condition))

    def forward(x_float, wm, bm, wi, cw, cb, wx, wd, db, al, ds, wo):
        modulation = matmul(cond_act, wm) + bm
        mod_rows = matmul(onehot, modulation)
        shift_rows = mod_rows[:, :model_width]
        scale_rows = mod_rows[:, model_width:2 * model_width]
        gate_rows = mod_rows[:, 2 * model_width:]
        row_mean = lax.optimization_barrier(jnp.mean(x_float, axis=1, keepdims=True))
        centered = x_float - row_mean
        normed = centered * lax.rsqrt(lax.optimization_barrier(jnp.mean(centered * centered, axis=1, keepdims=True)) + EPSILON)
        mixer_in = low(normed * (1.0 + scale_rows) + shift_rows)
        projected = low_back(matmul(mixer_in, wi))
        conv_input = low(projected[:, :inner_width])
        gate_branch = projected[:, inner_width:]
        mixed = jnp.zeros((n_tok, inner_width), jnp.float32)
        for direction in range(2):
            conv_sum = cb[direction][None, :]
            for tap_idx in range(kernel):
                offset = tap_idx - (kernel - 1) if direction == 0 else kernel - 1 - tap_idx
                conv_sum = conv_sum + cw[direction, tap_idx][None, :] * shifted(conv_input, offset) * same_seg[offset]
            active = low(jax.nn.silu(conv_sum))
            projection = low_back(matmul(active, wx[direction]))
            rank_low = low(projection[:, :rank_width])
            in_coef = projection[:, rank_width:rank_width + states]
            out_coef = projection[:, rank_width + states:]
            step_size = jax.nn.softplus(low_back(matmul(rank_low, wd[direction])) + db[direction][None, :])
            rate = -jnp.exp(al[direction])
            if direction == 0:
                scanned = run_scan(step_size, active, in_coef, out_coef, rate, keep_forward)
            else:
                scanned = jnp.flip(run_scan(jnp.flip(step_size, 0), jnp.flip(active, 0), jnp.flip(in_coef, 0), jnp.flip(out_coef, 0), rate, jnp.flip(keep_reverse, 0)), 0)
            mixed = mixed + scanned + ds[direction][None, :] * active
        gated = low(mixed * jax.nn.silu(gate_branch))
        branch = low_back(matmul(gated, wo))
        return x_float + gate_rows * branch
    output, pullback = jax.vjp(forward, hidden.astype(jnp.float32), w_mod.astype(jnp.float32), b_mod, w_in.astype(jnp.float32), conv_w, conv_b, w_x.astype(jnp.float32), w_dt.astype(jnp.float32), dt_bias, a_log, d_skip, w_out.astype(jnp.float32))
    gradients = pullback(grad_out.astype(jnp.float32))
    return (output.astype(jnp.bfloat16), gradients[0], gradients[1], gradients[2], gradients[3], gradients[4], gradients[5], gradients[6], gradients[7], gradients[8], gradients[9], gradients[10], gradients[11])
```

```python
import functools

import jax
import jax.numpy as jnp
from jax import lax
from jax.experimental import pallas as pl
from jax.experimental.pallas import tpu as pltpu
from jax.sharding import PartitionSpec as P

EPSILON = 1e-06
HIGHEST = lax.Precision.HIGHEST
MESH = pl.DeviceIdType.MESH
LANES = 128
LOG2E = 1.4426950408889634
LN2 = 0.6931471805599453
CUT_STEP = 1e9
PLANE = 8
RIM = 8
CHUNK = 16
MIB = 1024 * 1024


def segment_ids(positions, bounds):
    return jnp.sum((positions[:, None] >= bounds[None, :]).astype(jnp.int32), axis=1) - 1


def silu_slope(values):
    sigma = jax.nn.sigmoid(values)
    return sigma * (1.0 + values * (1.0 - sigma))


def contract_rows(left, right):
    return lax.dot_general(
        left, right, (((0,), (0,)), ((), ())), preferred_element_type=jnp.float32
    )


def contract_cols(left, right):
    return lax.dot_general(
        left, right, (((1,), (1,)), ((), ())), preferred_element_type=jnp.float32
    )


def tile_of(c):
    return pl.ds(c * LANES, LANES)


def row_of(ref, first, j, c):
    eight = pl.ds(pl.multiple_of(first + j // 8 * 8, 8), 8)
    return ref.at[eight, tile_of(c)][j % 8 : j % 8 + 1, :]


def summary_kernel(
    step0, step1, drv0, drv1, seed, in0, in1, out0, out1, rate, sums
):
    tokens = step0.shape[0]
    tiles = step0.shape[1] // LANES
    dirs = ((step0, drv0, in0, out0), (step1, drv1, in1, out1))

    def group(i, carry):
        carry = list(carry)
        for k in range(8):
            for d, (step, drv, inc, outc) in enumerate(dirs):
                first = pl.multiple_of((i if d == 0 else tokens // 8 - 1 - i) * 8, 8)
                j = k if d == 0 else 7 - k
                in_row = inc[first + j]
                out_row = outc[first + j]
                for c in range(tiles):
                    state, decay, adj = carry[d * tiles + c]
                    now = jnp.exp2(row_of(step, first, j, c) * rate[d, :, tile_of(c)])
                    state = now * state + in_row * row_of(drv, first, j, c)
                    decay = decay * now
                    adj = adj + decay * (out_row * row_of(seed, first, j, c))
                    carry[d * tiles + c] = (state, decay, adj)
        return tuple(carry)

    zero = jnp.zeros((rate.shape[1], LANES), jnp.float32)
    one = jnp.ones((rate.shape[1], LANES), jnp.float32)
    carry = lax.fori_loop(0, tokens // 8, group, tuple((zero, one, zero) for _ in range(2 * tiles)))
    for d in range(2):
        for c in range(tiles):
            state, decay, adj = carry[d * tiles + c]
            down, up = (adj, state) if d == 0 else (state, adj)
            sums[d, c, 0] = down
            sums[d, c, 1] = decay
            sums[d, c, 2] = up


def summaries(steps, drvs, seed, ins, outs, rate):
    tokens, width = seed.shape
    states = rate.shape[1]
    cols = 256 if width % 256 == 0 else LANES
    rows = pl.BlockSpec((tokens, cols), lambda b: (0, b))
    coef = pl.BlockSpec((tokens, states, LANES), lambda b: (0, 0, 0))
    return pl.pallas_call(
        summary_kernel,
        grid=(width // cols,),
        in_specs=[rows] * 5 + [coef] * 4 + [pl.BlockSpec((2, states, cols), lambda b: (0, 0, b))],
        out_specs=pl.BlockSpec((2, cols // LANES, 3, states, LANES), lambda b: (0, b, 0, 0, 0)),
        out_shape=jax.ShapeDtypeStruct((2, width // LANES, 3, states, LANES), jnp.float32),
        compiler_params=pltpu.CompilerParams(vmem_limit_bytes=48 * MIB),
        name="summaries",
    )(steps[0], steps[1], drvs[0], drvs[1], seed, ins[0], ins[1], outs[0], outs[1], rate)


def carry_kernel(
    count, sums, entering, got, total, others, back, send1, recv1, send2, recv2, send3, recv3
):
    groups = count // PLANE
    me = lax.axis_index("seq")
    mine = lax.rem(me, PLANE)
    level = me // PLANE
    base = level * PLANE
    share = sums.shape[1]

    barrier = pltpu.get_barrier_semaphore()
    for k in range(1, PLANE):
        pl.semaphore_signal(
            barrier, inc=1, device_id=(base + lax.rem(mine + k, PLANE),), device_id_type=MESH
        )
    for k in range(1, groups):
        pl.semaphore_signal(
            barrier,
            inc=1,
            device_id=(lax.rem(level + k, groups) * PLANE + mine,),
            device_id_type=MESH,
        )
    pl.semaphore_wait(barrier, PLANE - 1 + groups - 1)

    first = []
    for k in range(1, PLANE):
        peer = lax.rem(mine + k, PLANE)
        copy = pltpu.make_async_remote_copy(
            src_ref=sums.at[peer],
            dst_ref=got.at[mine],
            send_sem=send1.at[k],
            recv_sem=recv1.at[k],
            device_id=(base + peer,),
            device_id_type=MESH,
        )
        copy.start()
        first.append(copy)
    got[mine] = sums[mine]
    others[level] = jnp.zeros(others.shape[1:], jnp.float32)
    for copy in first:
        copy.wait_recv()

    block = sums.shape[1:2] + sums.shape[3:]
    up = jnp.zeros(block, jnp.float32)
    decay = jnp.ones(block, jnp.float32)
    for j in range(PLANE):
        up = got[j, :, 1] * up + got[j, :, 2]
        decay = decay * got[j, :, 1]
    down = jnp.zeros(block, jnp.float32)
    for j in reversed(range(PLANE)):
        down = got[j, :, 1] * down + got[j, :, 0]
    total[0] = down
    total[1] = decay
    total[2] = up

    second = []
    for k in range(1, groups):
        other = lax.rem(level + k, groups)
        start = jnp.where(other > level, 1, 0)
        copy = pltpu.make_async_remote_copy(
            src_ref=total.at[pl.ds(start, 2)],
            dst_ref=others.at[level],
            send_sem=send2.at[k],
            recv_sem=recv2.at[k],
            device_id=(other * PLANE + mine,),
            device_id_type=MESH,
        )
        copy.start()
        second.append(copy)
    for copy in second:
        copy.wait_recv()

    up = jnp.zeros(block, jnp.float32)
    for g in range(groups):
        up = jnp.where(g < level, others[g, 0] * up + others[g, 1], up)
    down = jnp.zeros(block, jnp.float32)
    for g in reversed(range(groups)):
        down = jnp.where(g > level, others[g, 1] * down + others[g, 0], down)
    for j in range(PLANE):
        back[j, :, 0] = up
        up = got[j, :, 1] * up + got[j, :, 2]
    for j in reversed(range(PLANE)):
        back[j, :, 1] = down
        down = got[j, :, 1] * down + got[j, :, 0]

    third = []
    here = pl.ds(mine * share, share)
    for k in range(1, PLANE):
        peer = lax.rem(mine + k, PLANE)
        copy = pltpu.make_async_remote_copy(
            src_ref=back.at[peer],
            dst_ref=entering.at[here],
            send_sem=send3.at[k],
            recv_sem=recv3.at[k],
            device_id=(base + peer,),
            device_id_type=MESH,
        )
        copy.start()
        third.append(copy)
    entering[here] = back[mine]
    for copy in third:
        copy.wait_recv()
    for copy in first + second + third:
        copy.wait_send()


def carries(sums, count):
    _, tiles, _, states, _ = sums.shape
    share = 2 * tiles // PLANE
    groups = count // PLANE
    stacked = sums.reshape(PLANE, share, 3, states, LANES)
    vmem = pl.BlockSpec(memory_space=pltpu.VMEM)
    entering = pl.pallas_call(
        functools.partial(carry_kernel, count),
        in_specs=[vmem],
        out_specs=vmem,
        out_shape=jax.ShapeDtypeStruct((2 * tiles, 2, states, LANES), jnp.float32),
        scratch_shapes=[
            pltpu.VMEM((PLANE, share, 3, states, LANES), jnp.float32),
            pltpu.VMEM((3, share, states, LANES), jnp.float32),
            pltpu.VMEM((groups, 2, share, states, LANES), jnp.float32),
            pltpu.VMEM((PLANE, share, 2, states, LANES), jnp.float32),
            pltpu.SemaphoreType.DMA((PLANE,)),
            pltpu.SemaphoreType.DMA((PLANE,)),
            pltpu.SemaphoreType.DMA((groups,)),
            pltpu.SemaphoreType.DMA((groups,)),
            pltpu.SemaphoreType.DMA((PLANE,)),
            pltpu.SemaphoreType.DMA((PLANE,)),
        ],
        compiler_params=pltpu.CompilerParams(
            collective_id=0, has_side_effects=True, vmem_limit_bytes=32 * MIB
        ),
        name="carries",
    )(stacked)
    return entering.reshape(2, tiles, 2, states, LANES)


def scan_kernel(
    step0,
    step1,
    drv0,
    drv1,
    seed,
    in0,
    in1,
    out0,
    out1,
    in_blk,
    out_blk,
    ones_blk,
    rate,
    entering,
    y0,
    y1,
    dec0,
    dec1,
    dg0,
    dg1,
    in_grad,
    out_grad,
    rate_grad,
    kept_decay,
    kept_held,
    rows_a,
    rows_b,
    rows_c,
    rows_d,
):
    tokens = step0.shape[0]
    tiles = step0.shape[1] // LANES
    states = rate.shape[1]
    chunks = tokens // CHUNK
    steps, drvs = (step0, step1), (drv0, drv1)
    ins, outs = (in0, in1), (out0, out1)
    ys, decs, dgs = (y0, y1), (dec0, dec1), (dg0, dg1)

    @pl.when(pl.program_id(0) == 0)
    def _():
        in_grad[...] = jnp.zeros_like(in_grad)
        out_grad[...] = jnp.zeros_like(out_grad)

    def forward(i, carry):
        carry = list(carry)
        for d in range(2):
            first = pl.multiple_of((i if d == 0 else chunks - 1 - i) * CHUNK, CHUNK)
            kept = (rows_a, rows_b)[d]
            for k in range(CHUNK):
                j = k if d == 0 else CHUNK - 1 - k
                t = first + j
                in_row = ins[d][t]
                for c in range(tiles):
                    lanes = tile_of(c)
                    now = jnp.exp2(row_of(steps[d], first, j, c) * rate[d, :, lanes])
                    held = now * carry[d * tiles + c]
                    state = held + in_row * row_of(drvs[d], first, j, c)
                    kept_decay[d, t, :, lanes] = now
                    kept_held[d, t, :, lanes] = held
                    kept[j * states : (j + 1) * states, lanes] = state.astype(jnp.bfloat16)
                    carry[d * tiles + c] = state
            here = pl.ds(first, CHUNK)
            block = kept[...]
            ys[d][here, :] = jnp.dot(
                out_blk[d, here, :], block, preferred_element_type=jnp.float32
            )
            out_grad[d, here, :] += contract_cols(seed[here, :].astype(jnp.bfloat16), block)
        return tuple(carry)

    start = tuple(entering[d, c, d] for d in range(2) for c in range(tiles))
    lax.fori_loop(0, chunks, forward, start)

    def backward(i, carry):
        carry = list(carry)
        for d in range(2):
            first = pl.multiple_of((chunks - 1 - i if d == 0 else i) * CHUNK, CHUNK)
            kept = (rows_a, rows_b)[d]
            grads = (rows_c, rows_d)[d]
            for k in range(CHUNK):
                j = CHUNK - 1 - k if d == 0 else k
                t = first + j
                out_row = outs[d][t]
                for c in range(tiles):
                    lanes = tile_of(c)
                    coming, total = carry[d * tiles + c]
                    step = row_of(steps[d], first, j, c)
                    adj = out_row * row_of(seed, first, j, c) + coming
                    coming = kept_decay[d, t, :, lanes] * adj
                    slope = adj * kept_held[d, t, :, lanes] * rate[d, :, lanes]
                    total = total + slope * step
                    kept[j * states : (j + 1) * states, lanes] = adj.astype(jnp.bfloat16)
                    grads[j * states : (j + 1) * states, lanes] = slope.astype(jnp.bfloat16)
                    carry[d * tiles + c] = (coming, total)
            here = pl.ds(first, CHUNK)
            block = kept[...]
            dgs[d][here, :] = jnp.dot(
                in_blk[d, here, :], block, preferred_element_type=jnp.float32
            )
            in_grad[d, here, :] += contract_cols(drvs[d][here, :].astype(jnp.bfloat16), block)
            decs[d][here, :] = (
                jnp.dot(ones_blk[...], grads[...], preferred_element_type=jnp.float32) * LN2
            )
        return tuple(carry)

    zero = jnp.zeros((states, LANES), jnp.float32)
    start = tuple((entering[d, c, 1 - d], zero) for d in range(2) for c in range(tiles))
    carry = lax.fori_loop(0, chunks, backward, start)
    for d in range(2):
        for c in range(tiles):
            rate_grad[d, :, c * LANES : (c + 1) * LANES] = carry[d * tiles + c][1] * LN2


def scans(steps, drvs, seed, ins, outs, in_blk, out_blk, ones_blk, rate, entering):
    tokens, width = seed.shape
    states = rate.shape[1]
    cols = 256 if width % 256 == 0 else LANES
    tiles = cols // LANES
    wide = CHUNK * states
    rows = pl.BlockSpec((tokens, cols), lambda b: (0, b))
    coef = pl.BlockSpec((tokens, states, LANES), lambda b: (0, 0, 0))
    diag = pl.BlockSpec((2, tokens, wide), lambda b: (0, 0, 0))
    by_state = pl.BlockSpec((2, states, cols), lambda b: (0, 0, b))
    full = jax.ShapeDtypeStruct((tokens, width), jnp.float32)
    diag_out = jax.ShapeDtypeStruct((2, tokens, wide), jnp.float32)
    return pl.pallas_call(
        scan_kernel,
        grid=(width // cols,),
        in_specs=[rows] * 5
        + [coef] * 4
        + [diag, diag, pl.BlockSpec((CHUNK, wide), lambda b: (0, 0)), by_state]
        + [pl.BlockSpec((2, tiles, 2, states, LANES), lambda b: (0, b, 0, 0, 0))],
        out_specs=[rows] * 6 + [diag, diag, by_state],
        out_shape=[full] * 6
        + [diag_out, diag_out, jax.ShapeDtypeStruct((2, states, width), jnp.float32)],
        scratch_shapes=[
            pltpu.VMEM((2, tokens, states, cols), jnp.float32),
            pltpu.VMEM((2, tokens, states, cols), jnp.float32),
        ]
        + [pltpu.VMEM((wide, cols), jnp.bfloat16)] * 4,
        compiler_params=pltpu.CompilerParams(vmem_limit_bytes=48 * MIB),
        name="scans",
    )(
        steps[0],
        steps[1],
        drvs[0],
        drvs[1],
        seed,
        ins[0],
        ins[1],
        outs[0],
        outs[1],
        in_blk,
        out_blk,
        ones_blk,
        rate,
        entering,
    )


def reduce_kernel(
    count,
    part_a,
    part_b,
    mod,
    rim,
    out_a,
    out_b,
    out_mod,
    out_rim,
    a1,
    b1,
    a2,
    b2,
    a3,
    b3,
    a4,
    b4,
    m1,
    m2,
    m3,
    m4,
    send,
    recv,
    send_far,
    recv_far,
):
    groups = count // PLANE
    me = lax.axis_index("seq")
    bit0 = lax.rem(me, 2)
    bit1 = lax.rem(me // 2, 2)
    bit2 = lax.rem(me // 4, 2)
    level = me // PLANE
    low = lax.rem(me, PLANE)
    flip0 = me + 1 - 2 * bit0
    flip1 = me + 2 - 4 * bit1
    flip2 = me + 4 - 8 * bit2
    left = lax.rem(me + count - 1, count)
    right = lax.rem(me + 1, count)

    def other(k):
        return lax.rem(level + k, groups)

    barrier = pltpu.get_barrier_semaphore()
    peers = [flip0, flip1, flip2, left, right] + [other(k) * PLANE + low for k in range(1, groups)]
    for peer in peers:
        pl.semaphore_signal(barrier, inc=1, device_id=(peer,), device_id_type=MESH)
    pl.semaphore_wait(barrier, len(peers))

    started = []

    def push(src, dst, slot, peer, sems=None):
        sends, recvs = sems or (send, recv)
        copy = pltpu.make_async_remote_copy(
            src_ref=src,
            dst_ref=dst,
            send_sem=sends.at[slot],
            recv_sem=recvs.at[slot],
            device_id=(peer,),
            device_id_type=MESH,
        )
        copy.start()
        started.append(copy)
        return copy

    def add(into, own, first):
        def one(i, none):
            into[i] = (
                into[i].astype(jnp.float32) + own[first + i].astype(jnp.float32)
            ).astype(into.dtype)
            return none

        lax.fori_loop(0, into.shape[0], one, 0)

    edge_l = push(rim.at[pl.ds(0, RIM)], out_rim.at[pl.ds(RIM, RIM)], 0, left)
    edge_r = push(rim.at[pl.ds(RIM, RIM)], out_rim.at[pl.ds(0, RIM)], 1, right)

    got_m = push(mod, m1, 2, flip0)
    got_a = push(part_a.at[1 - bit0], a1, 3, flip0)
    got_b = push(part_b.at[1 - bit0], b1, 4, flip0)
    got_m.wait_recv()
    m1[...] += mod[...]
    half = 2 * groups
    got_a.wait_recv()
    add(a1, part_a.at[bit0], 0)
    got_m = push(m1, m2, 5, flip1)
    got_a = push(a1.at[pl.ds((1 - bit1) * half, half)], a2, 6, flip1)
    got_b.wait_recv()
    add(b1, part_b.at[bit0], 0)
    got_b = push(b1.at[pl.ds((1 - bit2) * half, half)], b2, 7, flip2)
    got_m.wait_recv()
    m2[...] += m1[...]
    got_m = push(m2, m3, 8, flip2)
    got_a.wait_recv()
    add(a2, a1, bit1 * half)
    got_a = push(a2.at[pl.ds((1 - bit2) * groups, groups)], a3, 9, flip2)
    got_b.wait_recv()
    add(b2, b1, bit2 * half)
    got_b = push(b2.at[pl.ds((1 - bit1) * groups, groups)], b3, 10, flip1)
    got_m.wait_recv()
    m3[...] += m2[...]
    far = (send_far, recv_far)
    last = []
    for k in range(1, groups):
        last.append(push(m3, m4.at[level], 3 * k, other(k) * PLANE + low, far))
    got_a.wait_recv()
    add(a3, a2, bit2 * groups)
    for k in range(1, groups):
        last.append(
            push(a3.at[other(k)], a4.at[level], 3 * k + 1, other(k) * PLANE + low, far)
        )
    got_b.wait_recv()
    add(b3, b2, bit1 * groups)
    for k in range(1, groups):
        last.append(
            push(b3.at[other(k)], b4.at[level], 3 * k + 2, other(k) * PLANE + low, far)
        )
    a4[level] = a3[level]
    b4[level] = b3[level]
    m4[level] = m3[...]
    for copy in last:
        copy.wait_recv()
    edge_l.wait_recv()
    edge_r.wait_recv()
    for into, held in ((out_a, a4), (out_b, b4), (out_mod, m4)):
        total = held[0].astype(jnp.float32)
        for g in range(1, groups):
            total = total + held[g].astype(jnp.float32)
        into[...] = total
    for copy in started:
        copy.wait_send()


def reduce_shares(part_a, part_b, mod, rim, count):
    groups = count // PLANE
    vmem = pl.BlockSpec(memory_space=pltpu.VMEM)
    rows, cols_a = part_a.shape[-2:]
    cols_b = part_b.shape[-1]

    def slots(number):
        return [
            pltpu.VMEM((number, rows, cols_a), jnp.bfloat16),
            pltpu.VMEM((number, rows, cols_b), jnp.bfloat16),
        ]

    return pl.pallas_call(
        functools.partial(reduce_kernel, count),
        in_specs=[vmem] * 4,
        out_specs=[vmem] * 4,
        out_shape=[
            jax.ShapeDtypeStruct((rows, cols_a), jnp.float32),
            jax.ShapeDtypeStruct((rows, cols_b), jnp.float32),
            jax.ShapeDtypeStruct(mod.shape, jnp.float32),
            jax.ShapeDtypeStruct(rim.shape, jnp.float32),
        ],
        scratch_shapes=slots(4 * groups)
        + slots(2 * groups)
        + slots(groups)
        + slots(groups)
        + [pltpu.VMEM(mod.shape, jnp.float32)] * 3
        + [
            pltpu.VMEM((groups,) + mod.shape, jnp.float32),
            pltpu.SemaphoreType.DMA((11,)),
            pltpu.SemaphoreType.DMA((11,)),
            pltpu.SemaphoreType.DMA((3 * groups,)),
            pltpu.SemaphoreType.DMA((3 * groups,)),
        ],
        compiler_params=pltpu.CompilerParams(
            collective_id=1, has_side_effects=True, vmem_limit_bytes=48 * MIB
        ),
        name="reduce_shares",
    )(part_a, part_b, mod, rim)


def on_device(
    count,
    hidden,
    condition,
    seq_lengths,
    w_mod,
    b_mod,
    w_in,
    conv_w,
    conv_b,
    w_x,
    w_dt,
    dt_bias,
    a_log,
    d_skip,
    w_out,
    grad_out,
):
    tokens, model = hidden.shape
    seq_count = condition.shape[0]
    inner = w_in.shape[1] // 2
    rank = w_dt.shape[1]
    states = a_log.shape[1]
    taps = conv_w.shape[1]
    groups = count // PLANE
    me = lax.axis_index("seq")
    first_row = me * tokens

    below = lax.ppermute(hidden[-RIM:], "seq", [(i, i + 1) for i in range(count - 1)])
    above = lax.ppermute(hidden[:RIM], "seq", [(i + 1, i) for i in range(count - 1)])
    own = slice(RIM, RIM + tokens)
    positions = first_row - RIM + jnp.arange(tokens + 2 * RIM, dtype=jnp.int32)
    bounds = jnp.concatenate([jnp.zeros((1,), jnp.int32), jnp.cumsum(seq_lengths)])
    wide_segment = segment_ids(positions, bounds)
    segment = wide_segment[own]

    def same(offset):
        return wide_segment[RIM + offset : RIM + offset + tokens] == segment

    onehot = (wide_segment[:, None] == jnp.arange(seq_count, dtype=jnp.int32)[None, :]).astype(
        jnp.float32
    )
    cond_act = jax.nn.silu(condition).astype(jnp.bfloat16)
    modulation = jnp.dot(cond_act, w_mod, preferred_element_type=jnp.float32) + b_mod[None, :]
    mod_rows = jnp.dot(onehot, modulation, precision=HIGHEST, preferred_element_type=jnp.float32)
    shift_rows = mod_rows[:, :model]
    scale_rows = mod_rows[:, model : 2 * model]
    gate_rows = mod_rows[own, 2 * model :]

    x_wide = jnp.concatenate([below, hidden, above], axis=0).astype(jnp.float32)
    row_mean = jnp.mean(x_wide, axis=1, keepdims=True)
    centered = x_wide - row_mean
    rescale = lax.rsqrt(jnp.mean(centered * centered, axis=1, keepdims=True) + EPSILON)
    normed = centered * rescale
    mixer_in = (normed * (1.0 + scale_rows) + shift_rows).astype(jnp.bfloat16)
    conv_wide = (
        jnp.dot(mixer_in, w_in[:, :inner], preferred_element_type=jnp.float32)
        .astype(jnp.bfloat16)
        .astype(jnp.float32)
    )
    gate_branch = jnp.dot(mixer_in[own], w_in[:, inner:], preferred_element_type=jnp.float32)

    cotangent = grad_out.astype(jnp.float32)
    branch_grad = (cotangent * gate_rows).astype(jnp.bfloat16)
    gated_grad = contract_cols(branch_grad, w_out)
    gate_silu = jax.nn.silu(gate_branch)
    mixed_grad = gated_grad * gate_silu

    saved = []
    for d in range(2):
        conv_sum = conv_b[d][None, :]
        for k in range(taps):
            offset = k - (taps - 1) if d == 0 else taps - 1 - k
            conv_sum = conv_sum + conv_w[d, k][None, :] * conv_wide[
                RIM + offset : RIM + offset + tokens
            ] * same(offset).astype(jnp.float32)[:, None]
        active = jax.nn.silu(conv_sum).astype(jnp.bfloat16)
        projection = jnp.dot(active, w_x[d], preferred_element_type=jnp.float32)
        rank_low = projection[:, :rank].astype(jnp.bfloat16)
        in_coef = projection[:, rank : rank + states]
        out_coef = projection[:, rank + states :]
        logit = (
            jnp.dot(rank_low, w_dt[d], preferred_element_type=jnp.float32) + dt_bias[d][None, :]
        )
        step = jax.nn.softplus(logit)
        keep = same(-1) if d == 0 else same(1)
        masked = jnp.where(keep[:, None], step, CUT_STEP)
        driven = step * active.astype(jnp.float32)
        saved.append((conv_sum, active, rank_low, in_coef, out_coef, logit, step, masked, driven))

    def spread(coef):
        return jnp.broadcast_to(coef[:, :, None], (tokens, states, LANES))

    place = jnp.arange(tokens, dtype=jnp.int32) % CHUNK
    on_diag = (place[:, None] == jnp.arange(CHUNK, dtype=jnp.int32)[None, :]).astype(jnp.float32)

    def block_diag(coef):
        wide = on_diag[:, :, None] * coef[:, None, :]
        return wide.reshape(tokens, CHUNK * states).astype(jnp.bfloat16)

    rate = -jnp.exp(a_log)
    steps = [s[7] for s in saved]
    drvs = [s[8] for s in saved]
    ins = [spread(s[3]) for s in saved]
    outs = [spread(s[4]) for s in saved]
    in_blk = jnp.stack([block_diag(s[3]) for s in saved])
    out_blk = jnp.stack([block_diag(s[4]) for s in saved])
    ones_blk = block_diag(jnp.ones((tokens, states), jnp.float32))[:CHUNK]
    fast_rate = rate * LOG2E
    sums = summaries(steps, drvs, mixed_grad, ins, outs, fast_rate)
    entering = carries(sums, count)
    y0, y1, dec0, dec1, dg0, dg1, in_acc, out_acc, rate_grad = scans(
        steps, drvs, mixed_grad, ins, outs, in_blk, out_blk, ones_blk, fast_rate, entering
    )
    in_grads = jnp.sum(in_acc.reshape(2, tokens, CHUNK, states) * on_diag[None, :, :, None], axis=2)
    out_grads = jnp.sum(
        out_acc.reshape(2, tokens, CHUNK, states) * on_diag[None, :, :, None], axis=2
    )

    mixed = y0 + y1
    for d in range(2):
        mixed = mixed + d_skip[d][None, :] * saved[d][1].astype(jnp.float32)
    gated = (mixed * gate_silu).astype(jnp.bfloat16)
    branch = jnp.dot(gated, w_out, preferred_element_type=jnp.float32)
    output = (x_wide[own] + gate_rows * branch).astype(jnp.bfloat16)
    gate_grad = cotangent * branch
    grad_w_out = contract_rows(gated, branch_grad)
    gate_branch_grad = (gated_grad * mixed * silu_slope(gate_branch)).astype(jnp.bfloat16)

    wide_grad = jnp.zeros((tokens + 2 * RIM, inner), jnp.float32)
    x_proj, dt_proj, small = [], [], []
    conv_w_cols, conv_b_cols, dt_cols, skip_cols = [], [], [], []
    for d in range(2):
        conv_sum, active, rank_low, in_coef, out_coef, logit, step, masked, driven = saved[d]
        active_float = active.astype(jnp.float32)
        driven_grad = (dg0, dg1)[d]
        step_grad = (dec0, dec1)[d] + driven_grad * active_float
        active_grad = driven_grad * step + mixed_grad * d_skip[d][None, :]
        skip_cols.append(jnp.sum(mixed_grad * active_float, axis=0))
        logit_grad = step_grad * jax.nn.sigmoid(logit)
        dt_cols.append(jnp.sum(logit_grad, axis=0))
        logit_low = logit_grad.astype(jnp.bfloat16)
        dt_proj.append(contract_rows(logit_low, rank_low))
        rank_grad = contract_cols(logit_low, w_dt[d])
        proj_grad = jnp.concatenate([rank_grad, in_grads[d], out_grads[d]], axis=1).astype(
            jnp.bfloat16
        )
        x_proj.append(contract_rows(active, proj_grad))
        active_total = active_grad + contract_cols(proj_grad, w_x[d])
        conv_grad = active_total * silu_slope(conv_sum)
        conv_b_cols.append(jnp.sum(conv_grad, axis=0))
        for k in range(taps):
            offset = k - (taps - 1) if d == 0 else taps - 1 - k
            masked_grad = conv_grad * same(offset).astype(jnp.float32)[:, None]
            conv_w_cols.append(
                jnp.sum(
                    masked_grad * conv_wide[RIM + offset : RIM + offset + tokens], axis=0
                )
            )
            wide_grad = wide_grad + jnp.pad(
                conv_w[d, k][None, :] * masked_grad, ((RIM + offset, RIM - offset), (0, 0))
            )
    input_grad = wide_grad.astype(jnp.bfloat16)
    grad_in_conv = contract_rows(mixer_in, input_grad)
    grad_in_gate = contract_rows(mixer_in[own], gate_branch_grad)
    norm_wide = contract_cols(input_grad, w_in[:, :inner])
    norm_wide = norm_wide.at[own].add(contract_cols(gate_branch_grad, w_in[:, inner:]))

    mod_low = lax.dot_general(
        onehot,
        jnp.concatenate([norm_wide, norm_wide * normed], axis=1),
        (((0,), (0,)), ((), ())),
        precision=HIGHEST,
        preferred_element_type=jnp.float32,
    )
    mod_high = lax.dot_general(
        onehot[own],
        gate_grad,
        (((0,), (0,)), ((), ())),
        precision=HIGHEST,
        preferred_element_type=jnp.float32,
    )
    mod_part = jnp.concatenate([mod_low, mod_high], axis=1)
    mod_part = jnp.pad(mod_part, ((0, -seq_count % 8), (0, 0)))
    rim = jnp.concatenate([norm_wide[:RIM], norm_wide[-RIM:]], axis=0)

    rows = inner // count
    pad_rows = -rows % 16
    mrows = model // count
    both = jnp.stack(
        [grad_in_conv.reshape(count, mrows, inner), grad_in_gate.reshape(count, mrows, inner)],
        axis=1,
    ).reshape(count, 2 * mrows, inner)
    cols = jnp.concatenate(
        [
            x_proj[0],
            x_proj[1],
            dt_proj[0],
            dt_proj[1],
            jnp.stack(conv_w_cols + conv_b_cols + dt_cols + skip_cols, axis=1),
            rate_grad.reshape(2 * states, inner).T,
        ],
        axis=1,
    )
    cols = jnp.pad(cols, ((0, 0), (0, -cols.shape[1] % LANES)))
    pieces = [both, grad_w_out.reshape(count, rows, model), cols.reshape(count, rows, -1)]
    whole = jnp.concatenate([p.astype(jnp.bfloat16) for p in pieces], axis=2)
    whole = jnp.pad(whole, ((0, 0), (0, pad_rows), (0, 0)))
    width = whole.shape[2]
    split = width // LANES // 2 * LANES
    whole = whole.reshape(groups, 2, 2, 2, rows + pad_rows, width)
    part_a = whole[..., :split].transpose(3, 2, 1, 0, 4, 5)
    part_b = whole[..., split:].transpose(3, 1, 2, 0, 4, 5)
    part_a = part_a.reshape(2, 4 * groups, rows + pad_rows, split)
    part_b = part_b.reshape(2, 4 * groups, rows + pad_rows, width - split)
    share_a, share_b, mod_grad, edges = reduce_shares(part_a, part_b, mod_part, rim, count)
    share = jnp.concatenate([share_a, share_b], axis=1)[:rows]

    edges = jnp.concatenate(
        [
            jnp.where(me > 0, edges[:RIM], 0.0),
            jnp.zeros((tokens - 2 * RIM, model), jnp.float32),
            jnp.where(me < count - 1, edges[RIM:], 0.0),
        ],
        axis=0,
    )
    norm_grad = norm_wide[own] + edges
    scaled = norm_grad * (1.0 + scale_rows[own])
    normed_own = normed[own]
    grad_x = cotangent + rescale[own] * (
        scaled
        - jnp.mean(scaled, axis=1, keepdims=True)
        - normed_own * jnp.mean(scaled * normed_own, axis=1, keepdims=True)
    )

    my_cond = lax.dynamic_slice_in_dim(cond_act.astype(jnp.float32), me * mrows, mrows, axis=1)
    mod_grad = mod_grad[:seq_count]
    share_w_mod = lax.dot_general(
        my_cond,
        mod_grad,
        (((0,), (0,)), ((), ())),
        precision=HIGHEST,
        preferred_element_type=jnp.float32,
    )
    bias_cols = 3 * model // count
    share_b_mod = lax.dynamic_slice_in_dim(
        jnp.sum(mod_grad, axis=0), me * bias_cols, bias_cols, axis=0
    )

    w_in_share = jnp.concatenate([share[:mrows, :inner], share[mrows:, :inner]], axis=1)
    w_out_share = share[:, inner : inner + model]
    rest = share[:, inner + model :]
    proj = rank + 2 * states
    at = 0

    def take(number):
        nonlocal at
        piece = rest[:, at : at + number]
        at += number
        return piece

    share_w_x = jnp.stack([take(proj), take(proj)])
    share_w_dt = jnp.stack([take(rank).T, take(rank).T])
    share_conv_w = take(2 * taps).T.reshape(2, taps, rows)
    share_conv_b = take(2).T
    share_dt_bias = take(2).T
    share_skip = take(2).T
    share_a_log = take(2 * states).T.reshape(2, states, rows)
    return (
        output,
        grad_x,
        share_w_mod,
        share_b_mod,
        w_in_share,
        share_conv_w,
        share_conv_b,
        share_w_x,
        share_w_dt,
        share_dt_bias,
        share_a_log,
        share_skip,
        w_out_share,
    )


def solution(mesh):
    in_specs = (P("seq", None),) + (P(),) * 13 + (P("seq", None),)
    out_specs = (
        P("seq", None),
        P("seq", None),
        P("seq", None),
        P("seq"),
        P("seq", None),
        P(None, None, "seq"),
        P(None, "seq"),
        P(None, "seq", None),
        P(None, None, "seq"),
        P(None, "seq"),
        P(None, None, "seq"),
        P(None, "seq"),
        P("seq", None),
    )
    return jax.shard_map(
        functools.partial(on_device, mesh.shape["seq"]),
        mesh=mesh,
        in_specs=in_specs,
        out_specs=out_specs,
        check_vma=False,
    )
```

```python
import functools

import jax
import jax.numpy as jnp
from jax import lax
from jax.experimental import pallas as pl
from jax.experimental.pallas import tpu as pltpu
from jax.sharding import PartitionSpec as P

EPSILON = 1e-06
HIGHEST = lax.Precision.HIGHEST
MESH = pl.DeviceIdType.MESH
LANES = 128
LOG2E = 1.4426950408889634
LN2 = 0.6931471805599453
CUT_STEP = 1e9
PLANE = 8
RIM = 8
CHUNK = 16
COLS = 256
MIB = 1024 * 1024
F32 = jnp.float32
BF16 = jnp.bfloat16
VMEM = pl.BlockSpec(memory_space=pltpu.VMEM)
ANY = pl.BlockSpec(memory_space=pl.ANY)


def shaped(shape, dtype=F32):
    return jax.ShapeDtypeStruct(shape, dtype)


def dot(left, right, dims=((1,), (0,)), precision=None):
    return lax.dot_general(
        left, right, (dims, ((), ())), precision=precision, preferred_element_type=F32
    )


def contract_rows(left, right, precision=None):
    return dot(left, right, ((0,), (0,)), precision)


def contract_cols(left, right):
    return dot(left, right, ((1,), (1,)))


def sigmoid(values):
    return 1.0 / (1.0 + jnp.exp(-values))


def silu_slope(values):
    sigma = sigmoid(values)
    return sigma * (1.0 + values * (1.0 - sigma))


def softplus(values):
    return jnp.maximum(values, 0.0) + jnp.log1p(jnp.exp(-jnp.abs(values)))


def tile_at(start):
    return pl.ds(pl.multiple_of(start, LANES), LANES)


def row_of(ref, first, j, lanes):
    eight = pl.ds(pl.multiple_of(first + j // 8 * 8, 8), 8)
    return ref.at[eight, lanes][j % 8 : j % 8 + 1, :]


def segments(positions, bounds):
    total = jnp.full(positions.shape, -1, jnp.int32)
    for bound in bounds:
        total = total + (positions >= bound).astype(jnp.int32)
    return total


def read_bounds(lengths):
    bounds = [jnp.int32(0)]
    for j in range(lengths.shape[0]):
        bounds.append(bounds[-1] + lengths[j])
    return bounds


def rows_iota(rows):
    return lax.broadcasted_iota(jnp.int32, (rows, LANES), 0)


def offset_of(d, k, taps):
    return k - (taps - 1) if d == 0 else taps - 1 - k


def head_kernel(
    lengths,
    hidden,
    below,
    above,
    condition,
    b_mod,
    conv_w,
    conv_b,
    dt_bias,
    a_log,
    grad_out,
    w_mod_any,
    w_in_any,
    w_x_any,
    w_dt_any,
    w_out_any,
    mixer,
    mixer_own,
    normed,
    rescale,
    scale1,
    gate_rows,
    branch_grad,
    conv_keep,
    gate_branch,
    gated_grad,
    seed,
    conv_sum,
    active,
    rank_low,
    logit,
    masked,
    driven,
    in_spread,
    out_spread,
    in_blk,
    out_blk,
    rate,
    rate_tiles,
    sums,
    masks,
    hot,
    w_mod,
    w_conv,
    w_gate,
    w_x,
    w_dt,
    w_out,
    conv_wide,
    proj,
    modulation,
    sems,
):
    tokens, model = hidden.shape
    inner = seed.shape[1]
    rank = w_dt.shape[1]
    states = a_log.shape[1]
    taps = conv_w.shape[1]
    wide = tokens + 2 * RIM
    tiles = inner // LANES

    loads = [
        pltpu.make_async_copy(src, dst, sems.at[i])
        for i, (src, dst) in enumerate(
            (
                (w_mod_any, w_mod),
                (w_in_any.at[:, pl.ds(0, inner)], w_conv),
                (w_in_any.at[:, pl.ds(inner, inner)], w_gate),
                (w_out_any, w_out),
                (w_x_any, w_x),
                (w_dt_any, w_dt),
            )
        )
    ]
    for load in loads:
        load.start()

    first = lax.axis_index("seq") * tokens
    bounds = read_bounds(lengths)
    position = first + rows_iota(tokens)
    segment = segments(position, bounds)
    for offset in range(1 - taps, taps):
        masks[offset + taps - 1] = (segments(position + offset, bounds) == segment).astype(F32)
    wide_segment = segments(first - RIM + rows_iota(wide), bounds)
    lane = lax.broadcasted_iota(jnp.int32, (wide, LANES), 1)
    hot[...] = (wide_segment == lane).astype(F32)

    rate[...] = -jnp.exp(a_log[...]) * LOG2E
    for d in range(2):
        for c in range(tiles):
            rate_tiles[d * tiles + c] = rate[d, :, c * LANES : (c + 1) * LANES]

    x = jnp.concatenate(
        [below[...].astype(F32), hidden[...].astype(F32), above[...].astype(F32)], axis=0
    )
    centered = x - jnp.mean(x, axis=1, keepdims=True)
    scaling = lax.rsqrt(jnp.mean(centered * centered, axis=1, keepdims=True) + EPSILON)
    normal = centered * scaling
    normed[...] = normal
    rescale[...] = jnp.broadcast_to(scaling[RIM : RIM + tokens], (tokens, LANES))

    cond = condition[...]
    cond_act = (cond * sigmoid(cond)).astype(BF16)
    loads[0].wait()
    seqs = condition.shape[0]
    modulation[0:seqs, :] = dot(cond_act, w_mod[...]) + b_mod[...]
    for c in range(model // LANES):
        lanes = slice(c * LANES, (c + 1) * LANES)

        def rows_for(part, segs):
            total = jnp.zeros(segs.shape, F32)
            for j in range(seqs):
                at = part * model + c * LANES
                total = jnp.where(segs == j, modulation[j : j + 1, at : at + LANES], total)
            return total

        one_scale = 1.0 + rows_for(1, wide_segment)
        mixed_in = normed[:, lanes] * one_scale + rows_for(0, wide_segment)
        mixer[:, lanes] = mixed_in.astype(BF16)
        mixer_own[:, lanes] = mixed_in[RIM : RIM + tokens].astype(BF16)
        scale1[:, lanes] = one_scale[RIM : RIM + tokens]
        gate = rows_for(2, segment)
        gate_rows[:, lanes] = gate
        branch_grad[:, lanes] = (grad_out[:, lanes].astype(F32) * gate).astype(BF16)

    for load in loads[1:]:
        load.wait()

    proj[...] = jnp.zeros_like(proj)

    def block(b, none):
        cols = pl.ds(pl.multiple_of(b * COLS, COLS), COLS)
        conv = dot(mixer[...], w_conv[:, cols]).astype(BF16)
        conv_keep[:, cols] = conv
        conv_wide[...] = conv.astype(F32)
        gate = dot(mixer_own[...], w_gate[:, cols])
        gate_branch[:, cols] = gate
        back = contract_cols(branch_grad[...], w_out[cols, :])
        gated_grad[:, cols] = back
        seed[:, cols] = back * (gate * sigmoid(gate))
        for d in range(2):
            acts = []
            for c in range(COLS // LANES):
                lanes = tile_at(b * COLS + c * LANES)
                here = slice(c * LANES, (c + 1) * LANES)
                total = jnp.broadcast_to(conv_b[d : d + 1, lanes], (tokens, LANES))
                for k in range(taps):
                    offset = offset_of(d, k, taps)
                    total = total + conv_w[d, k : k + 1, lanes] * (
                        conv_wide[RIM + offset : RIM + offset + tokens, here]
                        * masks[offset + taps - 1]
                    )
                conv_sum[d, :, lanes] = total
                act = (total * sigmoid(total)).astype(BF16)
                active[d, :, lanes] = act
                acts.append(act)
            proj[d] += dot(jnp.concatenate(acts, axis=1), w_x[d, cols, :])
        return none

    lax.fori_loop(0, inner // COLS, block, 0)

    place = lax.rem(lax.broadcasted_iota(jnp.int32, (tokens, CHUNK * states), 0), CHUNK)
    owner = lax.broadcasted_iota(jnp.int32, (tokens, CHUNK * states), 1) // states
    on_diag = place == owner
    column = lax.rem(lax.broadcasted_iota(jnp.int32, (states, CHUNK * states), 1), states)
    repeat = (column == lax.broadcasted_iota(jnp.int32, (states, CHUNK * states), 0)).astype(BF16)
    for d in range(2):
        whole = proj[d]
        rank_low[d] = whole[:, :rank].astype(BF16)
        flipped = whole.T
        for start, blk, spread in (
            (rank, in_blk, in_spread),
            (rank + states, out_blk, out_spread),
        ):
            coef = whole[:, start : start + states].astype(BF16)
            blk[d] = jnp.where(on_diag, dot(coef, repeat), 0.0).astype(BF16)
            rows = flipped[start : start + states, :]
            for t in range(tokens):
                spread[d, t] = jnp.broadcast_to(rows[:, t : t + 1], (states, LANES))

    def stepping(b, none):
        cols = pl.ds(pl.multiple_of(b * COLS, COLS), COLS)
        for d in range(2):
            value = dot(rank_low[d], w_dt[d, :, cols]) + dt_bias[d : d + 1, cols]
            step = softplus(value)
            keep = masks[taps - 2] if d == 0 else masks[taps]
            keep = jnp.concatenate([keep] * (COLS // LANES), axis=1)
            logit[d, :, cols] = value
            masked[d, :, cols] = jnp.where(keep > 0.5, step, CUT_STEP)
            driven[d, :, cols] = step * active[d, :, cols].astype(F32)
        return none

    lax.fori_loop(0, inner // COLS, stepping, 0)

    per = COLS // LANES

    def summary(b, none):
        lanes = [tile_at(b * COLS + c * LANES) for c in range(per)]

        def group(i, carry):
            carry = list(carry)
            for k in range(8):
                for d in range(2):
                    start = pl.multiple_of((i if d == 0 else tokens // 8 - 1 - i) * 8, 8)
                    j = k if d == 0 else 7 - k
                    in_row = in_spread[d, start + j]
                    out_row = out_spread[d, start + j]
                    for c in range(per):
                        state, decay, adj = carry[d * per + c]
                        now = jnp.exp2(
                            row_of(masked.at[d], start, j, lanes[c]) * rate[d, :, lanes[c]]
                        )
                        state = now * state + in_row * row_of(driven.at[d], start, j, lanes[c])
                        decay = decay * now
                        adj = adj + decay * (out_row * row_of(seed, start, j, lanes[c]))
                        carry[d * per + c] = (state, decay, adj)
            return tuple(carry)

        zero = jnp.zeros((states, LANES), F32)
        one = jnp.ones((states, LANES), F32)
        carry = lax.fori_loop(
            0, tokens // 8, group, tuple((zero, one, zero) for _ in range(2 * per))
        )
        for d in range(2):
            for c in range(per):
                state, decay, adj = carry[d * per + c]
                down, up = (adj, state) if d == 0 else (state, adj)
                at = d * tiles + b * per + c
                sums[at, 0] = down.astype(BF16)
                sums[at, 1] = three_pieces(
                    jnp.sum(masked[d, :, lanes[c]], axis=0, keepdims=True), states
                )
                sums[at, 2] = up.astype(BF16)
        return none

    lax.fori_loop(0, inner // COLS, summary, 0)


def three_pieces(row, states):
    high = row.astype(BF16).astype(F32)
    middle = (row - high).astype(BF16).astype(F32)
    lowest = row - high - middle
    at = lax.broadcasted_iota(jnp.int32, (states, row.shape[-1]), 0)
    return jnp.where(
        at == 0, high, jnp.where(at == 1, middle, jnp.where(at == 2, lowest, 0.0))
    ).astype(BF16)


def head(lengths, hidden, below, above, condition, b_mod, conv_w, conv_b, dt_bias, a_log, grad_out, weights):
    w_mod, w_in, w_x, w_dt, w_out = weights
    tokens, model = hidden.shape
    inner = w_in.shape[1] // 2
    rank = w_dt.shape[1]
    states = a_log.shape[1]
    taps = conv_w.shape[1]
    wide = tokens + 2 * RIM
    both = (2, tokens, inner)
    spread = (2, tokens, states, LANES)
    diag = (2, tokens, CHUNK * states)
    outs = dict(
        mixer=shaped((wide, model), BF16),
        mixer_own=shaped((tokens, model), BF16),
        normed=shaped((wide, model)),
        rescale=shaped((tokens, LANES)),
        scale1=shaped((tokens, model)),
        gate_rows=shaped((tokens, model)),
        branch_grad=shaped((tokens, model), BF16),
        conv_keep=shaped((wide, inner), BF16),
        gate_branch=shaped((tokens, inner)),
        gated_grad=shaped((tokens, inner)),
        seed=shaped((tokens, inner)),
        conv_sum=shaped(both),
        active=shaped(both, BF16),
        rank_low=shaped((2, tokens, rank), BF16),
        logit=shaped(both),
        masked=shaped(both),
        driven=shaped(both),
        in_spread=shaped(spread),
        out_spread=shaped(spread),
        in_blk=shaped(diag, BF16),
        out_blk=shaped(diag, BF16),
        rate=shaped(a_log.shape),
        rate_tiles=shaped((2 * inner // LANES, states, LANES)),
        sums=shaped((2 * inner // LANES, 3, states, LANES), BF16),
        masks=shaped((2 * taps - 1, tokens, LANES)),
        hot=shaped((wide, LANES)),
    )
    results = pl.pallas_call(
        head_kernel,
        in_specs=[pl.BlockSpec(memory_space=pltpu.SMEM)] + [VMEM] * 10 + [ANY] * 5,
        out_specs=[VMEM] * len(outs),
        out_shape=list(outs.values()),
        scratch_shapes=[
            pltpu.VMEM(w_mod.shape, BF16),
            pltpu.VMEM((model, inner), BF16),
            pltpu.VMEM((model, inner), BF16),
            pltpu.VMEM(w_x.shape, BF16),
            pltpu.VMEM(w_dt.shape, BF16),
            pltpu.VMEM(w_out.shape, BF16),
            pltpu.VMEM((wide, COLS), F32),
            pltpu.VMEM((2, tokens, w_x.shape[2]), F32),
            pltpu.VMEM((8, w_mod.shape[1]), F32),
            pltpu.SemaphoreType.DMA((6,)),
        ],
        compiler_params=pltpu.CompilerParams(vmem_limit_bytes=56 * MIB),
        name="head",
    )(
        lengths,
        hidden,
        below,
        above,
        condition,
        b_mod.reshape(1, -1),
        conv_w,
        conv_b,
        dt_bias,
        a_log,
        grad_out,
        w_mod,
        w_in,
        w_x,
        w_dt,
        w_out,
    )
    return dict(zip(outs, results))


def carry_kernel(
    count, sums, rate, entering, got, total, others, back, send1, recv1, send2, recv2, send3, recv3
):
    groups = count // PLANE
    me = lax.axis_index("seq")
    mine = lax.rem(me, PLANE)
    level = me // PLANE
    base = level * PLANE
    share, _, states, _ = sums.shape
    share = share // PLANE
    here = pl.ds(mine * share, share)

    barrier = pltpu.get_barrier_semaphore()
    for k in range(1, PLANE):
        pl.semaphore_signal(
            barrier, inc=1, device_id=(base + lax.rem(mine + k, PLANE),), device_id_type=MESH
        )
    for k in range(1, groups):
        pl.semaphore_signal(
            barrier,
            inc=1,
            device_id=(lax.rem(level + k, groups) * PLANE + mine,),
            device_id_type=MESH,
        )
    pl.semaphore_wait(barrier, PLANE - 1 + groups - 1)

    first = []
    for k in range(1, PLANE):
        peer = lax.rem(mine + k, PLANE)
        copy = pltpu.make_async_remote_copy(
            src_ref=sums.at[pl.ds(peer * share, share)],
            dst_ref=got.at[mine],
            send_sem=send1.at[k],
            recv_sem=recv1.at[k],
            device_id=(base + peer,),
            device_id_type=MESH,
        )
        copy.start()
        first.append(copy)
    got[mine] = sums[here]
    others[level] = jnp.zeros(others.shape[1:], BF16)
    for copy in first:
        copy.wait_recv()

    block = (share, states, LANES)
    rates = rate[here]

    def whole(pieces):
        pieces = pieces.astype(F32)
        return pieces[:, 0:1] + pieces[:, 1:2] + pieces[:, 2:3]

    times = [whole(got[j, :, 1]) for j in range(PLANE)]
    decays = [jnp.exp2(rates * time) for time in times]
    up = jnp.zeros(block, F32)
    down = jnp.zeros(block, F32)
    time = times[0]
    for j in range(PLANE):
        up = decays[j] * up + got[j, :, 2].astype(F32)
        if j:
            time = time + times[j]
    for j in reversed(range(PLANE)):
        down = decays[j] * down + got[j, :, 0].astype(F32)
    total[0] = down.astype(BF16)
    for c in range(share):
        total[1, c] = three_pieces(time[c], states)
    total[2] = up.astype(BF16)

    second = []
    for k in range(1, groups):
        other = lax.rem(level + k, groups)
        start = jnp.where(other > level, 1, 0)
        copy = pltpu.make_async_remote_copy(
            src_ref=total.at[pl.ds(start, 2)],
            dst_ref=others.at[level],
            send_sem=send2.at[k],
            recv_sem=recv2.at[k],
            device_id=(other * PLANE + mine,),
            device_id_type=MESH,
        )
        copy.start()
        second.append(copy)
    for copy in second:
        copy.wait_recv()

    up = jnp.zeros(block, F32)
    for g in range(groups):
        decay = jnp.exp2(rates * whole(others[g, 0]))
        up = jnp.where(g < level, decay * up + others[g, 1].astype(F32), up)
    down = jnp.zeros(block, F32)
    for g in reversed(range(groups)):
        decay = jnp.exp2(rates * whole(others[g, 1]))
        down = jnp.where(g > level, decay * down + others[g, 0].astype(F32), down)
    for j in range(PLANE):
        back[j, :, 0] = up.astype(BF16)
        up = decays[j] * up + got[j, :, 2].astype(F32)
    for j in reversed(range(PLANE)):
        back[j, :, 1] = down.astype(BF16)
        down = decays[j] * down + got[j, :, 0].astype(F32)

    third = []
    for k in range(1, PLANE):
        peer = lax.rem(mine + k, PLANE)
        copy = pltpu.make_async_remote_copy(
            src_ref=back.at[peer],
            dst_ref=entering.at[here],
            send_sem=send3.at[k],
            recv_sem=recv3.at[k],
            device_id=(base + peer,),
            device_id_type=MESH,
        )
        copy.start()
        third.append(copy)
    entering[here] = back[mine]
    for copy in third:
        copy.wait_recv()
    for copy in first + second + third:
        copy.wait_send()


def carries(sums, rate, count):
    rows, _, states, _ = sums.shape
    share = rows // PLANE
    groups = count // PLANE
    entering = pl.pallas_call(
        functools.partial(carry_kernel, count),
        in_specs=[VMEM, VMEM],
        out_specs=VMEM,
        out_shape=shaped((rows, 2, states, LANES), BF16),
        scratch_shapes=[
            pltpu.VMEM((PLANE, share, 3, states, LANES), BF16),
            pltpu.VMEM((3, share, states, LANES), BF16),
            pltpu.VMEM((groups, 2, share, states, LANES), BF16),
            pltpu.VMEM((PLANE, share, 2, states, LANES), BF16),
            pltpu.SemaphoreType.DMA((PLANE,)),
            pltpu.SemaphoreType.DMA((PLANE,)),
            pltpu.SemaphoreType.DMA((groups,)),
            pltpu.SemaphoreType.DMA((groups,)),
            pltpu.SemaphoreType.DMA((PLANE,)),
            pltpu.SemaphoreType.DMA((PLANE,)),
        ],
        compiler_params=pltpu.CompilerParams(
            collective_id=0, has_side_effects=True, vmem_limit_bytes=32 * MIB
        ),
        name="carries",
    )(sums, rate)
    return entering.reshape(2, rows // 2, 2, states, LANES)


def states_kernel(masked, driven, seed, in_spread, out_blk, rate, entering, mixed, out_grad, kept):
    tokens, cols = seed.shape
    per = cols // LANES
    states = rate.shape[1]
    chunks = tokens // CHUNK

    @pl.when(pl.program_id(0) == 0)
    def _():
        out_grad[...] = jnp.zeros_like(out_grad)

    mixed[...] = jnp.zeros_like(mixed)
    for c in range(per):
        lanes = pl.ds(c * LANES, LANES)
        kept[0, 0:states, lanes] = entering[0, c, 0]
        kept[1, tokens * states : (tokens + 1) * states, lanes] = entering[1, c, 1]

    def forward(i, carry):
        carry = list(carry)
        for d in range(2):
            first = pl.multiple_of((i if d == 0 else chunks - 1 - i) * CHUNK, CHUNK)
            slot = pl.multiple_of((first + 1 - d) * states, states)
            block = kept.at[d, pl.ds(slot, CHUNK * states), :]
            for k in range(CHUNK):
                j = k if d == 0 else CHUNK - 1 - k
                in_row = in_spread[d, first + j]
                for c in range(per):
                    lanes = pl.ds(c * LANES, LANES)
                    now = jnp.exp2(row_of(masked.at[d], first, j, lanes) * rate[d, :, lanes])
                    state = now * carry[d * per + c] + in_row * row_of(
                        driven.at[d], first, j, lanes
                    )
                    block[j * states : (j + 1) * states, lanes] = state.astype(BF16)
                    carry[d * per + c] = state
            here = pl.ds(first, CHUNK)
            mixed[here, :] += dot(out_blk[d, here, :], block[...])
            out_grad[d, here, :] += contract_cols(seed[here, :].astype(BF16), block[...])
        return tuple(carry)

    start = tuple(entering[d, c, d].astype(F32) for d in range(2) for c in range(per))
    lax.fori_loop(0, chunks, forward, start)


def block_specs(tokens, states):
    wide = CHUNK * states
    return dict(
        both=pl.BlockSpec((2, tokens, COLS), lambda b: (0, 0, b)),
        rows=pl.BlockSpec((tokens, COLS), lambda b: (0, b)),
        spread=pl.BlockSpec((2, tokens, states, LANES), lambda b: (0, 0, 0, 0)),
        diag=pl.BlockSpec((2, tokens, wide), lambda b: (0, 0, 0)),
        rate=pl.BlockSpec((2, states, COLS), lambda b: (0, 0, b)),
        entering=pl.BlockSpec((2, COLS // LANES, 2, states, LANES), lambda b: (0, b, 0, 0, 0)),
        kept=pl.BlockSpec((2, (tokens + 1) * states, COLS), lambda b: (0, 0, b)),
    )


def run_states(h, entering):
    tokens, inner = h["seed"].shape
    states = h["rate"].shape[1]
    s = block_specs(tokens, states)
    return pl.pallas_call(
        states_kernel,
        grid=(inner // COLS,),
        in_specs=[s["both"], s["both"], s["rows"], s["spread"], s["diag"], s["rate"], s["entering"]],
        out_specs=[s["rows"], s["diag"], s["kept"]],
        out_shape=[
            shaped((tokens, inner)),
            shaped((2, tokens, CHUNK * states)),
            shaped((2, (tokens + 1) * states, inner), BF16),
        ],
        compiler_params=pltpu.CompilerParams(vmem_limit_bytes=48 * MIB),
        name="states",
    )(h["masked"], h["driven"], h["seed"], h["in_spread"], h["out_blk"], h["rate"], entering)


def adjoints_kernel(
    masked,
    driven,
    seed,
    out_spread,
    in_blk,
    rate,
    entering,
    kept,
    decay_grad,
    driven_grad,
    in_grad,
    rate_grad,
    rows_a,
    rows_b,
    rows_c,
    rows_d,
):
    tokens, cols = seed.shape
    per = cols // LANES
    states = rate.shape[1]
    chunks = tokens // CHUNK
    wide = CHUNK * states
    ones = (
        lax.broadcasted_iota(jnp.int32, (CHUNK, wide), 1) // states
        == lax.broadcasted_iota(jnp.int32, (CHUNK, wide), 0)
    ).astype(BF16)

    @pl.when(pl.program_id(0) == 0)
    def _():
        in_grad[...] = jnp.zeros_like(in_grad)

    def backward(i, carry):
        carry = list(carry)
        for d in range(2):
            first = pl.multiple_of((chunks - 1 - i if d == 0 else i) * CHUNK, CHUNK)
            slot = pl.multiple_of((first + d) * states, states)
            before = kept.at[d, pl.ds(slot, wide), :]
            adjs = (rows_a, rows_b)[d]
            slopes = (rows_c, rows_d)[d]
            for k in range(CHUNK):
                j = CHUNK - 1 - k if d == 0 else k
                out_row = out_spread[d, first + j]
                part = slice(j * states, (j + 1) * states)
                for c in range(per):
                    lanes = pl.ds(c * LANES, LANES)
                    coming, total = carry[d * per + c]
                    step = row_of(masked.at[d], first, j, lanes)
                    now = jnp.exp2(step * rate[d, :, lanes])
                    adj = out_row * row_of(seed, first, j, lanes) + coming
                    coming = now * adj
                    slope = coming * before[part, lanes].astype(F32) * rate[d, :, lanes]
                    total = total + slope * step
                    adjs[part, lanes] = adj.astype(BF16)
                    slopes[part, lanes] = slope.astype(BF16)
                    carry[d * per + c] = (coming, total)
            here = pl.ds(first, CHUNK)
            driven_grad[d, here, :] = dot(in_blk[d, here, :], adjs[...])
            in_grad[d, here, :] += contract_cols(driven[d, here, :].astype(BF16), adjs[...])
            decay_grad[d, here, :] = dot(ones, slopes[...]) * LN2
        return tuple(carry)

    zero = jnp.zeros((states, LANES), F32)
    start = tuple((entering[d, c, 1 - d].astype(F32), zero) for d in range(2) for c in range(per))
    carry = lax.fori_loop(0, chunks, backward, start)
    for d in range(2):
        for c in range(per):
            rate_grad[d, :, c * LANES : (c + 1) * LANES] = carry[d * per + c][1] * LN2


def run_adjoints(h, entering, kept):
    tokens, inner = h["seed"].shape
    states = h["rate"].shape[1]
    s = block_specs(tokens, states)
    return pl.pallas_call(
        adjoints_kernel,
        grid=(inner // COLS,),
        in_specs=[
            s["both"],
            s["both"],
            s["rows"],
            s["spread"],
            s["diag"],
            s["rate"],
            s["entering"],
            s["kept"],
        ],
        out_specs=[s["both"], s["both"], s["diag"], s["rate"]],
        out_shape=[
            shaped((2, tokens, inner)),
            shaped((2, tokens, inner)),
            shaped((2, tokens, CHUNK * states)),
            shaped((2, states, inner)),
        ],
        scratch_shapes=[pltpu.VMEM((CHUNK * states, COLS), BF16)] * 4,
        compiler_params=pltpu.CompilerParams(vmem_limit_bytes=48 * MIB),
        name="adjoints",
    )(
        h["masked"],
        h["driven"],
        h["seed"],
        h["out_spread"],
        h["in_blk"],
        h["rate"],
        entering,
        kept,
    )


def slot_of(o, count, order):
    bits = [o & 1, o >> 1 & 1, o >> 2 & 1]
    groups = count // PLANE
    later = (bits[1], bits[2]) if order == "xy" else (bits[2], bits[1])
    return bits[0], (later[0] * 2 + later[1]) * groups + o // PLANE


def slot_rows(count, inner):
    rows = inner // count
    return rows + -rows % 16


def stacked_rows(source, stage, o, rows):
    half = source.shape[1] // 2
    part = pl.ds(o * rows, rows)
    if rows % 8 == 0:
        return jnp.concatenate([source[part, :half], source[part, half:]], axis=0)
    stage[0:rows, :] = source[part, :half]
    stage[rows : 2 * rows, :] = source[part, half:]
    return stage[...]


def mid_kernel(
    count,
    states_sum,
    active,
    d_skip,
    gate_branch,
    gated_grad,
    gate_rows,
    branch_grad,
    mixer_own,
    hidden,
    grad_out,
    w_out,
    output,
    gate_grad,
    gate_branch_grad,
    slots_out,
    slots_gate,
    gated,
    branch,
    whole_out,
    whole_gate,
    stage,
):
    tokens, inner = states_sum.shape
    model = hidden.shape[1]
    branch[...] = jnp.zeros_like(branch)

    def block(b, none):
        cols = pl.ds(pl.multiple_of(b * COLS, COLS), COLS)
        mixed = states_sum[:, cols]
        for d in range(2):
            mixed = mixed + d_skip[d : d + 1, cols] * active[d, :, cols].astype(F32)
        gate = gate_branch[:, cols]
        sigma = sigmoid(gate)
        now = (mixed * (gate * sigma)).astype(BF16)
        gated[:, cols] = now
        slope = sigma * (1.0 + gate * (1.0 - sigma))
        back = (gated_grad[:, cols] * mixed * slope).astype(BF16)
        gate_branch_grad[:, cols] = back
        branch[...] += dot(now, w_out[cols, :])
        whole_out[cols, :] = contract_rows(now, branch_grad[...])
        whole_gate[:, cols] = contract_rows(mixer_own[...], back)
        return none

    lax.fori_loop(0, inner // COLS, block, 0)
    output[...] = (hidden[...].astype(F32) + gate_rows[...] * branch[...]).astype(BF16)
    gate_grad[...] = grad_out[...].astype(F32) * branch[...]
    rows, mrows = inner // count, model // count
    for o in range(count):
        first, rest = slot_of(o, count, "xy")
        slots_out[first, rest, 0:rows] = whole_out[o * rows : (o + 1) * rows, :].astype(BF16)
        first, rest = slot_of(o, count, "yx")
        slots_gate[first, rest] = stacked_rows(whole_gate, stage, o, mrows).astype(BF16)


def run_mid(h, count, states_sum, d_skip, hidden, grad_out, w_out):
    tokens, inner = states_sum.shape
    model = hidden.shape[1]
    slots = shaped((2, count // 2, slot_rows(count, inner), model), BF16)
    return pl.pallas_call(
        functools.partial(mid_kernel, count),
        in_specs=[VMEM] * 11,
        out_specs=[VMEM] * 5,
        out_shape=[
            shaped((tokens, model), BF16),
            shaped((tokens, model)),
            shaped((tokens, inner), BF16),
            slots,
            slots,
        ],
        scratch_shapes=[
            pltpu.VMEM((tokens, inner), BF16),
            pltpu.VMEM((tokens, model), F32),
            pltpu.VMEM((inner, model), F32),
            pltpu.VMEM((model, inner), F32),
            pltpu.VMEM((slot_rows(count, inner), model), F32),
        ],
        compiler_params=pltpu.CompilerParams(vmem_limit_bytes=56 * MIB),
        name="mid",
    )(
        states_sum,
        h["active"],
        d_skip,
        h["gate_branch"],
        h["gated_grad"],
        h["gate_rows"],
        h["branch_grad"],
        h["mixer_own"],
        hidden,
        grad_out,
        w_out,
    )


def post_kernel(
    count,
    decay_grad,
    driven_grad,
    in_acc,
    out_acc,
    rate_grad,
    logit,
    active,
    rank_low,
    seed,
    conv_sum,
    conv_keep,
    masks,
    hot,
    d_skip,
    conv_w,
    mixer,
    normed,
    gate_grad,
    gate_branch_grad,
    w_x,
    w_dt,
    w_in,
    norm_wide,
    mod_part,
    slots_a,
    slots_b,
    active_grad,
    rank_grad,
    proj_grad,
    conv_wide,
    input_wide,
    whole_conv,
    whole_cols,
    small,
    stage,
):
    tokens, inner = seed.shape
    model = normed.shape[1]
    wide = normed.shape[0]
    taps = conv_w.shape[1]
    rank = w_dt.shape[1]
    proj = w_x.shape[2]
    states = rate_grad.shape[1]
    seqs = mod_part.shape[0]
    rank_grad[...] = jnp.zeros_like(rank_grad)
    small[...] = jnp.zeros_like(small)
    at_conv, at_bias, at_dt, at_skip, at_rate = (
        0,
        2 * taps,
        2 * taps + 2,
        2 * taps + 4,
        2 * taps + 8,
    )

    def column_sum(values):
        return jnp.sum(values, axis=0, keepdims=True)

    def through_steps(b, none):
        cols = pl.ds(pl.multiple_of(b * COLS, COLS), COLS)
        for d in range(2):
            act = active[d, :, cols].astype(F32)
            value = logit[d, :, cols]
            back = driven_grad[d, :, cols]
            grown = seed[:, cols]
            grad = (decay_grad[d, :, cols] + back * act) * sigmoid(value)
            low = grad.astype(BF16)
            active_grad[d, :, cols] = back * softplus(value) + grown * d_skip[d : d + 1, cols]
            small[at_dt + d : at_dt + d + 1, cols] = column_sum(grad)
            small[at_skip + d : at_skip + d + 1, cols] = column_sum(grown * act)
            small[at_rate + d * states : at_rate + (d + 1) * states, cols] = rate_grad[d, :, cols]
            rank_grad[d] += contract_cols(low, w_dt[d, :, cols])
            start = 2 * proj + d * rank
            whole_cols[cols, start : start + rank] = contract_rows(low, rank_low[d])
        return none

    lax.fori_loop(0, inner // COLS, through_steps, 0)

    place = lax.rem(lax.broadcasted_iota(jnp.int32, (tokens, CHUNK * states), 0), CHUNK)
    owner = lax.broadcasted_iota(jnp.int32, (tokens, CHUNK * states), 1) // states
    on_diag = place == owner
    column = lax.rem(lax.broadcasted_iota(jnp.int32, (CHUNK * states, states), 0), states)
    gather = (column == lax.broadcasted_iota(jnp.int32, (CHUNK * states, states), 1)).astype(BF16)
    for d in range(2):
        proj_grad[d, :, 0:rank] = rank_grad[d].astype(BF16)
        for start, acc in ((rank, in_acc), (rank + states, out_acc)):
            kept = jnp.where(on_diag, acc[d], 0.0).astype(BF16)
            proj_grad[d, :, start : start + states] = dot(kept, gather).astype(BF16)

    norm_wide[...] = jnp.zeros_like(norm_wide)

    def through_conv(b, none):
        cols = pl.ds(pl.multiple_of(b * COLS, COLS), COLS)
        conv_wide[...] = conv_keep[:, cols].astype(F32)
        input_wide[...] = jnp.zeros_like(input_wide)
        for d in range(2):
            low = proj_grad[d]
            start = d * proj
            whole_cols[cols, start : start + proj] = contract_rows(active[d, :, cols], low)
            total = active_grad[d, :, cols] + contract_cols(low, w_x[d, cols, :])
            for c in range(COLS // LANES):
                lanes = tile_at(b * COLS + c * LANES)
                here = slice(c * LANES, (c + 1) * LANES)
                grad = total[:, here] * silu_slope(conv_sum[d, :, lanes])
                small[at_bias + d : at_bias + d + 1, lanes] = column_sum(grad)
                for k in range(taps):
                    offset = offset_of(d, k, taps)
                    window = slice(RIM + offset, RIM + offset + tokens)
                    part = grad * masks[offset + taps - 1]
                    at = at_conv + d * taps + k
                    small[at : at + 1, lanes] = column_sum(part * conv_wide[window, here])
                    input_wide[window, here] += conv_w[d, k : k + 1, lanes] * part
        low = input_wide[...].astype(BF16)
        whole_conv[:, cols] = contract_rows(mixer[...], low)
        norm_wide[...] += contract_cols(low, w_in[:, cols])
        gate_cols = pl.ds(pl.multiple_of(inner + b * COLS, COLS), COLS)
        norm_wide[RIM : RIM + tokens, :] += contract_cols(
            gate_branch_grad[:, cols], w_in[:, gate_cols]
        )
        whole_cols[cols, 2 * (proj + rank) :] = small[:, cols].T
        return none

    lax.fori_loop(0, inner // COLS, through_conv, 0)

    seq_rows = hot[:, 0:seqs]
    grads = norm_wide[...]
    mod_part[:, 0:model] = contract_rows(seq_rows, grads, HIGHEST)
    mod_part[:, model : 2 * model] = contract_rows(seq_rows, grads * normed[...], HIGHEST)
    mod_part[:, 2 * model :] = contract_rows(
        hot[RIM : RIM + tokens, 0:seqs], gate_grad[...], HIGHEST
    )

    rows, mrows = inner // count, model // count
    cut = slots_a.shape[3]
    rest = model - cut
    for o in range(count):
        both = stacked_rows(whole_conv, stage, o, mrows).astype(BF16)
        first, later = slot_of(o, count, "xy")
        slots_a[first, later] = both[:, :cut]
        first, later = slot_of(o, count, "yx")
        slots_b[first, later, :, 0:rest] = both[:, cut:]
        slots_b[first, later, 0:rows, rest:] = whole_cols[o * rows : (o + 1) * rows, :].astype(BF16)


def column_width(proj, rank, taps, states):
    small = 2 * taps + 8 + 2 * states
    small = small + -small % 8
    total = 2 * (proj + rank) + small
    return small + -total % LANES, total + -total % LANES


def run_post(h, count, adjoint_side, out_acc, mid_side, d_skip, conv_w, w_x, w_dt, w_in):
    decay_grad, driven_grad, in_acc, rate_grad = adjoint_side
    gate_grad, gate_branch_grad = mid_side
    tokens, inner = h["seed"].shape
    wide, model = h["normed"].shape
    rank = w_dt.shape[1]
    proj = w_x.shape[2]
    states = rate_grad.shape[1]
    small, width = column_width(proj, rank, conv_w.shape[1], states)
    rows = slot_rows(count, inner)
    cut = (model + width) // 2 // LANES * LANES
    return pl.pallas_call(
        functools.partial(post_kernel, count),
        in_specs=[VMEM] * 22,
        out_specs=[VMEM] * 4,
        out_shape=[
            shaped((wide, model)),
            shaped((8, 3 * model)),
            shaped((2, count // 2, rows, cut), BF16),
            shaped((2, count // 2, rows, model + width - cut), BF16),
        ],
        scratch_shapes=[
            pltpu.VMEM((2, tokens, inner), F32),
            pltpu.VMEM((2, tokens, rank), F32),
            pltpu.VMEM((2, tokens, proj), BF16),
            pltpu.VMEM((wide, COLS), F32),
            pltpu.VMEM((wide, COLS), F32),
            pltpu.VMEM((model, inner), F32),
            pltpu.VMEM((inner, width), F32),
            pltpu.VMEM((small, inner), F32),
            pltpu.VMEM((rows, model), F32),
        ],
        compiler_params=pltpu.CompilerParams(vmem_limit_bytes=58 * MIB),
        name="post",
    )(
        decay_grad,
        driven_grad,
        in_acc,
        out_acc,
        rate_grad,
        h["logit"],
        h["active"],
        h["rank_low"],
        h["seed"],
        h["conv_sum"],
        h["conv_keep"],
        h["masks"],
        h["hot"],
        d_skip,
        conv_w,
        h["mixer"],
        h["normed"],
        gate_grad,
        gate_branch_grad,
        w_x,
        w_dt,
        w_in,
    )


def reduce_kernel(count, orders, *refs):
    number = len(orders)
    refs = list(refs)

    def take(size):
        taken = refs[:size]
        del refs[:size]
        return taken

    parts, (mod, rim) = take(number), take(2)
    shares, (out_mod, out_rim) = take(number), take(2)
    got1, got2, got3, got4 = take(number), take(number), take(number), take(number)
    m1, m2, m3, m4 = take(4)
    send, recv, send_far, recv_far = take(4)
    groups = count // PLANE
    me = lax.axis_index("seq")
    bits = [lax.rem(me, 2), lax.rem(me // 2, 2), lax.rem(me // 4, 2)]
    flips = [me + (1 - 2 * bits[i]) * (1 << i) for i in range(3)]
    level = me // PLANE
    low = lax.rem(me, PLANE)
    left = lax.rem(me + count - 1, count)
    right = lax.rem(me + 1, count)
    far = [lax.rem(level + k, groups) for k in range(1, groups)]

    barrier = pltpu.get_barrier_semaphore()
    peers = flips + [left, right] + [g * PLANE + low for g in far]
    for peer in peers:
        pl.semaphore_signal(barrier, inc=1, device_id=(peer,), device_id_type=MESH)
    pl.semaphore_wait(barrier, len(peers))

    started = []

    def push(src, dst, sems, slot, peer):
        copy = pltpu.make_async_remote_copy(
            src_ref=src,
            dst_ref=dst,
            send_sem=sems[0].at[slot],
            recv_sem=sems[1].at[slot],
            device_id=(peer,),
            device_id_type=MESH,
        )
        copy.start()
        started.append(copy)
        return copy

    near_sems, far_sems = (send, recv), (send_far, recv_far)

    def near(src, dst, slot, peer):
        return push(src, dst, near_sems, slot, peer)

    def add(into, own, first):
        def one(i, none):
            into[i] = (into[i].astype(F32) + own[first + i].astype(F32)).astype(BF16)
            return none

        lax.fori_loop(0, into.shape[0], one, 0)

    edges = [
        near(rim.at[pl.ds(0, RIM)], out_rim.at[pl.ds(RIM, RIM)], 0, left),
        near(rim.at[pl.ds(rim.shape[0] - RIM, RIM)], out_rim.at[pl.ds(0, RIM)], 1, right),
    ]
    base = 5
    mods = near(mod, m1, 2, flips[0])
    waits = [
        near(parts[p].at[1 - bits[0]], got1[p], base + p, flips[0]) for p in range(number)
    ]
    half = 2 * groups
    mods.wait_recv()
    m1[...] += mod[...]
    mods = near(m1, m2, 3, flips[1])
    for p, order in enumerate(orders):
        i = 1 if order == "xy" else 2
        waits[p].wait_recv()
        add(got1[p], parts[p].at[bits[0]], 0)
        waits[p] = near(
            got1[p].at[pl.ds((1 - bits[i]) * half, half)], got2[p], base + number + p, flips[i]
        )
    mods.wait_recv()
    m2[...] += m1[...]
    mods = near(m2, m3, 4, flips[2])
    for p, order in enumerate(orders):
        i, j = (1, 2) if order == "xy" else (2, 1)
        waits[p].wait_recv()
        add(got2[p], got1[p], bits[i] * half)
        waits[p] = near(
            got2[p].at[pl.ds((1 - bits[j]) * groups, groups)],
            got3[p],
            base + 2 * number + p,
            flips[j],
        )
    mods.wait_recv()
    m3[...] += m2[...]
    last = []
    for k, g in enumerate(far):
        last.append(push(m3, m4.at[level], far_sems, k, g * PLANE + low))
    m4[level] = m3[...]
    for p, order in enumerate(orders):
        j = 2 if order == "xy" else 1
        waits[p].wait_recv()
        add(got3[p], got2[p], bits[j] * groups)
        for k, g in enumerate(far):
            slot = (p + 1) * len(far) + k
            last.append(push(got3[p].at[g], got4[p].at[level], far_sems, slot, g * PLANE + low))
        got4[p][level] = got3[p][level]
    for copy in last + edges:
        copy.wait_recv()
    for into, held in list(zip(shares, got4)) + [(out_mod, m4)]:
        total = held[0].astype(F32)
        for g in range(1, groups):
            total = total + held[g].astype(F32)
        into[...] = total
    for copy in started:
        copy.wait_send()


def reduce_shares(parts, orders, mod, rim, count):
    groups = count // PLANE
    number = len(parts)
    shapes = [part.shape[-2:] for part in parts]

    def slots(size):
        return [pltpu.VMEM((size,) + shape, BF16) for shape in shapes]

    near = 5 + 3 * number
    far = (number + 1) * (groups - 1)
    return pl.pallas_call(
        functools.partial(reduce_kernel, count, orders),
        in_specs=[VMEM] * (number + 2),
        out_specs=[VMEM] * (number + 2),
        out_shape=[shaped(shape) for shape in shapes]
        + [shaped(mod.shape), shaped((2 * RIM, rim.shape[1]))],
        scratch_shapes=slots(4 * groups)
        + slots(2 * groups)
        + slots(groups)
        + slots(groups)
        + [pltpu.VMEM(mod.shape, F32)] * 3
        + [pltpu.VMEM((groups,) + mod.shape, F32)]
        + [pltpu.SemaphoreType.DMA((near,))] * 2
        + [pltpu.SemaphoreType.DMA((far,))] * 2,
        compiler_params=pltpu.CompilerParams(
            collective_id=1, has_side_effects=True, vmem_limit_bytes=48 * MIB
        ),
        name="reduce_shares",
    )(*parts, mod, rim)


def finish_kernel(
    count,
    proj,
    rank,
    taps,
    states,
    share_out,
    share_gate,
    share_a,
    share_b,
    mod,
    edges,
    my_cond,
    norm_wide,
    normed,
    rescale,
    scale1,
    grad_out,
    grad_x,
    w_mod,
    b_mod,
    w_in,
    conv_w,
    conv_b,
    w_x,
    w_dt,
    dt_bias,
    a_log,
    d_skip,
    w_out,
):
    me = lax.axis_index("seq")
    tokens, model = grad_out.shape
    mrows, double = w_in.shape
    inner = double // 2
    rows = w_out.shape[0]
    seqs = my_cond.shape[0]
    cut = share_a.shape[1]

    w_out[...] = share_out[0:rows, :]
    w_in[:, 0:cut] = share_a[0:mrows, :]
    w_in[:, cut:model] = share_b[0:mrows, 0 : model - cut]
    w_in[:, model : model + cut] = share_a[mrows : 2 * mrows, :]
    w_in[:, model + cut : inner] = share_b[mrows : 2 * mrows, 0 : model - cut]
    w_in[:, inner : inner + model] = share_gate[0:mrows, :]
    w_in[:, inner + model :] = share_gate[mrows : 2 * mrows, :]

    start = model - cut
    for d in range(2):
        w_x[d] = share_b[0:rows, start + d * proj : start + (d + 1) * proj]
    start = start + 2 * proj
    flipped = share_b[:, model - cut :].T
    at = 2 * proj
    for d in range(2):
        w_dt[d] = flipped[at + d * rank : at + (d + 1) * rank, 0:rows]
    at = at + 2 * rank
    for d in range(2):
        conv_w[d] = flipped[at + d * taps : at + (d + 1) * taps, 0:rows]
    at = at + 2 * taps
    conv_b[...] = flipped[at : at + 2, 0:rows]
    dt_bias[...] = flipped[at + 2 : at + 4, 0:rows]
    d_skip[...] = flipped[at + 4 : at + 6, 0:rows]
    at = at + 8
    for d in range(2):
        a_log[d] = flipped[at + d * states : at + (d + 1) * states, 0:rows]

    cond = my_cond[...]
    cond_act = (cond * sigmoid(cond)).astype(BF16).astype(F32)
    totals = mod[0:seqs, :]
    w_mod[...] = contract_rows(cond_act, totals, HIGHEST)
    b_mod[...] = jnp.sum(totals, axis=0, keepdims=True)

    norm_grad = norm_wide[RIM : RIM + tokens, :]
    low = jnp.where(me > 0, edges[0:RIM, :], 0.0)
    high = jnp.where(me < count - 1, edges[RIM:, :], 0.0)
    middle = jnp.zeros((tokens - 2 * RIM, model), F32)
    norm_grad = norm_grad + jnp.concatenate([low, middle, high], axis=0)
    scaled = norm_grad * scale1[...]
    normal = normed[RIM : RIM + tokens, :]
    grad_x[...] = grad_out[...].astype(F32) + rescale[:, 0:1] * (
        scaled
        - jnp.mean(scaled, axis=1, keepdims=True)
        - normal * jnp.mean(scaled * normal, axis=1, keepdims=True)
    )


def on_device(
    count,
    hidden,
    condition,
    seq_lengths,
    w_mod,
    b_mod,
    w_in,
    conv_w,
    conv_b,
    w_x,
    w_dt,
    dt_bias,
    a_log,
    d_skip,
    w_out,
    grad_out,
):
    tokens, model = hidden.shape
    inner = w_in.shape[1] // 2
    rank = w_dt.shape[1]
    proj = w_x.shape[2]
    states = a_log.shape[1]
    taps = conv_w.shape[1]
    seqs = condition.shape[0]
    me = lax.axis_index("seq")
    rows, mrows = inner // count, model // count

    below = lax.ppermute(hidden[-RIM:], "seq", [(i, i + 1) for i in range(count - 1)])
    above = lax.ppermute(hidden[:RIM], "seq", [(i + 1, i) for i in range(count - 1)])
    h = head(
        seq_lengths,
        hidden,
        below,
        above,
        condition,
        b_mod,
        conv_w,
        conv_b,
        dt_bias,
        a_log,
        grad_out,
        (w_mod, w_in, w_x, w_dt, w_out),
    )
    entering = carries(h["sums"], h["rate_tiles"], count)
    states_sum, out_acc, kept = run_states(h, entering)
    output, gate_grad, gate_branch_grad, slots_out, slots_gate = run_mid(
        h, count, states_sum, d_skip, hidden, grad_out, w_out
    )
    adjoint_side = run_adjoints(h, entering, kept)
    norm_wide, mod_part, slots_a, slots_b = run_post(
        h, count, adjoint_side, out_acc, (gate_grad, gate_branch_grad), d_skip, conv_w, w_x, w_dt, w_in
    )
    share_out, share_gate, share_a, share_b, mod, edges = reduce_shares(
        (slots_out, slots_gate, slots_a, slots_b), ("xy", "yx", "xy", "yx"), mod_part, norm_wide, count
    )
    my_cond = lax.dynamic_slice_in_dim(condition, me * mrows, mrows, axis=1)
    results = pl.pallas_call(
        functools.partial(finish_kernel, count, proj, rank, taps, states),
        in_specs=[VMEM] * 12,
        out_specs=[VMEM] * 12,
        out_shape=[
            shaped((tokens, model)),
            shaped((mrows, 3 * model)),
            shaped((1, 3 * model)),
            shaped((mrows, 2 * inner)),
            shaped((2, taps, rows)),
            shaped((2, rows)),
            shaped((2, rows, proj)),
            shaped((2, rank, rows)),
            shaped((2, rows)),
            shaped((2, states, rows)),
            shaped((2, rows)),
            shaped((rows, model)),
        ],
        compiler_params=pltpu.CompilerParams(vmem_limit_bytes=32 * MIB),
        name="finish",
    )(
        share_out,
        share_gate,
        share_a,
        share_b,
        mod,
        edges,
        my_cond,
        norm_wide,
        h["normed"],
        h["rescale"],
        h["scale1"],
        grad_out,
    )
    bias_cols = 3 * model // count
    share_b_mod = lax.dynamic_slice_in_dim(results[2][0], me * bias_cols, bias_cols, axis=0)
    return (output,) + tuple(results[:2]) + (share_b_mod,) + tuple(results[3:])


def solution(mesh):
    in_specs = (P("seq", None),) + (P(),) * 13 + (P("seq", None),)
    out_specs = (
        P("seq", None),
        P("seq", None),
        P("seq", None),
        P("seq"),
        P("seq", None),
        P(None, None, "seq"),
        P(None, "seq"),
        P(None, "seq", None),
        P(None, None, "seq"),
        P(None, "seq"),
        P(None, None, "seq"),
        P(None, "seq"),
        P("seq", None),
    )
    return jax.shard_map(
        functools.partial(on_device, mesh.shape["seq"]),
        mesh=mesh,
        in_specs=in_specs,
        out_specs=out_specs,
        check_vma=False,
    )
```

```python
import functools

import jax
import jax.numpy as jnp
from jax import lax
from jax.experimental import pallas as pl
from jax.experimental.pallas import tpu as pltpu
from jax.sharding import PartitionSpec as P

EPSILON = 1e-06
HIGHEST = lax.Precision.HIGHEST
MESH = pl.DeviceIdType.MESH
LANES = 128
LOG2E = 1.4426950408889634
LN2 = 0.6931471805599453
CUT_STEP = 1e9
PLANE = 8
RIM = 8
CHUNK = 16
COLS = 256
MIB = 1024 * 1024
F32 = jnp.float32
BF16 = jnp.bfloat16
VMEM = pl.BlockSpec(memory_space=pltpu.VMEM)
ANY = pl.BlockSpec(memory_space=pl.ANY)


def shaped(shape, dtype=F32):
    return jax.ShapeDtypeStruct(shape, dtype)


def dot(left, right, dims=((1,), (0,)), precision=None):
    return lax.dot_general(
        left, right, (dims, ((), ())), precision=precision, preferred_element_type=F32
    )


def contract_rows(left, right, precision=None):
    return dot(left, right, ((0,), (0,)), precision)


def contract_cols(left, right):
    return dot(left, right, ((1,), (1,)))


def sigmoid(values):
    return 1.0 / (1.0 + jnp.exp(-values))


def silu_slope(values):
    sigma = sigmoid(values)
    return sigma * (1.0 + values * (1.0 - sigma))


def softplus(values):
    return jnp.maximum(values, 0.0) + jnp.log1p(jnp.exp(-jnp.abs(values)))


def tile_at(start):
    return pl.ds(pl.multiple_of(start, LANES), LANES)


def row_of(ref, first, j, lanes):
    eight = pl.ds(pl.multiple_of(first + j // 8 * 8, 8), 8)
    return ref.at[eight, lanes][j % 8 : j % 8 + 1, :]


def segments(positions, bounds):
    total = jnp.full(positions.shape, -1, jnp.int32)
    for bound in bounds:
        total = total + (positions >= bound).astype(jnp.int32)
    return total


def read_bounds(lengths):
    bounds = [jnp.int32(0)]
    for j in range(lengths.shape[0]):
        bounds.append(bounds[-1] + lengths[j])
    return bounds


def rows_iota(rows):
    return lax.broadcasted_iota(jnp.int32, (rows, LANES), 0)


def offset_of(d, k, taps):
    return k - (taps - 1) if d == 0 else taps - 1 - k


def head_kernel(
    lengths,
    hidden,
    below,
    above,
    condition,
    b_mod,
    conv_w,
    conv_b,
    dt_bias,
    a_log,
    grad_out,
    w_mod_any,
    w_in_any,
    w_x_any,
    w_dt_any,
    w_out_any,
    mixer,
    mixer_own,
    normed,
    rescale,
    scale1,
    gate_rows,
    branch_grad,
    conv_keep,
    gate_branch,
    gated_grad,
    seed,
    conv_sum,
    active,
    rank_low,
    logit,
    masked,
    driven,
    in_spread,
    out_spread,
    in_blk,
    out_blk,
    rate,
    rate_tiles,
    sums,
    masks,
    hot,
    w_mod,
    w_conv,
    w_gate,
    w_x,
    w_dt,
    w_out,
    conv_wide,
    proj,
    modulation,
    sems,
):
    tokens, model = hidden.shape
    inner = seed.shape[1]
    rank = w_dt.shape[1]
    states = a_log.shape[1]
    taps = conv_w.shape[1]
    wide = tokens + 2 * RIM
    tiles = inner // LANES

    loads = [
        pltpu.make_async_copy(src, dst, sems.at[i])
        for i, (src, dst) in enumerate(
            (
                (w_mod_any, w_mod),
                (w_in_any.at[:, pl.ds(0, inner)], w_conv),
                (w_in_any.at[:, pl.ds(inner, inner)], w_gate),
                (w_out_any, w_out),
                (w_x_any, w_x),
                (w_dt_any, w_dt),
            )
        )
    ]
    for load in loads:
        load.start()

    first = lax.axis_index("seq") * tokens
    bounds = read_bounds(lengths)
    position = first + rows_iota(tokens)
    segment = segments(position, bounds)
    for offset in range(1 - taps, taps):
        masks[offset + taps - 1] = (segments(position + offset, bounds) == segment).astype(F32)
    wide_segment = segments(first - RIM + rows_iota(wide), bounds)
    lane = lax.broadcasted_iota(jnp.int32, (wide, LANES), 1)
    hot[...] = (wide_segment == lane).astype(F32)

    rate[...] = -jnp.exp(a_log[...]) * LOG2E
    for d in range(2):
        for c in range(tiles):
            rate_tiles[d * tiles + c] = rate[d, :, c * LANES : (c + 1) * LANES]

    x = jnp.concatenate(
        [below[...].astype(F32), hidden[...].astype(F32), above[...].astype(F32)], axis=0
    )
    centered = x - jnp.mean(x, axis=1, keepdims=True)
    scaling = lax.rsqrt(jnp.mean(centered * centered, axis=1, keepdims=True) + EPSILON)
    normal = centered * scaling
    normed[...] = normal
    rescale[...] = jnp.broadcast_to(scaling[RIM : RIM + tokens], (tokens, LANES))

    cond = condition[...]
    cond_act = (cond * sigmoid(cond)).astype(BF16)
    loads[0].wait()
    seqs = condition.shape[0]
    modulation[0:seqs, :] = dot(cond_act, w_mod[...]) + b_mod[...]
    for c in range(model // LANES):
        lanes = slice(c * LANES, (c + 1) * LANES)

        def rows_for(part, segs):
            total = jnp.zeros(segs.shape, F32)
            for j in range(seqs):
                at = part * model + c * LANES
                total = jnp.where(segs == j, modulation[j : j + 1, at : at + LANES], total)
            return total

        one_scale = 1.0 + rows_for(1, wide_segment)
        mixed_in = normed[:, lanes] * one_scale + rows_for(0, wide_segment)
        mixer[:, lanes] = mixed_in.astype(BF16)
        mixer_own[:, lanes] = mixed_in[RIM : RIM + tokens].astype(BF16)
        scale1[:, lanes] = one_scale[RIM : RIM + tokens]
        gate = rows_for(2, segment)
        gate_rows[:, lanes] = gate
        branch_grad[:, lanes] = (grad_out[:, lanes].astype(F32) * gate).astype(BF16)

    for load in loads[1:]:
        load.wait()

    proj[...] = jnp.zeros_like(proj)

    def block(b, none):
        cols = pl.ds(pl.multiple_of(b * COLS, COLS), COLS)
        conv = dot(mixer[...], w_conv[:, cols]).astype(BF16)
        conv_keep[:, cols] = conv
        conv_wide[...] = conv.astype(F32)
        gate = dot(mixer_own[...], w_gate[:, cols])
        gate_branch[:, cols] = gate
        back = contract_cols(branch_grad[...], w_out[cols, :])
        gated_grad[:, cols] = back
        seed[:, cols] = back * (gate * sigmoid(gate))
        for d in range(2):
            acts = []
            for c in range(COLS // LANES):
                lanes = tile_at(b * COLS + c * LANES)
                here = slice(c * LANES, (c + 1) * LANES)
                total = jnp.broadcast_to(conv_b[d : d + 1, lanes], (tokens, LANES))
                for k in range(taps):
                    offset = offset_of(d, k, taps)
                    total = total + conv_w[d, k : k + 1, lanes] * (
                        conv_wide[RIM + offset : RIM + offset + tokens, here]
                        * masks[offset + taps - 1]
                    )
                conv_sum[d, :, lanes] = total
                act = (total * sigmoid(total)).astype(BF16)
                active[d, :, lanes] = act
                acts.append(act)
            proj[d] += dot(jnp.concatenate(acts, axis=1), w_x[d, cols, :])
        return none

    lax.fori_loop(0, inner // COLS, block, 0)

    place = lax.rem(lax.broadcasted_iota(jnp.int32, (tokens, CHUNK * states), 0), CHUNK)
    owner = lax.broadcasted_iota(jnp.int32, (tokens, CHUNK * states), 1) // states
    on_diag = place == owner
    column = lax.rem(lax.broadcasted_iota(jnp.int32, (states, CHUNK * states), 1), states)
    repeat = (column == lax.broadcasted_iota(jnp.int32, (states, CHUNK * states), 0)).astype(BF16)
    for d in range(2):
        whole = proj[d]
        rank_low[d] = whole[:, :rank].astype(BF16)
        flipped = whole.T
        for start, blk, spread in (
            (rank, in_blk, in_spread),
            (rank + states, out_blk, out_spread),
        ):
            coef = whole[:, start : start + states].astype(BF16)
            blk[d] = jnp.where(on_diag, dot(coef, repeat), 0.0).astype(BF16)
            rows = flipped[start : start + states, :]
            for t in range(tokens):
                spread[d, t] = jnp.broadcast_to(rows[:, t : t + 1], (states, LANES))

    def stepping(b, none):
        cols = pl.ds(pl.multiple_of(b * COLS, COLS), COLS)
        for d in range(2):
            value = dot(rank_low[d], w_dt[d, :, cols]) + dt_bias[d : d + 1, cols]
            step = softplus(value)
            keep = masks[taps - 2] if d == 0 else masks[taps]
            keep = jnp.concatenate([keep] * (COLS // LANES), axis=1)
            logit[d, :, cols] = value
            masked[d, :, cols] = jnp.where(keep > 0.5, step, CUT_STEP)
            driven[d, :, cols] = step * active[d, :, cols].astype(F32)
        return none

    lax.fori_loop(0, inner // COLS, stepping, 0)

    per = COLS // LANES

    def summary(b, none):
        lanes = [tile_at(b * COLS + c * LANES) for c in range(per)]

        def group(i, carry):
            carry = list(carry)
            for k in range(8):
                for d in range(2):
                    start = pl.multiple_of((i if d == 0 else tokens // 8 - 1 - i) * 8, 8)
                    j = k if d == 0 else 7 - k
                    in_row = in_spread[d, start + j]
                    out_row = out_spread[d, start + j]
                    for c in range(per):
                        state, decay, adj = carry[d * per + c]
                        now = jnp.exp2(
                            row_of(masked.at[d], start, j, lanes[c]) * rate[d, :, lanes[c]]
                        )
                        state = now * state + in_row * row_of(driven.at[d], start, j, lanes[c])
                        decay = decay * now
                        adj = adj + decay * (out_row * row_of(seed, start, j, lanes[c]))
                        carry[d * per + c] = (state, decay, adj)
            return tuple(carry)

        zero = jnp.zeros((states, LANES), F32)
        one = jnp.ones((states, LANES), F32)
        carry = lax.fori_loop(
            0, tokens // 8, group, tuple((zero, one, zero) for _ in range(2 * per))
        )
        for d in range(2):
            for c in range(per):
                state, decay, adj = carry[d * per + c]
                down, up = (adj, state) if d == 0 else (state, adj)
                at = d * tiles + b * per + c
                sums[at, 0] = down.astype(BF16)
                sums[at, 1] = three_pieces(
                    jnp.sum(masked[d, :, lanes[c]], axis=0, keepdims=True), states
                )
                sums[at, 2] = up.astype(BF16)
        return none

    lax.fori_loop(0, inner // COLS, summary, 0)


def three_pieces(row, states):
    high = row.astype(BF16).astype(F32)
    middle = (row - high).astype(BF16).astype(F32)
    lowest = row - high - middle
    at = lax.broadcasted_iota(jnp.int32, (states, row.shape[-1]), 0)
    return jnp.where(
        at == 0, high, jnp.where(at == 1, middle, jnp.where(at == 2, lowest, 0.0))
    ).astype(BF16)


def head(lengths, hidden, below, above, condition, b_mod, conv_w, conv_b, dt_bias, a_log, grad_out, weights):
    w_mod, w_in, w_x, w_dt, w_out = weights
    tokens, model = hidden.shape
    inner = w_in.shape[1] // 2
    rank = w_dt.shape[1]
    states = a_log.shape[1]
    taps = conv_w.shape[1]
    wide = tokens + 2 * RIM
    both = (2, tokens, inner)
    spread = (2, tokens, states, LANES)
    diag = (2, tokens, CHUNK * states)
    outs = dict(
        mixer=shaped((wide, model), BF16),
        mixer_own=shaped((tokens, model), BF16),
        normed=shaped((wide, model)),
        rescale=shaped((tokens, LANES)),
        scale1=shaped((tokens, model)),
        gate_rows=shaped((tokens, model)),
        branch_grad=shaped((tokens, model), BF16),
        conv_keep=shaped((wide, inner), BF16),
        gate_branch=shaped((tokens, inner)),
        gated_grad=shaped((tokens, inner)),
        seed=shaped((tokens, inner)),
        conv_sum=shaped(both),
        active=shaped(both, BF16),
        rank_low=shaped((2, tokens, rank), BF16),
        logit=shaped(both),
        masked=shaped(both),
        driven=shaped(both),
        in_spread=shaped(spread),
        out_spread=shaped(spread),
        in_blk=shaped(diag, BF16),
        out_blk=shaped(diag, BF16),
        rate=shaped(a_log.shape),
        rate_tiles=shaped((2 * inner // LANES, states, LANES)),
        sums=shaped((2 * inner // LANES, 3, states, LANES), BF16),
        masks=shaped((2 * taps - 1, tokens, LANES)),
        hot=shaped((wide, LANES)),
    )
    results = pl.pallas_call(
        head_kernel,
        in_specs=[pl.BlockSpec(memory_space=pltpu.SMEM)] + [VMEM] * 10 + [ANY] * 5,
        out_specs=[VMEM] * len(outs),
        out_shape=list(outs.values()),
        scratch_shapes=[
            pltpu.VMEM(w_mod.shape, BF16),
            pltpu.VMEM((model, inner), BF16),
            pltpu.VMEM((model, inner), BF16),
            pltpu.VMEM(w_x.shape, BF16),
            pltpu.VMEM(w_dt.shape, BF16),
            pltpu.VMEM(w_out.shape, BF16),
            pltpu.VMEM((wide, COLS), F32),
            pltpu.VMEM((2, tokens, w_x.shape[2]), F32),
            pltpu.VMEM((8, w_mod.shape[1]), F32),
            pltpu.SemaphoreType.DMA((6,)),
        ],
        compiler_params=pltpu.CompilerParams(vmem_limit_bytes=56 * MIB),
        name="head",
    )(
        lengths,
        hidden,
        below,
        above,
        condition,
        b_mod.reshape(1, -1),
        conv_w,
        conv_b,
        dt_bias,
        a_log,
        grad_out,
        w_mod,
        w_in,
        w_x,
        w_dt,
        w_out,
    )
    return dict(zip(outs, results))


def carry_kernel(
    count, sums, rate, entering, got, total, others, back, send1, recv1, send2, recv2, send3, recv3
):
    groups = count // PLANE
    me = lax.axis_index("seq")
    mine = lax.rem(me, PLANE)
    level = me // PLANE
    base = level * PLANE
    share, _, states, _ = sums.shape
    share = share // PLANE
    here = pl.ds(mine * share, share)

    barrier = pltpu.get_barrier_semaphore()
    for k in range(1, PLANE):
        pl.semaphore_signal(
            barrier, inc=1, device_id=(base + lax.rem(mine + k, PLANE),), device_id_type=MESH
        )
    for k in range(1, groups):
        pl.semaphore_signal(
            barrier,
            inc=1,
            device_id=(lax.rem(level + k, groups) * PLANE + mine,),
            device_id_type=MESH,
        )
    pl.semaphore_wait(barrier, PLANE - 1 + groups - 1)

    first = []
    for k in range(1, PLANE):
        peer = lax.rem(mine + k, PLANE)
        copy = pltpu.make_async_remote_copy(
            src_ref=sums.at[pl.ds(peer * share, share)],
            dst_ref=got.at[mine],
            send_sem=send1.at[k],
            recv_sem=recv1.at[k],
            device_id=(base + peer,),
            device_id_type=MESH,
        )
        copy.start()
        first.append(copy)
    got[mine] = sums[here]
    others[level] = jnp.zeros(others.shape[1:], BF16)
    for copy in first:
        copy.wait_recv()

    block = (share, states, LANES)
    rates = rate[here]

    def whole(pieces):
        pieces = pieces.astype(F32)
        return pieces[:, 0:1] + pieces[:, 1:2] + pieces[:, 2:3]

    times = [whole(got[j, :, 1]) for j in range(PLANE)]
    decays = [jnp.exp2(rates * time) for time in times]
    up = jnp.zeros(block, F32)
    down = jnp.zeros(block, F32)
    time = times[0]
    for j in range(PLANE):
        up = decays[j] * up + got[j, :, 2].astype(F32)
        if j:
            time = time + times[j]
    for j in reversed(range(PLANE)):
        down = decays[j] * down + got[j, :, 0].astype(F32)
    total[0] = down.astype(BF16)
    for c in range(share):
        total[1, c] = three_pieces(time[c], states)
    total[2] = up.astype(BF16)

    second = []
    for k in range(1, groups):
        other = lax.rem(level + k, groups)
        start = jnp.where(other > level, 1, 0)
        copy = pltpu.make_async_remote_copy(
            src_ref=total.at[pl.ds(start, 2)],
            dst_ref=others.at[level],
            send_sem=send2.at[k],
            recv_sem=recv2.at[k],
            device_id=(other * PLANE + mine,),
            device_id_type=MESH,
        )
        copy.start()
        second.append(copy)
    for copy in second:
        copy.wait_recv()

    up = jnp.zeros(block, F32)
    for g in range(groups):
        decay = jnp.exp2(rates * whole(others[g, 0]))
        up = jnp.where(g < level, decay * up + others[g, 1].astype(F32), up)
    down = jnp.zeros(block, F32)
    for g in reversed(range(groups)):
        decay = jnp.exp2(rates * whole(others[g, 1]))
        down = jnp.where(g > level, decay * down + others[g, 0].astype(F32), down)
    for j in range(PLANE):
        back[j, :, 0] = up.astype(BF16)
        up = decays[j] * up + got[j, :, 2].astype(F32)
    for j in reversed(range(PLANE)):
        back[j, :, 1] = down.astype(BF16)
        down = decays[j] * down + got[j, :, 0].astype(F32)

    third = []
    for k in range(1, PLANE):
        peer = lax.rem(mine + k, PLANE)
        copy = pltpu.make_async_remote_copy(
            src_ref=back.at[peer],
            dst_ref=entering.at[here],
            send_sem=send3.at[k],
            recv_sem=recv3.at[k],
            device_id=(base + peer,),
            device_id_type=MESH,
        )
        copy.start()
        third.append(copy)
    entering[here] = back[mine]
    for copy in third:
        copy.wait_recv()
    for copy in first + second + third:
        copy.wait_send()


def carries(sums, rate, count):
    rows, _, states, _ = sums.shape
    share = rows // PLANE
    groups = count // PLANE
    entering = pl.pallas_call(
        functools.partial(carry_kernel, count),
        in_specs=[VMEM, VMEM],
        out_specs=VMEM,
        out_shape=shaped((rows, 2, states, LANES), BF16),
        scratch_shapes=[
            pltpu.VMEM((PLANE, share, 3, states, LANES), BF16),
            pltpu.VMEM((3, share, states, LANES), BF16),
            pltpu.VMEM((groups, 2, share, states, LANES), BF16),
            pltpu.VMEM((PLANE, share, 2, states, LANES), BF16),
            pltpu.SemaphoreType.DMA((PLANE,)),
            pltpu.SemaphoreType.DMA((PLANE,)),
            pltpu.SemaphoreType.DMA((groups,)),
            pltpu.SemaphoreType.DMA((groups,)),
            pltpu.SemaphoreType.DMA((PLANE,)),
            pltpu.SemaphoreType.DMA((PLANE,)),
        ],
        compiler_params=pltpu.CompilerParams(
            collective_id=0, has_side_effects=True, vmem_limit_bytes=32 * MIB
        ),
        name="carries",
    )(sums, rate)
    return entering.reshape(2, rows // 2, 2, states, LANES)


def pipelined(chunks, compute, finish, carry):
    carry = compute(0, 0, carry)

    def pair(i, carry):
        carry = compute(2 * i + 1, 1, carry)
        finish(2 * i, 0)
        carry = compute(2 * i + 2, 0, carry)
        finish(2 * i + 1, 1)
        return carry

    carry = lax.fori_loop(0, chunks // 2 - 1, pair, carry)
    carry = compute(chunks - 1, 1, carry)
    finish(chunks - 2, 0)
    finish(chunks - 1, 1)
    return carry


def states_kernel(masked, driven, seed, in_spread, out_blk, rate, entering, mixed, out_grad, kept, r00, r01, r10, r11):
    tokens, cols = seed.shape
    per = cols // LANES
    states = rate.shape[1]
    chunks = tokens // CHUNK
    rows = ((r00, r01), (r10, r11))

    @pl.when(pl.program_id(0) == 0)
    def _():
        out_grad[...] = jnp.zeros_like(out_grad)

    mixed[...] = jnp.zeros_like(mixed)
    for c in range(per):
        lanes = pl.ds(c * LANES, LANES)
        kept[0, 0:states, lanes] = entering[0, c, 0]
        kept[1, tokens * states : (tokens + 1) * states, lanes] = entering[1, c, 1]

    def first_of(d, i):
        return pl.multiple_of((i if d == 0 else chunks - 1 - i) * CHUNK, CHUNK)

    def compute(i, side, carry):
        carry = list(carry)
        for k in range(CHUNK):
            for d in range(2):
                first = first_of(d, i)
                j = k if d == 0 else CHUNK - 1 - k
                in_row = in_spread[d, first + j]
                for c in range(per):
                    lanes = pl.ds(c * LANES, LANES)
                    now = jnp.exp2(row_of(masked.at[d], first, j, lanes) * rate[d, :, lanes])
                    state = now * carry[d * per + c] + in_row * row_of(
                        driven.at[d], first, j, lanes
                    )
                    rows[side][d][j * states : (j + 1) * states, lanes] = state.astype(BF16)
                    carry[d * per + c] = state
        return tuple(carry)

    def finish(i, side):
        for d in range(2):
            first = first_of(d, i)
            here = pl.ds(first, CHUNK)
            slot = pl.multiple_of((first + 1 - d) * states, states)
            block = rows[side][d][...]
            kept[d, pl.ds(slot, CHUNK * states), :] = block
            mixed[here, :] += dot(out_blk[d, here, :], block)
            out_grad[d, here, :] += contract_cols(seed[here, :].astype(BF16), block)

    start = tuple(entering[d, c, d].astype(F32) for d in range(2) for c in range(per))
    pipelined(chunks, compute, finish, start)


def block_specs(tokens, states):
    wide = CHUNK * states
    return dict(
        both=pl.BlockSpec((2, tokens, COLS), lambda b: (0, 0, b)),
        rows=pl.BlockSpec((tokens, COLS), lambda b: (0, b)),
        spread=pl.BlockSpec((2, tokens, states, LANES), lambda b: (0, 0, 0, 0)),
        diag=pl.BlockSpec((2, tokens, wide), lambda b: (0, 0, 0)),
        rate=pl.BlockSpec((2, states, COLS), lambda b: (0, 0, b)),
        entering=pl.BlockSpec((2, COLS // LANES, 2, states, LANES), lambda b: (0, b, 0, 0, 0)),
        kept=pl.BlockSpec((2, (tokens + 1) * states, COLS), lambda b: (0, 0, b)),
    )


def run_states(h, entering):
    tokens, inner = h["seed"].shape
    states = h["rate"].shape[1]
    s = block_specs(tokens, states)
    return pl.pallas_call(
        states_kernel,
        grid=(inner // COLS,),
        in_specs=[s["both"], s["both"], s["rows"], s["spread"], s["diag"], s["rate"], s["entering"]],
        out_specs=[s["rows"], s["diag"], s["kept"]],
        out_shape=[
            shaped((tokens, inner)),
            shaped((2, tokens, CHUNK * states)),
            shaped((2, (tokens + 1) * states, inner), BF16),
        ],
        scratch_shapes=[pltpu.VMEM((CHUNK * states, COLS), BF16)] * 4,
        compiler_params=pltpu.CompilerParams(vmem_limit_bytes=48 * MIB),
        name="states",
    )(h["masked"], h["driven"], h["seed"], h["in_spread"], h["out_blk"], h["rate"], entering)


def slot_of(o, count, order):
    bits = [o & 1, o >> 1 & 1, o >> 2 & 1]
    groups = count // PLANE
    later = (bits[1], bits[2]) if order == "xy" else (bits[2], bits[1])
    return bits[0], (later[0] * 2 + later[1]) * groups + o // PLANE


def slot_rows(count, inner):
    rows = inner // count
    return rows + -rows % 16


def stacked_rows(source, stage, o, rows):
    half = source.shape[1] // 2
    part = pl.ds(o * rows, rows)
    if rows % 8 == 0:
        return jnp.concatenate([source[part, :half], source[part, half:]], axis=0)
    stage[0:rows, :] = source[part, :half]
    stage[rows : 2 * rows, :] = source[part, half:]
    return stage[...]


def mid_kernel(
    count,
    states_sum,
    active,
    d_skip,
    gate_branch,
    gated_grad,
    gate_rows,
    branch_grad,
    mixer_own,
    hidden,
    grad_out,
    w_out,
    output,
    gate_grad,
    gate_branch_grad,
    slots_out,
    slots_gate,
    gated,
    branch,
    whole_out,
    whole_gate,
    stage,
):
    tokens, inner = states_sum.shape
    model = hidden.shape[1]
    branch[...] = jnp.zeros_like(branch)

    def block(b, none):
        cols = pl.ds(pl.multiple_of(b * COLS, COLS), COLS)
        mixed = states_sum[:, cols]
        for d in range(2):
            mixed = mixed + d_skip[d : d + 1, cols] * active[d, :, cols].astype(F32)
        gate = gate_branch[:, cols]
        sigma = sigmoid(gate)
        now = (mixed * (gate * sigma)).astype(BF16)
        gated[:, cols] = now
        slope = sigma * (1.0 + gate * (1.0 - sigma))
        back = (gated_grad[:, cols] * mixed * slope).astype(BF16)
        gate_branch_grad[:, cols] = back
        branch[...] += dot(now, w_out[cols, :])
        whole_out[cols, :] = contract_rows(now, branch_grad[...])
        whole_gate[:, cols] = contract_rows(mixer_own[...], back)
        return none

    lax.fori_loop(0, inner // COLS, block, 0)
    output[...] = (hidden[...].astype(F32) + gate_rows[...] * branch[...]).astype(BF16)
    gate_grad[...] = grad_out[...].astype(F32) * branch[...]
    rows, mrows = inner // count, model // count
    for o in range(count):
        first, rest = slot_of(o, count, "xy")
        slots_out[first, rest, 0:rows] = whole_out[o * rows : (o + 1) * rows, :].astype(BF16)
        first, rest = slot_of(o, count, "yx")
        slots_gate[first, rest] = stacked_rows(whole_gate, stage, o, mrows).astype(BF16)


def run_mid(h, count, states_sum, d_skip, hidden, grad_out, w_out):
    tokens, inner = states_sum.shape
    model = hidden.shape[1]
    slots = shaped((2, count // 2, slot_rows(count, inner), model), BF16)
    return pl.pallas_call(
        functools.partial(mid_kernel, count),
        in_specs=[VMEM] * 11,
        out_specs=[VMEM] * 5,
        out_shape=[
            shaped((tokens, model), BF16),
            shaped((tokens, model)),
            shaped((tokens, inner), BF16),
            slots,
            slots,
        ],
        scratch_shapes=[
            pltpu.VMEM((tokens, inner), BF16),
            pltpu.VMEM((tokens, model), F32),
            pltpu.VMEM((inner, model), F32),
            pltpu.VMEM((model, inner), F32),
            pltpu.VMEM((slot_rows(count, inner), model), F32),
        ],
        compiler_params=pltpu.CompilerParams(vmem_limit_bytes=56 * MIB),
        name="mid",
    )(
        states_sum,
        h["active"],
        d_skip,
        h["gate_branch"],
        h["gated_grad"],
        h["gate_rows"],
        h["branch_grad"],
        h["mixer_own"],
        hidden,
        grad_out,
        w_out,
    )


class Place:
    def __init__(self, count):
        self.count = count
        self.groups = count // PLANE
        self.me = lax.axis_index("seq")
        self.bits = [lax.rem(self.me, 2), lax.rem(self.me // 2, 2), lax.rem(self.me // 4, 2)]
        self.flips = [self.me + (1 - 2 * self.bits[i]) * (1 << i) for i in range(3)]
        self.level = self.me // PLANE
        self.low = lax.rem(self.me, PLANE)
        self.left = lax.rem(self.me + count - 1, count)
        self.right = lax.rem(self.me + 1, count)
        self.far = [lax.rem(self.level + k, self.groups) for k in range(1, self.groups)]

    def meet(self):
        barrier = pltpu.get_barrier_semaphore()
        peers = self.flips + [self.left, self.right] + [g * PLANE + self.low for g in self.far]
        for peer in peers:
            pl.semaphore_signal(barrier, inc=1, device_id=(peer,), device_id_type=MESH)
        pl.semaphore_wait(barrier, len(peers))


def remote(src, dst, sems, slot, peer):
    return pltpu.make_async_remote_copy(
        src_ref=src,
        dst_ref=dst,
        send_sem=sems[0].at[slot],
        recv_sem=sems[1].at[slot],
        device_id=(peer,),
        device_id_type=MESH,
    )


def add_into(into, own, first):
    def one(i, none):
        into[i] = into[i] + own[first + i]
        return none

    lax.fori_loop(0, into.shape[0], one, 0)


class Halving:
    def __init__(self, place, orders, parts, owns, got, sems):
        self.place, self.orders, self.parts, self.owns = place, orders, parts, owns
        self.got1, self.got2, self.got3, self.got4 = got
        self.sems = sems
        self.number = len(orders)

    def turns(self, p):
        return (1, 2) if self.orders[p] == "xy" else (2, 1)

    def first(self, p):
        bit = self.place.bits[0]
        return remote(
            self.parts[p].at[1 - bit], self.got1[p], self.sems, p, self.place.flips[0]
        )

    def second(self, p):
        i, _ = self.turns(p)
        half = 2 * self.place.groups
        src = self.got1[p].at[pl.ds((1 - self.place.bits[i]) * half, half)]
        return remote(src, self.got2[p], self.sems, self.number + p, self.place.flips[i])

    def third(self, p):
        _, j = self.turns(p)
        half = self.place.groups
        src = self.got2[p].at[pl.ds((1 - self.place.bits[j]) * half, half)]
        return remote(src, self.got3[p], self.sems, 2 * self.number + p, self.place.flips[j])

    def fourth(self, p):
        copies = []
        for k, g in enumerate(self.place.far):
            slot = 3 * self.number + p * len(self.place.far) + k
            copies.append(
                remote(
                    self.got3[p].at[g],
                    self.got4[p].at[self.place.level],
                    self.sems,
                    slot,
                    g * PLANE + self.place.low,
                )
            )
        return copies

    def start(self, p):
        self.first(p).start()

    def step2(self, p):
        self.first(p).wait_recv()
        add_into(self.got1[p], self.owns[p], 0)
        self.second(p).start()

    def step3(self, p):
        i, _ = self.turns(p)
        self.second(p).wait_recv()
        add_into(self.got2[p], self.got1[p], self.place.bits[i] * 2 * self.place.groups)
        self.third(p).start()

    def step4(self, p):
        _, j = self.turns(p)
        self.third(p).wait_recv()
        add_into(self.got3[p], self.got2[p], self.place.bits[j] * self.place.groups)
        for copy in self.fourth(p):
            copy.start()
        self.got4[p][self.place.level] = self.got3[p][self.place.level]

    def end(self, p, share):
        for copy in self.fourth(p):
            copy.wait_recv()
        total = self.got4[p][0].astype(F32)
        for g in range(1, self.place.groups):
            total = total + self.got4[p][g].astype(F32)
        share[...] = total
        for copy in [self.first(p), self.second(p), self.third(p)] + self.fourth(p):
            copy.wait_send()

    def all(self, step):
        for p in range(self.number):
            getattr(self, step)(p)


def halving_sems(number, groups):
    return [pltpu.SemaphoreType.DMA((3 * number + number * (groups - 1),))] * 2


def halving_slots(shapes, groups):
    return [
        pltpu.VMEM((size,) + shape, BF16)
        for size in (4 * groups, 2 * groups, groups, groups)
        for shape in shapes
    ]


BLOCKED = ("masked", "driven", "seed", "rate", "entering", "kept")
FIXED = ("out_spread", "in_blk", "d_skip", "conv_w")
FETCHED = (
    "out_acc",
    "rank_low",
    "w_dt",
    "logit",
    "active",
    "seed_all",
    "w_x",
    "conv_sum",
    "conv_keep",
    "masks",
    "mixer",
    "w_in",
    "gate_branch_grad",
    "hot",
    "normed",
    "gate_grad",
)
BACK_OUT = ("norm_wide", "share_out", "share_gate", "share_a", "share_b", "mod", "edges")
BACK_SCRATCH = (
    "decay_grad",
    "driven_grad",
    "in_acc",
    "small",
    "adj00",
    "adj01",
    "adj10",
    "adj11",
    "slope00",
    "slope01",
    "slope10",
    "slope11",
    "active_grad",
    "rank_grad",
    "proj_grad",
    "conv_wide",
    "input_wide",
    "whole_conv",
    "whole_cols",
    "stage",
    "late_a",
    "late_b",
    "mod_part",
    "m1",
    "m2",
    "m3",
    "m4",
    "edge_got",
    "own_out",
    "own_gate",
)


class Refs:
    def __init__(self, names, refs):
        for name, ref in zip(names, refs):
            setattr(self, name, ref)


def small_rows(taps):
    return 0, 2 * taps, 2 * taps + 2, 2 * taps + 4, 2 * taps + 8


def adjoint_block(r, b):
    tokens, cols = r.seed.shape
    per = cols // LANES
    states = r.rate.shape[1]
    taps = r.conv_w.shape[1]
    chunks = tokens // CHUNK
    wide = CHUNK * states
    adjs = ((r.adj00, r.adj01), (r.adj10, r.adj11))
    slopes = ((r.slope00, r.slope01), (r.slope10, r.slope11))
    at_cols = pl.ds(pl.multiple_of(b * cols, cols), cols)
    ones = (
        lax.broadcasted_iota(jnp.int32, (CHUNK, wide), 1) // states
        == lax.broadcasted_iota(jnp.int32, (CHUNK, wide), 0)
    ).astype(BF16)

    def first_of(d, i):
        return pl.multiple_of((chunks - 1 - i if d == 0 else i) * CHUNK, CHUNK)

    def compute(i, side, carry):
        carry = list(carry)
        for k in range(CHUNK):
            for d in range(2):
                first = first_of(d, i)
                slot = pl.multiple_of((first + d) * states, states)
                before = r.kept.at[d, pl.ds(slot, wide), :]
                j = CHUNK - 1 - k if d == 0 else k
                out_row = r.out_spread[d, first + j]
                part = slice(j * states, (j + 1) * states)
                for c in range(per):
                    lanes = pl.ds(c * LANES, LANES)
                    coming, total = carry[d * per + c]
                    step = row_of(r.masked.at[d], first, j, lanes)
                    now = jnp.exp2(step * r.rate[d, :, lanes])
                    adj = out_row * row_of(r.seed, first, j, lanes) + coming
                    coming = now * adj
                    slope = coming * before[part, lanes].astype(F32) * r.rate[d, :, lanes]
                    total = total + slope * step
                    adjs[side][d][part, lanes] = adj.astype(BF16)
                    slopes[side][d][part, lanes] = slope.astype(BF16)
                    carry[d * per + c] = (coming, total)
        return tuple(carry)

    def finish(i, side):
        for d in range(2):
            here = pl.ds(first_of(d, i), CHUNK)
            block = adjs[side][d][...]
            r.driven_grad[d, here, at_cols] = dot(r.in_blk[d, here, :], block)
            r.in_acc[d, here, :] += contract_cols(r.driven[d, here, :].astype(BF16), block)
            r.decay_grad[d, here, at_cols] = dot(ones, slopes[side][d][...]) * LN2

    zero = jnp.zeros((states, LANES), F32)
    start = tuple(
        (r.entering[d, c, 1 - d].astype(F32), zero) for d in range(2) for c in range(per)
    )
    carry = pipelined(chunks, compute, finish, start)
    at_rate = small_rows(taps)[4]
    for d in range(2):
        for c in range(per):
            lanes = tile_at(b * cols + c * LANES)
            r.small[at_rate + d * states : at_rate + (d + 1) * states, lanes] = (
                carry[d * per + c][1] * LN2
            )


def column_sum(values):
    return jnp.sum(values, axis=0, keepdims=True)


def through_steps(r):
    tokens, inner = r.seed_all.shape
    taps = r.conv_w.shape[1]
    rank = r.w_dt.shape[1]
    proj = r.w_x.shape[2]
    states = r.rate.shape[1]
    _, _, at_dt, at_skip, _ = small_rows(taps)
    r.rank_grad[...] = jnp.zeros_like(r.rank_grad)

    def block(b, none):
        cols = pl.ds(pl.multiple_of(b * COLS, COLS), COLS)
        for d in range(2):
            act = r.active[d, :, cols].astype(F32)
            value = r.logit[d, :, cols]
            back = r.driven_grad[d, :, cols]
            grown = r.seed_all[:, cols]
            grad = (r.decay_grad[d, :, cols] + back * act) * sigmoid(value)
            low = grad.astype(BF16)
            r.active_grad[d, :, cols] = back * softplus(value) + grown * r.d_skip[d : d + 1, cols]
            r.small[at_dt + d : at_dt + d + 1, cols] = column_sum(grad)
            r.small[at_skip + d : at_skip + d + 1, cols] = column_sum(grown * act)
            r.rank_grad[d] += contract_cols(low, r.w_dt[d, :, cols])
            start = 2 * proj + d * rank
            r.whole_cols[cols, start : start + rank] = contract_rows(low, r.rank_low[d])
        return none

    lax.fori_loop(0, inner // COLS, block, 0)

    place = lax.rem(lax.broadcasted_iota(jnp.int32, (tokens, CHUNK * states), 0), CHUNK)
    owner = lax.broadcasted_iota(jnp.int32, (tokens, CHUNK * states), 1) // states
    on_diag = place == owner
    column = lax.rem(lax.broadcasted_iota(jnp.int32, (CHUNK * states, states), 0), states)
    gather = (column == lax.broadcasted_iota(jnp.int32, (CHUNK * states, states), 1)).astype(BF16)
    for d in range(2):
        r.proj_grad[d, :, 0:rank] = r.rank_grad[d].astype(BF16)
        for start, acc in ((rank, r.in_acc), (rank + states, r.out_acc)):
            kept = jnp.where(on_diag, acc[d], 0.0).astype(BF16)
            r.proj_grad[d, :, start : start + states] = dot(kept, gather).astype(BF16)


def through_conv(r):
    tokens, inner = r.seed_all.shape
    taps = r.conv_w.shape[1]
    rank = r.w_dt.shape[1]
    proj = r.w_x.shape[2]
    at_conv, at_bias, _, _, _ = small_rows(taps)
    r.norm_wide[...] = jnp.zeros_like(r.norm_wide)

    def block(b, none):
        cols = pl.ds(pl.multiple_of(b * COLS, COLS), COLS)
        r.conv_wide[...] = r.conv_keep[:, cols].astype(F32)
        r.input_wide[...] = jnp.zeros_like(r.input_wide)
        for d in range(2):
            low = r.proj_grad[d]
            start = d * proj
            r.whole_cols[cols, start : start + proj] = contract_rows(r.active[d, :, cols], low)
            total = r.active_grad[d, :, cols] + contract_cols(low, r.w_x[d, cols, :])
            for c in range(COLS // LANES):
                lanes = tile_at(b * COLS + c * LANES)
                here = slice(c * LANES, (c + 1) * LANES)
                grad = total[:, here] * silu_slope(r.conv_sum[d, :, lanes])
                r.small[at_bias + d : at_bias + d + 1, lanes] = column_sum(grad)
                for k in range(taps):
                    offset = offset_of(d, k, taps)
                    window = slice(RIM + offset, RIM + offset + tokens)
                    part = grad * r.masks[offset + taps - 1]
                    at = at_conv + d * taps + k
                    r.small[at : at + 1, lanes] = column_sum(part * r.conv_wide[window, here])
                    r.input_wide[window, here] += r.conv_w[d, k : k + 1, lanes] * part
        low = r.input_wide[...].astype(BF16)
        r.whole_conv[:, cols] = contract_rows(r.mixer[...], low)
        r.norm_wide[...] += contract_cols(low, r.w_in[:, cols])
        gate_cols = pl.ds(pl.multiple_of(inner + b * COLS, COLS), COLS)
        r.norm_wide[RIM : RIM + tokens, :] += contract_cols(
            r.gate_branch_grad[:, cols], r.w_in[:, gate_cols]
        )
        r.whole_cols[cols, 2 * (proj + rank) :] = r.small[:, cols].T
        return none

    lax.fori_loop(0, inner // COLS, block, 0)


def fill_slots(r, count):
    inner = r.seed_all.shape[1]
    model = r.normed.shape[1]
    rows, mrows = inner // count, model // count
    cut = r.late_a.shape[3]
    rest = model - cut
    for o in range(count):
        both = stacked_rows(r.whole_conv, r.stage, o, mrows).astype(BF16)
        first, later = slot_of(o, count, "xy")
        r.late_a[first, later] = both[:, :cut]
        first, later = slot_of(o, count, "yx")
        r.late_b[first, later, :, 0:rest] = both[:, cut:]
        r.late_b[first, later, 0:rows, rest:] = r.whole_cols[o * rows : (o + 1) * rows, :].astype(
            BF16
        )


def modulation_sums(r):
    tokens = r.seed_all.shape[0]
    model = r.normed.shape[1]
    seqs = r.mod_part.shape[0]
    seq_rows = r.hot[:, 0:seqs]
    grads = r.norm_wide[...]
    r.mod_part[:, 0:model] = contract_rows(seq_rows, grads, HIGHEST)
    r.mod_part[:, model : 2 * model] = contract_rows(seq_rows, grads * r.normed[...], HIGHEST)
    r.mod_part[:, 2 * model :] = contract_rows(
        r.hot[RIM : RIM + tokens, 0:seqs], r.gate_grad[...], HIGHEST
    )


def back_kernel(count, *refs):
    refs = list(refs)

    def take(size):
        taken = refs[:size]
        del refs[:size]
        return taken

    blocked, fixed = take(len(BLOCKED)), take(len(FIXED))
    early = take(2)
    sources = take(len(FETCHED))
    out = take(len(BACK_OUT))
    scratch = take(len(BACK_SCRATCH))
    fetched = take(len(FETCHED))
    early_got = [take(2) for _ in range(4)]
    late_got = [take(2) for _ in range(4)]
    early_sems, late_sems, mod_sems = take(2), take(2), take(2)
    fetch_sems, own_sems = take(2)
    r = Refs(
        BLOCKED + FIXED + BACK_OUT + BACK_SCRATCH + FETCHED,
        blocked + fixed + out + scratch + fetched,
    )
    b = pl.program_id(0)
    blocks = pl.num_programs(0)
    place = Place(count)
    orders = ("xy", "yx")
    owns = (r.own_out, r.own_gate)
    one = Halving(place, orders, early, owns, early_got, early_sems)
    two = Halving(
        place,
        orders,
        (r.late_a, r.late_b),
        (r.late_a.at[place.bits[0]], r.late_b.at[place.bits[0]]),
        late_got,
        late_sems,
    )

    def fetch(i):
        return pltpu.make_async_copy(sources[i], fetched[i], fetch_sems.at[i])

    def own(p):
        return pltpu.make_async_copy(early[p].at[place.bits[0]], owns[p], own_sems.at[p])

    @pl.when(b == 0)
    def _():
        place.meet()
        one.all("start")
        for p in range(2):
            own(p).start()
        for i in range(len(FETCHED)):
            fetch(i).start()
        r.in_acc[...] = jnp.zeros_like(r.in_acc)
        r.small[...] = jnp.zeros_like(r.small)

    adjoint_block(r, b)

    @pl.when(b == 0)
    def _():
        for p in range(2):
            own(p).wait()
        one.all("step2")

    @pl.when(b == blocks - 2)
    def _():
        one.all("step3")

    @pl.when(b == blocks - 1)
    def _():
        for i in range(len(FETCHED)):
            fetch(i).wait()
        through_steps(r)
        one.all("step4")
        through_conv(r)
        fill_slots(r, count)
        two.all("start")
        far = len(place.far)
        edges = [
            remote(
                r.norm_wide.at[pl.ds(0, RIM)],
                r.edge_got.at[pl.ds(RIM, RIM)],
                mod_sems,
                3 + far,
                place.left,
            ),
            remote(
                r.norm_wide.at[pl.ds(r.norm_wide.shape[0] - RIM, RIM)],
                r.edge_got.at[pl.ds(0, RIM)],
                mod_sems,
                4 + far,
                place.right,
            ),
        ]
        for copy in edges:
            copy.start()
        modulation_sums(r)
        levels = ((r.mod_part, r.m1), (r.m1, r.m2), (r.m2, r.m3))
        mods = [
            remote(src, dst, mod_sems, i, place.flips[i]) for i, (src, dst) in enumerate(levels)
        ]
        last = [
            remote(r.m3, r.m4.at[place.level], mod_sems, 3 + k, g * PLANE + place.low)
            for k, g in enumerate(place.far)
        ]

        def mod_step(i):
            mods[i].wait_recv()
            levels[i][1][...] += levels[i][0][...]
            if i < 2:
                mods[i + 1].start()
                return
            for copy in last:
                copy.start()
            r.m4[place.level] = r.m3[...]

        mods[0].start()
        two.all("step2")
        mod_step(0)
        one.end(0, r.share_out)
        one.end(1, r.share_gate)
        two.step3(0)
        mod_step(1)
        two.step3(1)
        two.step4(0)
        mod_step(2)
        two.step4(1)
        for copy in last + edges:
            copy.wait_recv()
        r.edges[...] = r.edge_got[...]
        total = r.m4[0]
        for g in range(1, place.groups):
            total = total + r.m4[g]
        r.mod[...] = total
        two.end(0, r.share_a)
        two.end(1, r.share_b)
        for copy in mods + last + edges:
            copy.wait_send()


def column_width(proj, rank, taps, states):
    small = 2 * taps + 8 + 2 * states
    small = small + -small % 8
    total = 2 * (proj + rank) + small
    return small + -total % LANES, total + -total % LANES


def once(shape):
    return pl.BlockSpec(shape, lambda b: (0,) * len(shape), pipeline_mode=pl.Buffered(1))


def run_back(h, count, entering, kept, out_acc, mid_side, d_skip, conv_w, w_x, w_dt, w_in):
    gate_grad, gate_branch_grad, slots_out, slots_gate = mid_side
    tokens, inner = h["seed"].shape
    wide, model = h["normed"].shape
    groups = count // PLANE
    rank = w_dt.shape[1]
    proj = w_x.shape[2]
    states = h["rate"].shape[1]
    small, width = column_width(proj, rank, conv_w.shape[1], states)
    rows = slot_rows(count, inner)
    cut = (model + width) // 2 // LANES * LANES
    far = groups - 1
    given = dict(
        h,
        entering=entering,
        kept=kept,
        out_acc=out_acc,
        seed_all=h["seed"],
        gate_grad=gate_grad,
        gate_branch_grad=gate_branch_grad,
        d_skip=d_skip,
        conv_w=conv_w,
        w_x=w_x,
        w_dt=w_dt,
        w_in=w_in,
    )
    s = block_specs(tokens, states)
    kinds = dict(masked="both", driven="both", seed="rows", rate="rate", entering="entering", kept="kept")
    late = [(rows, cut), (rows, model + width - cut)]
    early = [(rows, model)] * 2
    diag = (CHUNK * states, COLS)
    mod = (8, 3 * model)
    scratch = dict(
        decay_grad=pltpu.VMEM((2, tokens, inner), F32),
        driven_grad=pltpu.VMEM((2, tokens, inner), F32),
        in_acc=pltpu.VMEM((2, tokens, CHUNK * states), F32),
        small=pltpu.VMEM((small, inner), F32),
        active_grad=pltpu.VMEM((2, tokens, inner), F32),
        rank_grad=pltpu.VMEM((2, tokens, rank), F32),
        proj_grad=pltpu.VMEM((2, tokens, proj), BF16),
        conv_wide=pltpu.VMEM((wide, COLS), F32),
        input_wide=pltpu.VMEM((wide, COLS), F32),
        whole_conv=pltpu.VMEM((model, inner), F32),
        whole_cols=pltpu.VMEM((inner, width), F32),
        stage=pltpu.VMEM((rows, model), F32),
        late_a=pltpu.VMEM((2, 4 * groups) + late[0], BF16),
        late_b=pltpu.VMEM((2, 4 * groups) + late[1], BF16),
        mod_part=pltpu.VMEM(mod, F32),
        m1=pltpu.VMEM(mod, F32),
        m2=pltpu.VMEM(mod, F32),
        m3=pltpu.VMEM(mod, F32),
        m4=pltpu.VMEM((groups,) + mod, F32),
        edge_got=pltpu.VMEM((2 * RIM, model), F32),
        own_out=pltpu.VMEM((4 * groups,) + early[0], BF16),
        own_gate=pltpu.VMEM((4 * groups,) + early[1], BF16),
    )
    outs = dict(
        norm_wide=shaped((wide, model)),
        share_out=shaped(early[0]),
        share_gate=shaped(early[1]),
        share_a=shaped(late[0]),
        share_b=shaped(late[1]),
        mod=shaped(mod),
        edges=shaped((2 * RIM, model)),
    )
    return pl.pallas_call(
        functools.partial(back_kernel, count),
        grid=(inner // COLS,),
        in_specs=[s[kinds[name]] for name in BLOCKED]
        + [once(given[name].shape) for name in FIXED]
        + [ANY] * (2 + len(FETCHED)),
        out_specs=[once(outs[name].shape) for name in BACK_OUT],
        out_shape=[outs[name] for name in BACK_OUT],
        scratch_shapes=[scratch.get(name, pltpu.VMEM(diag, BF16)) for name in BACK_SCRATCH]
        + [pltpu.VMEM(given[name].shape, given[name].dtype) for name in FETCHED]
        + halving_slots(early, groups)
        + halving_slots(late, groups)
        + halving_sems(2, groups)
        + halving_sems(2, groups)
        + [pltpu.SemaphoreType.DMA((5 + far,))] * 2
        + [pltpu.SemaphoreType.DMA((len(FETCHED),)), pltpu.SemaphoreType.DMA((2,))],
        compiler_params=pltpu.CompilerParams(
            collective_id=1, has_side_effects=True, vmem_limit_bytes=60 * MIB
        ),
        name="back",
    )(
        *[given[name] for name in BLOCKED + FIXED],
        slots_out,
        slots_gate,
        *[given[name] for name in FETCHED],
    )


def finish_kernel(
    count,
    proj,
    rank,
    taps,
    states,
    share_out,
    share_gate,
    share_a,
    share_b,
    mod,
    edges,
    my_cond,
    norm_wide,
    normed,
    rescale,
    scale1,
    grad_out,
    grad_x,
    w_mod,
    b_mod,
    w_in,
    conv_w,
    conv_b,
    w_x,
    w_dt,
    dt_bias,
    a_log,
    d_skip,
    w_out,
):
    me = lax.axis_index("seq")
    tokens, model = grad_out.shape
    mrows, double = w_in.shape
    inner = double // 2
    rows = w_out.shape[0]
    seqs = my_cond.shape[0]
    cut = share_a.shape[1]

    w_out[...] = share_out[0:rows, :]
    w_in[:, 0:cut] = share_a[0:mrows, :]
    w_in[:, cut:model] = share_b[0:mrows, 0 : model - cut]
    w_in[:, model : model + cut] = share_a[mrows : 2 * mrows, :]
    w_in[:, model + cut : inner] = share_b[mrows : 2 * mrows, 0 : model - cut]
    w_in[:, inner : inner + model] = share_gate[0:mrows, :]
    w_in[:, inner + model :] = share_gate[mrows : 2 * mrows, :]

    start = model - cut
    for d in range(2):
        w_x[d] = share_b[0:rows, start + d * proj : start + (d + 1) * proj]
    start = start + 2 * proj
    flipped = share_b[:, model - cut :].T
    at = 2 * proj
    for d in range(2):
        w_dt[d] = flipped[at + d * rank : at + (d + 1) * rank, 0:rows]
    at = at + 2 * rank
    for d in range(2):
        conv_w[d] = flipped[at + d * taps : at + (d + 1) * taps, 0:rows]
    at = at + 2 * taps
    conv_b[...] = flipped[at : at + 2, 0:rows]
    dt_bias[...] = flipped[at + 2 : at + 4, 0:rows]
    d_skip[...] = flipped[at + 4 : at + 6, 0:rows]
    at = at + 8
    for d in range(2):
        a_log[d] = flipped[at + d * states : at + (d + 1) * states, 0:rows]

    cond = my_cond[...]
    cond_act = (cond * sigmoid(cond)).astype(BF16).astype(F32)
    totals = mod[0:seqs, :]
    w_mod[...] = contract_rows(cond_act, totals, HIGHEST)
    b_mod[...] = jnp.sum(totals, axis=0, keepdims=True)

    norm_grad = norm_wide[RIM : RIM + tokens, :]
    low = jnp.where(me > 0, edges[0:RIM, :], 0.0)
    high = jnp.where(me < count - 1, edges[RIM:, :], 0.0)
    middle = jnp.zeros((tokens - 2 * RIM, model), F32)
    norm_grad = norm_grad + jnp.concatenate([low, middle, high], axis=0)
    scaled = norm_grad * scale1[...]
    normal = normed[RIM : RIM + tokens, :]
    grad_x[...] = grad_out[...].astype(F32) + rescale[:, 0:1] * (
        scaled
        - jnp.mean(scaled, axis=1, keepdims=True)
        - normal * jnp.mean(scaled * normal, axis=1, keepdims=True)
    )


def on_device(
    count,
    hidden,
    condition,
    seq_lengths,
    w_mod,
    b_mod,
    w_in,
    conv_w,
    conv_b,
    w_x,
    w_dt,
    dt_bias,
    a_log,
    d_skip,
    w_out,
    grad_out,
):
    tokens, model = hidden.shape
    inner = w_in.shape[1] // 2
    rank = w_dt.shape[1]
    proj = w_x.shape[2]
    states = a_log.shape[1]
    taps = conv_w.shape[1]
    seqs = condition.shape[0]
    me = lax.axis_index("seq")
    rows, mrows = inner // count, model // count

    below = lax.ppermute(hidden[-RIM:], "seq", [(i, i + 1) for i in range(count - 1)])
    above = lax.ppermute(hidden[:RIM], "seq", [(i + 1, i) for i in range(count - 1)])
    h = head(
        seq_lengths,
        hidden,
        below,
        above,
        condition,
        b_mod,
        conv_w,
        conv_b,
        dt_bias,
        a_log,
        grad_out,
        (w_mod, w_in, w_x, w_dt, w_out),
    )
    entering = carries(h["sums"], h["rate_tiles"], count)
    states_sum, out_acc, kept = run_states(h, entering)
    output, gate_grad, gate_branch_grad, slots_out, slots_gate = run_mid(
        h, count, states_sum, d_skip, hidden, grad_out, w_out
    )
    norm_wide, share_out, share_gate, share_a, share_b, mod, edges = run_back(
        h,
        count,
        entering,
        kept,
        out_acc,
        (gate_grad, gate_branch_grad, slots_out, slots_gate),
        d_skip,
        conv_w,
        w_x,
        w_dt,
        w_in,
    )
    my_cond = lax.dynamic_slice_in_dim(condition, me * mrows, mrows, axis=1)
    results = pl.pallas_call(
        functools.partial(finish_kernel, count, proj, rank, taps, states),
        in_specs=[VMEM] * 12,
        out_specs=[VMEM] * 12,
        out_shape=[
            shaped((tokens, model)),
            shaped((mrows, 3 * model)),
            shaped((1, 3 * model)),
            shaped((mrows, 2 * inner)),
            shaped((2, taps, rows)),
            shaped((2, rows)),
            shaped((2, rows, proj)),
            shaped((2, rank, rows)),
            shaped((2, rows)),
            shaped((2, states, rows)),
            shaped((2, rows)),
            shaped((rows, model)),
        ],
        compiler_params=pltpu.CompilerParams(vmem_limit_bytes=32 * MIB),
        name="finish",
    )(
        share_out,
        share_gate,
        share_a,
        share_b,
        mod,
        edges,
        my_cond,
        norm_wide,
        h["normed"],
        h["rescale"],
        h["scale1"],
        grad_out,
    )
    bias_cols = 3 * model // count
    share_b_mod = lax.dynamic_slice_in_dim(results[2][0], me * bias_cols, bias_cols, axis=0)
    return (output,) + tuple(results[:2]) + (share_b_mod,) + tuple(results[3:])


def solution(mesh):
    in_specs = (P("seq", None),) + (P(),) * 13 + (P("seq", None),)
    out_specs = (
        P("seq", None),
        P("seq", None),
        P("seq", None),
        P("seq"),
        P("seq", None),
        P(None, None, "seq"),
        P(None, "seq"),
        P(None, "seq", None),
        P(None, None, "seq"),
        P(None, "seq"),
        P(None, None, "seq"),
        P(None, "seq"),
        P("seq", None),
    )
    return jax.shard_map(
        functools.partial(on_device, mesh.shape["seq"]),
        mesh=mesh,
        in_specs=in_specs,
        out_specs=out_specs,
        check_vma=False,
    )
```

```python
import functools
import types

import jax
import jax.numpy as jnp
from jax import lax
from jax.experimental import pallas as pl
from jax.experimental.pallas import tpu as pltpu
from jax.sharding import PartitionSpec as P

EPSILON = 1e-06
HIGHEST = lax.Precision.HIGHEST
MESH = pl.DeviceIdType.MESH
LANES = 128
LOG2E = 1.4426950408889634
LN2 = 0.6931471805599453
CUT_STEP = 1e9
PLANE = 8
RIM = 8
CHUNK = 16
XY, YX = (1, 2), (2, 1)
COLS = 256
MIB = 1024 * 1024
F32 = jnp.float32
BF16 = jnp.bfloat16
VMEM = pl.BlockSpec(memory_space=pltpu.VMEM)
ANY = pl.BlockSpec(memory_space=pl.ANY)


def shaped(shape, dtype=F32):
    return jax.ShapeDtypeStruct(shape, dtype)


def dot(left, right, dims=((1,), (0,)), precision=None):
    return lax.dot_general(
        left, right, (dims, ((), ())), precision=precision, preferred_element_type=F32
    )


def contract_rows(left, right, precision=None):
    return dot(left, right, ((0,), (0,)), precision)


def contract_cols(left, right):
    return dot(left, right, ((1,), (1,)))


def sigmoid(values):
    return 1.0 / (1.0 + jnp.exp(-values))


def silu_slope(values):
    sigma = sigmoid(values)
    return sigma * (1.0 + values * (1.0 - sigma))


def softplus(values):
    return jnp.maximum(values, 0.0) + jnp.log1p(jnp.exp(-jnp.abs(values)))


def tile_at(start):
    return pl.ds(pl.multiple_of(start, LANES), LANES)


def row_of(ref, first, j, lanes):
    eight = pl.ds(pl.multiple_of(first + j // 8 * 8, 8), 8)
    return ref.at[eight, lanes][j % 8 : j % 8 + 1, :]


def segments(positions, bounds):
    total = jnp.full(positions.shape, -1, jnp.int32)
    for bound in bounds:
        total = total + (positions >= bound).astype(jnp.int32)
    return total


def read_bounds(lengths):
    bounds = [jnp.int32(0)]
    for j in range(lengths.shape[0]):
        bounds.append(bounds[-1] + lengths[j])
    return bounds


def rows_iota(rows):
    return lax.broadcasted_iota(jnp.int32, (rows, LANES), 0)


def offset_of(d, k, taps):
    return k - (taps - 1) if d == 0 else taps - 1 - k


def slot_of(o, count, order):
    bits = [o & 1, o >> 1 & 1, o >> 2 & 1]
    return bits[0], (bits[order[0]] * 2 + bits[order[1]]) * (count // PLANE) + o // PLANE


def slot_rows(count, inner):
    rows = inner // count
    return rows + -rows % 16


def stacked_rows(source, stage, o, rows, begin, end):
    middle = (begin + end) // 2
    part = pl.ds(o * rows, rows)
    if rows % 8 == 0:
        return jnp.concatenate([source[part, begin:middle], source[part, middle:end]], axis=0)
    stage[0:rows, :] = source[part, begin:middle]
    stage[rows : 2 * rows, :] = source[part, middle:end]
    return stage[...]


class Refs:
    def __init__(self, names, refs):
        for name, ref in zip(names, refs):
            setattr(self, name, ref)


def token_masks(r, first):
    tokens = r.hidden.shape[0]
    wide = r.normed.shape[0]
    taps = r.conv_w.shape[1]
    bounds = read_bounds(r.lengths)
    position = first + rows_iota(tokens)
    segment = segments(position, bounds)
    for offset in range(1 - taps, taps):
        r.masks[offset + taps - 1] = (segments(position + offset, bounds) == segment).astype(F32)
    wide_segment = segments(first - RIM + rows_iota(wide), bounds)
    lane = lax.broadcasted_iota(jnp.int32, (wide, LANES), 1)
    r.hot[...] = (wide_segment == lane).astype(F32)
    return segment, wide_segment


def normalise(r, below, above):
    tokens = r.hidden.shape[0]
    x = jnp.concatenate([below, r.hidden[...].astype(F32), above], axis=0)
    centered = x - jnp.mean(x, axis=1, keepdims=True)
    scaling = lax.rsqrt(jnp.mean(centered * centered, axis=1, keepdims=True) + EPSILON)
    r.normed[...] = centered * scaling
    r.rescale[...] = jnp.broadcast_to(scaling[RIM : RIM + tokens], (tokens, LANES))


def modulate(r, segment, wide_segment):
    tokens, model = r.hidden.shape
    seqs = r.condition.shape[0]
    for c in range(model // LANES):
        lanes = slice(c * LANES, (c + 1) * LANES)

        def rows_for(part, segs):
            total = jnp.zeros(segs.shape, F32)
            at = part * model + c * LANES
            bias = r.b_mod[at // LANES : at // LANES + 1, :]
            for j in range(seqs):
                row = r.modulation[j : j + 1, at : at + LANES] + bias
                total = jnp.where(segs == j, row, total)
            return total

        one_scale = 1.0 + rows_for(1, wide_segment)
        mixed_in = r.normed[:, lanes] * one_scale + rows_for(0, wide_segment)
        r.mixer[:, lanes] = mixed_in.astype(BF16)
        r.mixer_own[:, lanes] = mixed_in[RIM : RIM + tokens].astype(BF16)
        r.scale1[:, lanes] = one_scale[RIM : RIM + tokens]
        gate = rows_for(2, segment)
        r.gate_rows[:, lanes] = gate
        r.branch_grad[:, lanes] = (r.grad_out[:, lanes].astype(F32) * gate).astype(BF16)


def project(r):
    tokens, inner = r.seed.shape
    taps = r.conv_w.shape[1]
    r.proj[...] = jnp.zeros_like(r.proj)

    def block(b, none):
        cols = pl.ds(pl.multiple_of(b * COLS, COLS), COLS)
        conv = dot(r.mixer[...], r.w_conv[:, cols]).astype(BF16)
        r.conv_keep[:, cols] = conv
        r.conv_wide[...] = conv.astype(F32)
        gate = dot(r.mixer_own[...], r.w_gate[:, cols])
        r.gate_branch[:, cols] = gate
        back = contract_cols(r.branch_grad[...], r.w_out[cols, :])
        r.gated_grad[:, cols] = back
        r.seed[:, cols] = back * (gate * sigmoid(gate))
        for d in range(2):
            acts = []
            for c in range(COLS // LANES):
                lanes = tile_at(b * COLS + c * LANES)
                here = slice(c * LANES, (c + 1) * LANES)
                total = jnp.broadcast_to(r.conv_b[d : d + 1, lanes], (tokens, LANES))
                for k in range(taps):
                    offset = offset_of(d, k, taps)
                    total = total + r.conv_w[d, k : k + 1, lanes] * (
                        r.conv_wide[RIM + offset : RIM + offset + tokens, here]
                        * r.masks[offset + taps - 1]
                    )
                r.conv_sum[d, :, lanes] = total
                act = (total * sigmoid(total)).astype(BF16)
                r.active[d, :, lanes] = act
                acts.append(act)
            r.proj[d] += contract_cols(jnp.concatenate(acts, axis=1), r.w_x[d, :, cols])
        return none

    lax.fori_loop(0, inner // COLS, block, 0)


def coefficients(r):
    tokens = r.seed.shape[0]
    rank = r.w_dt.shape[1]
    states = r.rate.shape[1]
    place = lax.rem(lax.broadcasted_iota(jnp.int32, (tokens, CHUNK * states), 0), CHUNK)
    owner = lax.broadcasted_iota(jnp.int32, (tokens, CHUNK * states), 1) // states
    on_diag = place == owner
    column = lax.rem(lax.broadcasted_iota(jnp.int32, (states, CHUNK * states), 1), states)
    repeat = (column == lax.broadcasted_iota(jnp.int32, (states, CHUNK * states), 0)).astype(BF16)
    for d in range(2):
        whole = r.proj[d]
        r.rank_low[d] = whole[:, :rank].astype(BF16)
        flipped = whole.T
        for start, blk, spread in (
            (rank, r.in_blk, r.in_spread),
            (rank + states, r.out_blk, r.out_spread),
        ):
            coef = whole[:, start : start + states].astype(BF16)
            blk[d] = jnp.where(on_diag, dot(coef, repeat), 0.0).astype(BF16)
            rows = flipped[start : start + states, :]
            for t in range(tokens):
                spread[d, t] = jnp.broadcast_to(rows[:, t : t + 1], (states, LANES))


def stepping(r):
    inner = r.seed.shape[1]
    taps = r.conv_w.shape[1]

    def block(b, none):
        cols = pl.ds(pl.multiple_of(b * COLS, COLS), COLS)
        for d in range(2):
            value = dot(r.rank_low[d], r.w_dt[d, :, cols]) + r.dt_bias[d : d + 1, cols]
            step = softplus(value)
            keep = r.masks[taps - 2] if d == 0 else r.masks[taps]
            keep = jnp.concatenate([keep] * (COLS // LANES), axis=1)
            r.logit[d, :, cols] = value
            r.masked[d, :, cols] = jnp.where(keep > 0.5, step, CUT_STEP)
            r.driven[d, :, cols] = step * r.active[d, :, cols].astype(F32)
        return none

    lax.fori_loop(0, inner // COLS, block, 0)


def summarise(r, begin, end):
    tokens, inner = r.seed.shape
    states = r.rate.shape[1]
    tiles = inner // LANES
    per = COLS // LANES

    def block(b, none):
        lanes = [tile_at(b * COLS + c * LANES) for c in range(per)]

        def group(i, carry):
            carry = list(carry)
            for k in range(8):
                for d in range(2):
                    start = pl.multiple_of((i if d == 0 else tokens // 8 - 1 - i) * 8, 8)
                    j = k if d == 0 else 7 - k
                    in_row = r.in_spread[d, start + j]
                    out_row = r.out_spread[d, start + j]
                    for c in range(per):
                        state, decay, adj = carry[d * per + c]
                        now = jnp.exp2(
                            row_of(r.masked.at[d], start, j, lanes[c]) * r.rate[d, :, lanes[c]]
                        )
                        state = now * state + in_row * row_of(r.driven.at[d], start, j, lanes[c])
                        decay = decay * now
                        adj = adj + decay * (out_row * row_of(r.seed, start, j, lanes[c]))
                        carry[d * per + c] = (state, decay, adj)
            return tuple(carry)

        zero = jnp.zeros((states, LANES), F32)
        one = jnp.ones((states, LANES), F32)
        carry = lax.fori_loop(
            0, tokens // 8, group, tuple((zero, one, zero) for _ in range(2 * per))
        )
        for d in range(2):
            for c in range(per):
                state, decay, adj = carry[d * per + c]
                down, up = (adj, state) if d == 0 else (state, adj)
                at = d * tiles + b * per + c
                r.sums[at, 0] = down.astype(BF16)
                r.sums[at, 1] = three_pieces(
                    jnp.sum(r.masked[d, :, lanes[c]], axis=0, keepdims=True), states
                )
                r.sums[at, 2] = up.astype(BF16)
        return none

    lax.fori_loop(begin, end, block, 0)


def three_pieces(row, states):
    high = row.astype(BF16).astype(F32)
    middle = (row - high).astype(BF16).astype(F32)
    lowest = row - high - middle
    at = lax.broadcasted_iota(jnp.int32, (states, row.shape[-1]), 0)
    return jnp.where(
        at == 0, high, jnp.where(at == 1, middle, jnp.where(at == 2, lowest, 0.0))
    ).astype(BF16)


def remote(src, dst, sems, slot, peer, there=None):
    return pltpu.make_async_remote_copy(
        src_ref=src,
        dst_ref=dst,
        send_sem=sems[0].at[slot],
        recv_sem=sems[1].at[slot if there is None else there],
        device_id=(peer,),
        device_id_type=MESH,
    )


class Carries:
    def __init__(self, r, count, sems):
        self.r, self.sems = r, sems
        self.groups = count // PLANE
        self.me = lax.axis_index("seq")
        self.mine = lax.rem(self.me, PLANE)
        self.level = self.me // PLANE
        self.base = self.level * PLANE
        self.share = r.sums.shape[0] // PLANE

    def rows(self, j):
        return pl.ds(j * self.share, self.share)

    def out(self, j):
        r = self.r
        src, dst = r.sums.at[self.rows(j)], r.got.at[self.mine]
        return remote(src, dst, self.sems[0], j, self.base + j, self.mine)

    def send(self, j):
        @pl.when(self.mine != j)
        def _():
            self.out(j).start()

    def back(self, j):
        r = self.r
        src, dst = r.back.at[j], r.entering.at[self.rows(self.mine)]
        return remote(src, dst, self.sems[2], j, self.base + j, self.mine)

    def arrival(self, phase, s):
        r = self.r
        src, dst = (r.sums.at[self.rows(s)], r.got.at[s])
        if phase == 2:
            src, dst = r.back.at[s], r.entering.at[self.rows(s)]
        return remote(src, dst, self.sems[phase], s, self.base + s)

    def await_all(self, phase):
        for s in range(PLANE):

            @pl.when(self.mine != s)
            def _():
                self.arrival(phase, s).wait_recv()

    def between(self):
        r = self.r
        copies = []
        for k in range(1, self.groups):
            other = lax.rem(self.level + k, self.groups)
            start = jnp.where(other > self.level, 1, 0)
            copies.append(
                remote(
                    r.total.at[pl.ds(start, 2)],
                    r.others.at[self.level],
                    self.sems[1],
                    k,
                    other * PLANE + self.mine,
                )
            )
        return copies

    def exchange(self):
        r = self.r
        states = r.rate.shape[1]
        mine, level, share = self.mine, self.level, self.share
        r.got[mine] = r.sums[self.rows(mine)]
        r.others[level] = jnp.zeros(r.others.shape[1:], BF16)
        tiles = r.rate.shape[2] // LANES
        rates = []
        for c in range(share):
            at = mine * share + c
            rates.append(r.rate[at // tiles, :, tile_at(lax.rem(at, tiles) * LANES)][None])
        rates = jnp.concatenate(rates, axis=0)
        self.await_all(0)

        def whole(pieces):
            pieces = pieces.astype(F32)
            return pieces[:, 0:1] + pieces[:, 1:2] + pieces[:, 2:3]

        block = (share, states, LANES)
        times = [whole(r.got[j, :, 1]) for j in range(PLANE)]
        decays = [jnp.exp2(rates * time) for time in times]
        up = jnp.zeros(block, F32)
        down = jnp.zeros(block, F32)
        time = times[0]
        for j in range(PLANE):
            up = decays[j] * up + r.got[j, :, 2].astype(F32)
            if j:
                time = time + times[j]
        for j in reversed(range(PLANE)):
            down = decays[j] * down + r.got[j, :, 0].astype(F32)
        r.total[0] = down.astype(BF16)
        for c in range(share):
            r.total[1, c] = three_pieces(time[c], states)
        r.total[2] = up.astype(BF16)
        second = self.between()
        for copy in second:
            copy.start()
        for copy in second:
            copy.wait_recv()

        up = jnp.zeros(block, F32)
        for g in range(self.groups):
            decay = jnp.exp2(rates * whole(r.others[g, 0]))
            up = jnp.where(g < level, decay * up + r.others[g, 1].astype(F32), up)
        down = jnp.zeros(block, F32)
        for g in reversed(range(self.groups)):
            decay = jnp.exp2(rates * whole(r.others[g, 1]))
            down = jnp.where(g > level, decay * down + r.others[g, 0].astype(F32), down)
        for j in range(PLANE):
            r.back[j, :, 0] = up.astype(BF16)
            up = decays[j] * up + r.got[j, :, 2].astype(F32)
        for j in reversed(range(PLANE)):
            r.back[j, :, 1] = down.astype(BF16)
            down = decays[j] * down + r.got[j, :, 0].astype(F32)
        for j in range(PLANE):

            @pl.when(mine != j)
            def _():
                self.back(j).start()

        r.entering[self.rows(mine)] = r.back[mine]
        self.await_all(2)

    def finish(self):
        for j in range(PLANE):

            @pl.when(self.mine != j)
            def _():
                self.out(j).wait_send()
                self.back(j).wait_send()

        for copy in self.between():
            copy.wait_send()


def interleaved(chunks, compute, pieces, carry):
    jobs = []
    for i in range(chunks):
        carry = compute(i, i % 2, carry, jobs)
        jobs = pieces(i, i % 2)
    for job in jobs:
        job()
    return carry


def jobs_between(jobs, k):
    every = max(CHUNK // max(len(jobs), 1), 1)
    if jobs and k % every == 0 and k // every < len(jobs):
        jobs[k // every]()


def forward_block(r, b, kept):
    tokens, inner = r.seed.shape
    tiles = inner // LANES
    per = COLS // LANES
    states = r.rate.shape[1]
    chunks = tokens // CHUNK
    rows = ((r.rows00, r.rows01), (r.rows10, r.rows11))
    cols = pl.ds(pl.multiple_of(b * COLS, COLS), COLS)
    lanes = [tile_at(b * COLS + c * LANES) for c in range(per)]
    first_tile = [d * tiles + b * per for d in range(2)]
    for c in range(per):
        here = pl.ds(c * LANES, LANES)
        kept[0, 0:states, here] = r.entering[first_tile[0] + c, 0]
        kept[1, tokens * states : (tokens + 1) * states, here] = r.entering[first_tile[1] + c, 1]
    r.mixed[:, cols] = jnp.zeros((tokens, COLS), F32)

    def first_of(d, i):
        return (i if d == 0 else chunks - 1 - i) * CHUNK

    def compute(i, side, carry, jobs):
        carry = list(carry)
        for k in range(CHUNK):
            jobs_between(jobs, k)
            for d in range(2):
                first = first_of(d, i)
                j = k if d == 0 else CHUNK - 1 - k
                in_row = r.in_spread[d, first + j]
                for c in range(per):
                    now = jnp.exp2(
                        row_of(r.masked.at[d], first, j, lanes[c]) * r.rate[d, :, lanes[c]]
                    )
                    state = now * carry[d * per + c] + in_row * row_of(
                        r.driven.at[d], first, j, lanes[c]
                    )
                    rows[side][d][
                        j * states : (j + 1) * states, c * LANES : (c + 1) * LANES
                    ] = state.astype(BF16)
                    carry[d * per + c] = state
        return tuple(carry)

    def pieces(i, side):
        def keep(d, q):
            half = CHUNK * states // 2
            slot = (first_of(d, i) + 1 - d) * states + q * half
            kept[d, slot : slot + half, :] = rows[side][d][q * half : (q + 1) * half, :]

        def mix(d):
            here = pl.ds(first_of(d, i), CHUNK)
            r.mixed[here, cols] += dot(r.out_blk[d, here, :], rows[side][d][...])

        def grad(d):
            here = pl.ds(first_of(d, i), CHUNK)
            r.out_acc[d, here, :] += contract_cols(
                r.seed[here, cols].astype(BF16), rows[side][d][...]
            )

        jobs = []
        for d in range(2):
            jobs += [
                functools.partial(mix, d),
                functools.partial(keep, d, 0),
                functools.partial(grad, d),
                functools.partial(keep, d, 1),
            ]
        return jobs

    start = tuple(
        r.entering[first_tile[d] + c, d].astype(F32) for d in range(2) for c in range(per)
    )
    interleaved(chunks, compute, pieces, start)


def output_side(r, count):
    tokens, inner = r.mixed.shape
    model = r.hidden.shape[1]
    rows, mrows = inner // count, model // count
    r.branch[...] = jnp.zeros_like(r.branch)

    def block(b, none):
        cols = pl.ds(pl.multiple_of(b * COLS, COLS), COLS)
        mixed = r.mixed[:, cols]
        for d in range(2):
            mixed = mixed + r.d_skip[d : d + 1, cols] * r.active[d, :, cols].astype(F32)
        gate = r.gate_branch[:, cols]
        sigma = sigmoid(gate)
        now = (mixed * (gate * sigma)).astype(BF16)
        r.gated[:, cols] = now
        slope = sigma * (1.0 + gate * (1.0 - sigma))
        back = (r.gated_grad[:, cols] * mixed * slope).astype(BF16)
        r.gate_branch_grad[:, cols] = back
        r.branch[...] += dot(now, r.w_out[cols, :])
        r.whole[:, cols] = contract_rows(r.mixer_own[...], back)
        return none

    lax.fori_loop(0, inner // COLS, block, 0)
    half = model // 2
    for o in range(count):
        first, rest = slot_of(o, count, YX)
        r.gate0[first, rest] = stacked_rows(r.whole, r.stage, o, mrows, 0, model).astype(BF16)
        r.gate1[first, rest] = stacked_rows(r.whole, r.stage, o, mrows, model, inner).astype(BF16)
    r.output[...] = (r.hidden[...].astype(F32) + r.gate_rows[...] * r.branch[...]).astype(BF16)
    r.gate_grad[...] = r.grad_out[...].astype(F32) * r.branch[...]
    chunk = inner // 8
    per = count // 8
    for q in range(8):
        part = contract_rows(r.gated[:, q * chunk : (q + 1) * chunk], r.branch_grad[...])
        r.whole[0:chunk, 0:model] = part
        for i in range(per):
            first, rest = slot_of(q * per + i, count, XY)
            low = r.whole[i * rows : (i + 1) * rows, 0:model].astype(BF16)
            r.out0[first, rest, 0:rows] = low[:, :half]
            r.out1[first, rest, 0:rows] = low[:, half:]


def front_kernel(count, names, *refs):
    refs = list(refs)

    def take(size):
        taken = refs[:size]
        del refs[:size]
        return taken

    in_names, weight_names, head_names, tail_names, scratch_names = names
    given = take(len(in_names))
    weights_any = take(5)
    head_any, tail_any = take(len(head_names)), take(len(tail_names))
    (kept_any,) = take(1)
    weights = take(len(weight_names))
    head_refs, tail_refs = take(len(head_names)), take(len(tail_names))
    scratch = take(len(scratch_names))
    load_sems, head_sems, tail_sems, kept_sems = take(4)
    halo_sems = take(2)
    carry_sems = [take(2) for _ in range(3)]
    r = Refs(
        in_names + weight_names + head_names + tail_names + scratch_names,
        given + weights + head_refs + tail_refs + scratch,
    )
    tokens, inner = r.seed.shape
    w_mod_any, w_in_any, w_out_any, w_x_any, w_dt_any = weights_any
    sources = (
        w_mod_any,
        w_in_any.at[:, pl.ds(0, inner)],
        w_in_any.at[:, pl.ds(inner, inner)],
        w_out_any,
        w_x_any,
        w_dt_any,
    )
    loads = [
        pltpu.make_async_copy(src, dst, load_sems.at[i])
        for i, (src, dst) in enumerate(zip(sources, weights))
    ]
    for load in loads:
        load.start()
    carries = Carries(r, count, carry_sems)
    me = carries.me
    left = lax.rem(me + count - 1, count)
    right = lax.rem(me + 1, count)
    barrier = pltpu.get_barrier_semaphore()
    peers = [left, right]
    peers += [carries.base + lax.rem(carries.mine + k, PLANE) for k in range(1, PLANE)]
    peers += [
        lax.rem(carries.level + k, carries.groups) * PLANE + carries.mine
        for k in range(1, carries.groups)
    ]
    for peer in peers:
        pl.semaphore_signal(barrier, inc=1, device_id=(peer,), device_id_type=MESH)

    segment, wide_segment = token_masks(r, me * tokens)
    r.rate[...] = -jnp.exp(r.a_log[...]) * LOG2E
    r.out_acc[...] = jnp.zeros_like(r.out_acc)

    pl.semaphore_wait(barrier, len(peers))
    halos = [
        remote(r.hidden.at[pl.ds(tokens - 16, 16)], r.below, halo_sems, 0, right),
        remote(r.hidden.at[pl.ds(0, 16)], r.above, halo_sems, 1, left),
    ]
    for halo in halos:
        halo.start()
    cond = r.condition[...]
    cond_act = (cond * sigmoid(cond)).astype(BF16)
    loads[0].wait()
    r.modulation[0 : cond.shape[0], :] = dot(cond_act, r.w_mod[...])
    for halo in halos:
        halo.wait_recv()
    below = jnp.where(me > 0, r.below[...].astype(F32), 0.0)[16 - RIM :]
    above = jnp.where(me < count - 1, r.above[...].astype(F32), 0.0)[:RIM]
    normalise(r, below, above)
    modulate(r, segment, wide_segment)
    for load in loads[1:]:
        load.wait()
    project(r)
    coefficients(r)
    stepping(r)

    head_copies = [
        pltpu.make_async_copy(src, dst, head_sems.at[i])
        for i, (src, dst) in enumerate(zip(head_refs, head_any))
    ]
    for copy in head_copies:
        copy.start()

    blocks = inner // COLS
    tiles = inner // LANES
    per = COLS // LANES
    half = PLANE // 2
    begin, sent = 0, 0
    for end in (blocks // 2, blocks):
        summarise(r, begin, end)
        whole = end * per * half // tiles
        for j in range(sent, whole):
            carries.send(j)
            carries.send(half + j)
        begin, sent = end, whole
    carries.exchange()

    def stored(b):
        cols = pl.ds(pl.multiple_of(b * COLS, COLS), COLS)
        side = lax.rem(b, 2)
        return pltpu.make_async_copy(
            r.stage_kept.at[side], kept_any.at[:, :, cols], kept_sems.at[side]
        )

    def scan_block(b, none):
        @pl.when(b >= 2)
        def _():
            stored(b - 2).wait()

        forward_block(r, b, r.stage_kept.at[lax.rem(b, 2)])
        stored(b).start()
        return none

    lax.fori_loop(0, blocks, scan_block, 0)
    output_side(r, count)
    tail_copies = [
        pltpu.make_async_copy(src, dst, tail_sems.at[i])
        for i, (src, dst) in enumerate(zip(tail_refs, tail_any))
    ]
    for copy in tail_copies:
        copy.start()
    for b in (blocks - 2, blocks - 1):
        stored(b).wait()
    carries.finish()
    for halo in halos:
        halo.wait_send()
    for copy in head_copies + tail_copies:
        copy.wait()


def run_front(count, given, weights):
    w_mod, w_in, w_out, w_x, w_dt = weights
    tokens, model = given.hidden.shape
    inner = w_in.shape[1] // 2
    rank = w_dt.shape[1]
    proj = w_x.shape[1]
    states = given.a_log.shape[1]
    taps = given.conv_w.shape[1]
    groups = count // PLANE
    wide = tokens + 2 * RIM
    tiles = inner // LANES
    share = 2 * tiles // PLANE
    both = (2, tokens, inner)
    spread = (2, tokens, states, LANES)
    diag = (2, tokens, CHUNK * states)
    slots = shaped((2, count // 2, slot_rows(count, inner), model // 2), BF16)
    head_out = dict(
        mixer=shaped((wide, model), BF16),
        normed=shaped((wide, model)),
        rescale=shaped((tokens, LANES)),
        scale1=shaped((tokens, model)),
        conv_keep=shaped((wide, inner), BF16),
        seed=shaped((tokens, inner)),
        conv_sum=shaped(both),
        active=shaped(both, BF16),
        rank_low=shaped((2, tokens, rank), BF16),
        logit=shaped(both),
        masked=shaped(both),
        driven=shaped(both),
        out_spread=shaped(spread),
        in_blk=shaped(diag, BF16),
        rate=shaped((2, states, inner)),
        masks=shaped((2 * taps - 1, tokens, LANES)),
        hot=shaped((wide, LANES)),
    )
    tail_out = dict(
        entering=shaped((2 * tiles, 2, states, LANES), BF16),
        out_acc=shaped(diag),
        output=shaped((tokens, model), BF16),
        gate_grad=shaped((tokens, model)),
        gate_branch_grad=shaped((tokens, inner), BF16),
        out0=slots,
        gate0=slots,
        out1=slots,
        gate1=slots,
    )
    outs = dict(head_out, **tail_out)
    kept = shaped((2, (tokens + 1) * states, inner), BF16)
    rows = pltpu.VMEM((CHUNK * states, COLS), BF16)
    scratch = dict(
        below=pltpu.VMEM((16, model), BF16),
        above=pltpu.VMEM((16, model), BF16),
        mixer_own=pltpu.VMEM((tokens, model), BF16),
        gate_rows=pltpu.VMEM((tokens, model), F32),
        branch_grad=pltpu.VMEM((tokens, model), BF16),
        gate_branch=pltpu.VMEM((tokens, inner), F32),
        gated_grad=pltpu.VMEM((tokens, inner), F32),
        in_spread=pltpu.VMEM(spread, F32),
        out_blk=pltpu.VMEM(diag, BF16),
        conv_wide=pltpu.VMEM((wide, COLS), F32),
        proj=pltpu.VMEM((2, tokens, proj), F32),
        modulation=pltpu.VMEM((8, w_mod.shape[1]), F32),
        sums=pltpu.VMEM((2 * tiles, 3, states, LANES), BF16),
        got=pltpu.VMEM((PLANE, share, 3, states, LANES), BF16),
        total=pltpu.VMEM((3, share, states, LANES), BF16),
        others=pltpu.VMEM((groups, 2, share, states, LANES), BF16),
        back=pltpu.VMEM((PLANE, share, 2, states, LANES), BF16),
        mixed=pltpu.VMEM((tokens, inner), F32),
        stage_kept=pltpu.VMEM((2, 2, (tokens + 1) * states, COLS), BF16),
        gated=pltpu.VMEM((tokens, inner), BF16),
        branch=pltpu.VMEM((tokens, model), F32),
        whole=pltpu.VMEM((model, inner), F32),
        stage=pltpu.VMEM((slot_rows(count, inner), model // 2), F32),
        rows00=rows,
        rows01=rows,
        rows10=rows,
        rows11=rows,
    )
    sems = pltpu.SemaphoreType.DMA
    held = dict(
        w_mod=pltpu.VMEM(w_mod.shape, BF16),
        w_conv=pltpu.VMEM((model, inner), BF16),
        w_gate=pltpu.VMEM((model, inner), BF16),
        w_out=pltpu.VMEM(w_out.shape, BF16),
        w_x=pltpu.VMEM(w_x.shape, BF16),
        w_dt=pltpu.VMEM(w_dt.shape, BF16),
    )
    given = vars(given)
    names = tuple(tuple(part) for part in (given, held, head_out, tail_out, scratch))
    results = pl.pallas_call(
        functools.partial(front_kernel, count, names),
        in_specs=[pl.BlockSpec(memory_space=pltpu.SMEM)] + [VMEM] * (len(given) - 1) + [ANY] * 5,
        out_specs=[ANY] * (len(outs) + 1),
        out_shape=list(outs.values()) + [kept],
        scratch_shapes=list(held.values())
        + [pltpu.VMEM(out.shape, out.dtype) for out in outs.values()]
        + list(scratch.values())
        + [sems((len(held),)), sems((len(head_out),)), sems((len(tail_out),)), sems((2,))]
        + [sems((2,))] * 2
        + [sems((PLANE,))] * 2
        + [sems((groups,))] * 2
        + [sems((PLANE,))] * 2,
        compiler_params=pltpu.CompilerParams(
            collective_id=0, has_side_effects=True, vmem_limit_bytes=60 * MIB
        ),
        name="front",
    )(*given.values(), *weights)
    return types.SimpleNamespace(kept=results[-1], **dict(zip(outs, results)))


def block_specs(tokens, states):
    wide = CHUNK * states
    return types.SimpleNamespace(
        both=pl.BlockSpec((2, tokens, COLS), lambda b: (0, 0, b)),
        rows=pl.BlockSpec((tokens, COLS), lambda b: (0, b)),
        spread=pl.BlockSpec((2, tokens, states, LANES), lambda b: (0, 0, 0, 0)),
        diag=pl.BlockSpec((2, tokens, wide), lambda b: (0, 0, 0)),
        rate=pl.BlockSpec((2, states, COLS), lambda b: (0, 0, b)),
        entering=pl.BlockSpec((2, COLS // LANES, 2, states, LANES), lambda b: (0, b, 0, 0, 0)),
        kept=pl.BlockSpec((2, (tokens + 1) * states, COLS), lambda b: (0, 0, b)),
    )


class Place:
    def __init__(self, count):
        self.count = count
        self.groups = count // PLANE
        self.me = lax.axis_index("seq")
        self.bits = [lax.rem(self.me, 2), lax.rem(self.me // 2, 2), lax.rem(self.me // 4, 2)]
        self.flips = [self.me + (1 - 2 * self.bits[i]) * (1 << i) for i in range(3)]
        self.level = self.me // PLANE
        self.low = lax.rem(self.me, PLANE)
        self.left = lax.rem(self.me + count - 1, count)
        self.right = lax.rem(self.me + 1, count)
        self.far = [lax.rem(self.level + k, self.groups) for k in range(1, self.groups)]

    def meet(self):
        barrier = pltpu.get_barrier_semaphore()
        across = self.flips[1] + self.flips[2] - self.me
        peers = self.flips + [across, self.left, self.right]
        peers += [g * PLANE + self.low for g in self.far]
        for peer in peers:
            pl.semaphore_signal(barrier, inc=1, device_id=(peer,), device_id_type=MESH)
        pl.semaphore_wait(barrier, len(peers))


def add_into(into, own, first):
    def one(i, none):
        into[i] = into[i] + own[first + i]
        return none

    lax.fori_loop(0, into.shape[0], one, 0)


class Piece:
    def __init__(self, place, order, part, own, refs):
        self.place, self.order, self.part, self.own = place, order, part, own
        self.got1, self.got2, self.got3, self.got4 = refs[:4]
        self.sems = refs[4:]
        self.bits = [place.bits[0], place.bits[order[0]], place.bits[order[1]]]
        self.flips = [place.flips[0], place.flips[order[0]], place.flips[order[1]]]

    def hop(self, i):
        if i == 0:
            src = self.part.at[1 - self.bits[0]]
        else:
            half = 4 * self.place.groups >> i
            held = (self.got1, self.got2)[i - 1]
            src = held.at[pl.ds((1 - self.bits[i]) * half, half)]
        return remote(src, (self.got1, self.got2, self.got3)[i], self.sems, i, self.flips[i])

    def fan(self):
        return [
            remote(
                self.got3.at[g],
                self.got4.at[self.place.level],
                self.sems,
                3 + k,
                g * PLANE + self.place.low,
            )
            for k, g in enumerate(self.place.far)
        ]

    def step(self, i):
        groups = self.place.groups
        if i:
            self.hop(i - 1).wait_recv()
        if i == 1:
            add_into(self.got1, self.own, 0)
        elif i == 2:
            add_into(self.got2, self.got1, self.bits[1] * 2 * groups)
        elif i == 3:
            add_into(self.got3, self.got2, self.bits[2] * groups)
        if i < 3:
            self.hop(i).start()
            return
        for copy in self.fan():
            copy.start()
        self.got4[self.place.level] = self.got3[self.place.level]

    def end(self, share, begin):
        for copy in self.fan():
            copy.wait_recv()
        total = self.got4[0].astype(F32)
        for g in range(1, self.place.groups):
            total = total + self.got4[g].astype(F32)
        share[:, begin : begin + total.shape[1]] = total
        for copy in [self.hop(0), self.hop(1), self.hop(2)] + self.fan():
            copy.wait_send()


def piece_scratch(rows, cols, groups):
    return [
        pltpu.VMEM((size, rows, cols), BF16) for size in (4 * groups, 2 * groups, groups, groups)
    ] + [pltpu.SemaphoreType.DMA((2 + groups,))] * 2


def small_rows(taps):
    return 0, 2 * taps, 2 * taps + 2, 2 * taps + 4, 2 * taps + 8


def adjoint_block(r, b):
    tokens, cols = r.seed.shape
    per = cols // LANES
    states = r.rate.shape[1]
    taps = r.conv_w.shape[1]
    chunks = tokens // CHUNK
    wide = CHUNK * states
    adjs = ((r.adj00, r.adj01), (r.adj10, r.adj11))
    slopes = ((r.slope00, r.slope01), (r.slope10, r.slope11))
    at_cols = pl.ds(pl.multiple_of(b * cols, cols), cols)
    ones = (
        lax.broadcasted_iota(jnp.int32, (CHUNK, wide), 1) // states
        == lax.broadcasted_iota(jnp.int32, (CHUNK, wide), 0)
    ).astype(BF16)

    def first_of(d, i):
        return (chunks - 1 - i if d == 0 else i) * CHUNK

    low_rates = [
        r.rate[d, :, c * LANES : (c + 1) * LANES].astype(BF16) for d in range(2) for c in range(per)
    ]

    def compute(i, side, carry, jobs):
        carry = list(carry)
        for k in range(CHUNK):
            jobs_between(jobs, k)
            for d in range(2):
                first = first_of(d, i)
                slot = (first + d) * states
                j = CHUNK - 1 - k if d == 0 else k
                out_row = r.out_spread[d, first + j]
                part = slice(j * states, (j + 1) * states)
                before = slice(slot + j * states, slot + (j + 1) * states)
                for c in range(per):
                    lanes = pl.ds(c * LANES, LANES)
                    coming, total = carry[d * per + c]
                    step = row_of(r.masked.at[d], first, j, lanes)
                    now = jnp.exp2(step * r.rate[d, :, lanes])
                    adj = out_row * row_of(r.seed, first, j, lanes) + coming
                    coming = now * adj
                    slope = coming.astype(BF16) * r.kept[d, before, lanes] * low_rates[d * per + c]
                    total = total + slope.astype(F32) * step
                    adjs[side][d][part, lanes] = adj.astype(BF16)
                    slopes[side][d][part, lanes] = slope
                    carry[d * per + c] = (coming, total)
        return tuple(carry)

    def pieces(i, side):
        def driven_side(d):
            here = pl.ds(first_of(d, i), CHUNK)
            r.driven_grad[d, here, at_cols] = dot(r.in_blk[d, here, :], adjs[side][d][...])

        def in_side(d):
            here = pl.ds(first_of(d, i), CHUNK)
            r.in_acc[d, here, :] += contract_cols(
                r.driven[d, here, :].astype(BF16), adjs[side][d][...]
            )

        def decay_side(d):
            here = pl.ds(first_of(d, i), CHUNK)
            r.decay_grad[d, here, at_cols] = dot(ones, slopes[side][d][...]) * LN2

        return [
            functools.partial(job, d) for d in range(2) for job in (driven_side, in_side, decay_side)
        ]

    zero = jnp.zeros((states, LANES), F32)
    start = tuple(
        (r.entering[d, c, 1 - d].astype(F32), zero) for d in range(2) for c in range(per)
    )
    carry = interleaved(chunks, compute, pieces, start)
    at_rate = small_rows(taps)[4]
    for d in range(2):
        for c in range(per):
            lanes = tile_at(b * cols + c * LANES)
            r.small[at_rate + d * states : at_rate + (d + 1) * states, lanes] = (
                carry[d * per + c][1] * LN2
            )


def column_sum(values):
    return jnp.sum(values, axis=0, keepdims=True)


def through_steps(r):
    tokens, inner = r.seed_all.shape
    taps = r.conv_w.shape[1]
    rank = r.w_dt.shape[1]
    proj = r.w_x.shape[1]
    states = r.rate.shape[1]
    _, _, at_dt, at_skip, _ = small_rows(taps)
    r.rank_grad[...] = jnp.zeros_like(r.rank_grad)

    def block(b, none):
        cols = pl.ds(pl.multiple_of(b * COLS, COLS), COLS)
        for d in range(2):
            act = r.active[d, :, cols].astype(F32)
            value = r.logit[d, :, cols]
            back = r.driven_grad[d, :, cols]
            grown = r.seed_all[:, cols]
            grad = (r.decay_grad[d, :, cols] + back * act) * sigmoid(value)
            low = grad.astype(BF16)
            r.active_grad[d, :, cols] = back * softplus(value) + grown * r.d_skip[d : d + 1, cols]
            r.small[at_dt + d : at_dt + d + 1, cols] = column_sum(grad)
            r.small[at_skip + d : at_skip + d + 1, cols] = column_sum(grown * act)
            r.rank_grad[d] += contract_cols(low, r.w_dt[d, :, cols])
            start = 2 * proj + d * rank
            r.whole_cols[cols, start : start + rank] = contract_rows(low, r.rank_low[d])
        return none

    lax.fori_loop(0, inner // COLS, block, 0)

    place = lax.rem(lax.broadcasted_iota(jnp.int32, (tokens, CHUNK * states), 0), CHUNK)
    owner = lax.broadcasted_iota(jnp.int32, (tokens, CHUNK * states), 1) // states
    on_diag = place == owner
    column = lax.rem(lax.broadcasted_iota(jnp.int32, (CHUNK * states, states), 0), states)
    gather = (column == lax.broadcasted_iota(jnp.int32, (CHUNK * states, states), 1)).astype(BF16)
    for d in range(2):
        r.proj_grad[d, :, 0:rank] = r.rank_grad[d].astype(BF16)
        for start, acc in ((rank, r.in_acc), (rank + states, r.out_acc)):
            kept = jnp.where(on_diag, acc[d], 0.0).astype(BF16)
            r.proj_grad[d, :, start : start + states] = dot(kept, gather).astype(BF16)

    def weights(b, none):
        cols = pl.ds(pl.multiple_of(b * COLS, COLS), COLS)
        for d in range(2):
            r.whole_cols[cols, d * proj : (d + 1) * proj] = contract_rows(
                r.active[d, :, cols], r.proj_grad[d]
            )
        return none

    lax.fori_loop(0, inner // COLS, weights, 0)


def through_conv(r, begin, end):
    tokens, inner = r.seed_all.shape
    taps = r.conv_w.shape[1]
    at_conv, at_bias, _, _, _ = small_rows(taps)

    def block(b, none):
        cols = pl.ds(pl.multiple_of(b * COLS, COLS), COLS)
        r.conv_wide[...] = r.conv_keep[:, cols].astype(F32)
        r.input_wide[...] = jnp.zeros_like(r.input_wide)
        for d in range(2):
            total = r.active_grad[d, :, cols] + dot(r.proj_grad[d], r.w_x[d, :, cols])
            for c in range(COLS // LANES):
                lanes = tile_at(b * COLS + c * LANES)
                here = slice(c * LANES, (c + 1) * LANES)
                grad = total[:, here] * silu_slope(r.conv_sum[d, :, lanes])
                r.small[at_bias + d : at_bias + d + 1, lanes] = column_sum(grad)
                for k in range(taps):
                    offset = offset_of(d, k, taps)
                    window = slice(RIM + offset, RIM + offset + tokens)
                    part = grad * r.masks[offset + taps - 1]
                    at = at_conv + d * taps + k
                    r.small[at : at + 1, lanes] = column_sum(part * r.conv_wide[window, here])
                    r.input_wide[window, here] += r.conv_w[d, k : k + 1, lanes] * part
        low = r.input_wide[...].astype(BF16)
        here = pl.ds(pl.multiple_of((b - begin) * COLS, COLS), COLS)
        r.whole_conv[:, here] = contract_rows(r.mixer[...], low)
        r.norm_wide[...] += contract_cols(low, r.w_in[:, cols])
        gate_cols = pl.ds(pl.multiple_of(inner + b * COLS, COLS), COLS)
        r.norm_wide[RIM : RIM + tokens, :] += contract_cols(
            r.gate_branch_grad[:, cols], r.w_in[:, gate_cols]
        )
        r.small_cols[cols, :] = r.small[:, cols].T
        return none

    lax.fori_loop(begin, end, block, 0)


def fill_columns(r, count):
    rows = r.seed_all.shape[1] // count
    for o in range(count):
        first, later = slot_of(o, count, XY)
        r.late0[first, later, 0:rows] = r.whole_cols[o * rows : (o + 1) * rows, :].astype(BF16)


def fill_conv(r, count, half):
    inner = r.seed_all.shape[1]
    model = r.normed.shape[1]
    rows, mrows = inner // count, model // count
    cut = r.late2.shape[3]
    rest = model // 2 - cut
    for o in range(count):
        both = stacked_rows(r.whole_conv, r.stage, o, mrows, 0, model).astype(BF16)
        first, later = slot_of(o, count, YX)
        if half == 0:
            r.late1[first, later] = both
            continue
        r.late3[first, later, :, 0:rest] = both[:, cut:]
        r.late3[first, later, 0:rows, rest:] = r.small_cols[o * rows : (o + 1) * rows, :].astype(
            BF16
        )
        first, later = slot_of(o, count, XY)
        r.late2[first, later] = both[:, :cut]


def modulation_sums(r):
    tokens = r.seed_all.shape[0]
    model = r.normed.shape[1]
    seqs = r.mod_part.shape[1]
    half = r.mod_part.shape[2]
    seq_rows = r.hot[:, 0:seqs]
    grads = r.norm_wide[...]
    sums = [
        contract_rows(seq_rows, grads, HIGHEST),
        contract_rows(seq_rows, grads * r.normed[...], HIGHEST),
        contract_rows(r.hot[RIM : RIM + tokens, 0:seqs], r.gate_grad[...], HIGHEST),
    ]
    whole = jnp.concatenate(sums, axis=1)
    r.mod_part[0] = whole[:, :half].astype(BF16)
    r.mod_part[1] = whole[:, half:].astype(BF16)


class ModSums:
    def __init__(self, place, r, sems):
        self.place, self.r, self.sems = place, r, sems
        self.core = place.bits[0]
        self.chip = place.bits[1] + 2 * place.bits[2]

    def copies(self, i):
        place, r, sems = self.place, self.r, self.sems
        if i == 0:
            return [remote(r.mod_part.at[1 - self.core], r.m1, sems, 0, place.flips[0])]
        if i == 1:
            peers = (place.flips[1], place.flips[2], place.flips[1] + place.flips[2] - place.me)
            return [
                remote(r.m1, r.m2.at[self.chip], sems, 1 + k, peer) for k, peer in enumerate(peers)
            ]
        if i == 2:
            return [
                remote(r.m1, r.m3.at[place.level], sems, 4 + k, g * PLANE + place.low)
                for k, g in enumerate(place.far)
            ]
        slot = 4 + len(place.far)
        return [
            remote(r.m4.at[self.core], r.m4.at[self.core], sems, slot, place.flips[0])
        ]

    def total(self, ref, number):
        total = ref[0].astype(F32)
        for g in range(1, number):
            total = total + ref[g].astype(F32)
        return total.astype(BF16)

    def step(self, i):
        place, r = self.place, self.r
        if i:
            for copy in self.copies(i - 1):
                copy.wait_recv()
        if i == 1:
            r.m1[...] = r.m1[...] + r.mod_part[self.core]
            r.m2[self.chip] = r.m1[...]
        elif i == 2:
            for copy in self.copies(1):
                copy.wait_send()
            summed = self.total(r.m2, 4)
            r.m1[...] = summed
            r.m3[place.level] = summed
        elif i == 3:
            r.m4[self.core] = self.total(r.m3, place.groups)
        for copy in self.copies(i):
            copy.start()

    def end(self, mod):
        half = mod.shape[1] // 2
        self.copies(3)[0].wait_recv()
        for c in range(2):
            mod[:, c * half : (c + 1) * half] = self.r.m4[c].astype(F32)[0 : mod.shape[0]]
        for i in (0, 2, 3):
            for copy in self.copies(i):
                copy.wait_send()


def back_kernel(count, names, *refs):
    refs = list(refs)

    def take(size):
        taken = refs[:size]
        del refs[:size]
        return taken

    blocked, fixed = take(len(names[0])), take(len(names[1]))
    early = take(4)
    sources = take(len(names[2]))
    out, scratch = take(len(names[3])), take(len(names[4]))
    fetched = take(len(names[2]))
    owns = take(4)
    early_refs = [take(6) for _ in range(4)]
    late_refs = [take(6) for _ in range(4)]
    mod_sems = take(2)
    fetch_sems, own_sems = take(2)
    r = Refs(
        names[0] + names[1] + names[3] + names[4] + names[2],
        blocked + fixed + out + scratch + fetched,
    )
    b = pl.program_id(0)
    blocks = pl.num_programs(0)
    place = Place(count)
    core = place.bits[0]
    one = [Piece(place, (XY, YX)[p % 2], early[p], owns[p], early_refs[p]) for p in range(4)]
    lates = (r.late0, r.late1, r.late2, r.late3)
    two = [
        Piece(place, (XY, YX)[p % 2], part, part.at[core], late_refs[p])
        for p, part in enumerate(lates)
    ]

    def fetch(i):
        return pltpu.make_async_copy(sources[i], fetched[i], fetch_sems.at[i])

    def own(p):
        return pltpu.make_async_copy(early[p].at[core], owns[p], own_sems.at[p])

    @pl.when(b == 0)
    def _():
        for p in range(4):
            own(p).start()
        place.meet()
        for p in range(4):
            one[p].step(0)
        for i in range(len(sources)):
            fetch(i).start()
        r.in_acc[...] = jnp.zeros_like(r.in_acc)
        r.small[...] = jnp.zeros_like(r.small)

    adjoint_block(r, b)

    for turn, pieces in ((0, (0, 1)), (1, (2, 3))):

        @pl.when(b == turn)
        def _():
            for p in pieces:
                own(p).wait()
                one[p].step(1)

    @pl.when(b == blocks - 2)
    def _():
        one[0].step(2)
        one[1].step(2)

    @pl.when(b == blocks - 1)
    def _():
        for i in range(len(sources)):
            fetch(i).wait()
        through_steps(r)
        fill_columns(r, count)
        two[0].step(0)
        one[2].step(2)
        one[3].step(2)
        one[0].step(3)
        one[1].step(3)
        r.norm_wide[...] = jnp.zeros_like(r.norm_wide)
        through_conv(r, 0, blocks // 2)
        fill_conv(r, count, 0)
        two[1].step(0)
        two[0].step(1)
        one[2].step(3)
        one[3].step(3)
        through_conv(r, blocks // 2, blocks)
        two[1].step(1)
        modulation_sums(r)
        mods = ModSums(place, r, mod_sems)
        mods.step(0)
        fill_conv(r, count, 1)
        two[2].step(0)
        two[3].step(0)
        mods.step(1)
        far = len(place.far)
        edges = [
            remote(
                r.norm_wide.at[pl.ds(0, RIM)],
                r.edge_got.at[pl.ds(RIM, RIM)],
                mod_sems,
                5 + far,
                place.left,
            ),
            remote(
                r.norm_wide.at[pl.ds(r.norm_wide.shape[0] - RIM, RIM)],
                r.edge_got.at[pl.ds(0, RIM)],
                mod_sems,
                6 + far,
                place.right,
            ),
        ]
        for copy in edges:
            copy.start()
        two[2].step(1)
        two[3].step(1)
        width = r.share_early.shape[1] // 4
        one[0].end(r.share_early, 0)
        one[2].end(r.share_early, width)
        one[1].end(r.share_early, 2 * width)
        one[3].end(r.share_early, 3 * width)
        two[0].step(2)
        two[1].step(2)
        mods.step(2)
        two[2].step(2)
        two[3].step(2)
        two[0].step(3)
        two[1].step(3)
        mods.step(3)
        two[2].step(3)
        two[3].step(3)
        begin = 0
        for p in range(4):
            two[p].end(r.share_late, begin)
            begin += lates[p].shape[3]
        mods.end(r.mod)
        for copy in edges:
            copy.wait_recv()
        r.edges[...] = r.edge_got[...]
        for copy in edges:
            copy.wait_send()


def late_columns(model, proj, rank, taps, states):
    first = 2 * (proj + rank)
    small = 2 * taps + 8 + 2 * states
    half = model // 2
    cut = half // 2 // LANES * LANES + LANES
    return first + -first % LANES, half, cut, half - cut + small + -small % LANES


def once(shape):
    return pl.BlockSpec(shape, lambda b: (0,) * len(shape), pipeline_mode=pl.Buffered(1))


def run_back(h, count, d_skip, conv_w, w_x, w_dt, w_in):
    tokens, inner = h.seed.shape
    wide, model = h.normed.shape
    groups = count // PLANE
    rank = w_dt.shape[1]
    proj = w_x.shape[1]
    states = h.rate.shape[1]
    taps = conv_w.shape[1]
    rows = slot_rows(count, inner)
    lates = late_columns(model, proj, rank, taps, states)
    small = lates[3] - (model // 2 - lates[2])
    s = block_specs(tokens, states)
    entering = h.entering.reshape(2, -1, 2, states, LANES)
    blocked = dict(
        masked=(h.masked, s.both),
        driven=(h.driven, s.both),
        seed=(h.seed, s.rows),
        rate=(h.rate, s.rate),
        entering=(entering, s.entering),
        kept=(h.kept, s.kept),
    )
    fixed = dict(out_spread=h.out_spread, in_blk=h.in_blk, d_skip=d_skip, conv_w=conv_w)
    early = (h.out0, h.gate0, h.out1, h.gate1)
    fetched = dict(
        out_acc=h.out_acc,
        rank_low=h.rank_low,
        w_dt=w_dt,
        logit=h.logit,
        active=h.active,
        seed_all=h.seed,
        w_x=w_x,
        conv_sum=h.conv_sum,
        conv_keep=h.conv_keep,
        masks=h.masks,
        mixer=h.mixer,
        w_in=w_in,
        gate_branch_grad=h.gate_branch_grad,
        hot=h.hot,
        normed=h.normed,
        gate_grad=h.gate_grad,
    )
    buffer = pltpu.VMEM((CHUNK * states, COLS), BF16)
    mod = (8, 3 * model)
    half_mod = (16, 3 * model // 2)
    scratch = dict(
        decay_grad=pltpu.VMEM((2, tokens, inner), F32),
        driven_grad=pltpu.VMEM((2, tokens, inner), F32),
        in_acc=pltpu.VMEM((2, tokens, CHUNK * states), F32),
        small=pltpu.VMEM((small, inner), F32),
        adj00=buffer,
        adj01=buffer,
        adj10=buffer,
        adj11=buffer,
        slope00=buffer,
        slope01=buffer,
        slope10=buffer,
        slope11=buffer,
        active_grad=pltpu.VMEM((2, tokens, inner), F32),
        rank_grad=pltpu.VMEM((2, tokens, rank), F32),
        proj_grad=pltpu.VMEM((2, tokens, proj), BF16),
        conv_wide=pltpu.VMEM((wide, COLS), F32),
        input_wide=pltpu.VMEM((wide, COLS), F32),
        whole_conv=pltpu.VMEM((model, inner // 2), F32),
        whole_cols=pltpu.VMEM((inner, lates[0]), F32),
        small_cols=pltpu.VMEM((inner, small), F32),
        stage=pltpu.VMEM((rows, model // 2), F32),
        late0=pltpu.VMEM((2, 4 * groups, rows, lates[0]), BF16),
        late1=pltpu.VMEM((2, 4 * groups, rows, lates[1]), BF16),
        late2=pltpu.VMEM((2, 4 * groups, rows, lates[2]), BF16),
        late3=pltpu.VMEM((2, 4 * groups, rows, lates[3]), BF16),
        mod_part=pltpu.VMEM((2,) + half_mod, BF16),
        m1=pltpu.VMEM(half_mod, BF16),
        m2=pltpu.VMEM((4,) + half_mod, BF16),
        m3=pltpu.VMEM((groups,) + half_mod, BF16),
        m4=pltpu.VMEM((2,) + half_mod, BF16),
        edge_got=pltpu.VMEM((2 * RIM, model), F32),
    )
    outs = dict(
        norm_wide=shaped((wide, model)),
        share_early=shaped((rows, 2 * model)),
        share_late=shaped((rows, sum(lates))),
        mod=shaped(mod),
        edges=shaped((2 * RIM, model)),
    )
    sems = pltpu.SemaphoreType.DMA
    pieces = []
    for cols in (model // 2,) * 4 + lates:
        pieces += piece_scratch(rows, cols, groups)
    names = tuple(tuple(part) for part in (blocked, fixed, fetched, outs, scratch))
    return pl.pallas_call(
        functools.partial(back_kernel, count, names),
        grid=(inner // COLS,),
        in_specs=[spec for _, spec in blocked.values()]
        + [once(value.shape) for value in fixed.values()]
        + [ANY] * (len(early) + len(fetched)),
        out_specs=[once(out.shape) for out in outs.values()],
        out_shape=list(outs.values()),
        scratch_shapes=list(scratch.values())
        + [pltpu.VMEM(value.shape, value.dtype) for value in fetched.values()]
        + [pltpu.VMEM((4 * groups, rows, model // 2), BF16)] * 4
        + pieces
        + [sems((6 + groups,))] * 2
        + [sems((len(fetched),)), sems((4,))],
        compiler_params=pltpu.CompilerParams(
            collective_id=1, has_side_effects=True, vmem_limit_bytes=60 * MIB
        ),
        name="back",
    )(
        *[value for value, _ in blocked.values()],
        *fixed.values(),
        *early,
        *fetched.values(),
    )


def finish_kernel(
    count,
    proj,
    rank,
    taps,
    states,
    proj_at,
    share_early,
    share_late,
    mod,
    edges,
    condition,
    norm_wide,
    normed,
    rescale,
    scale1,
    grad_out,
    made,
    output,
    grad_x,
    w_mod,
    b_mod,
    w_in,
    conv_w,
    conv_b,
    w_x,
    w_dt,
    dt_bias,
    a_log,
    d_skip,
    w_out,
):
    me = lax.axis_index("seq")
    tokens, model = grad_out.shape
    mrows, double = w_in.shape
    inner = double // 2
    rows = w_out.shape[0]
    seqs, _ = condition.shape
    half = model // 2

    output[...] = made[...]
    w_out[...] = share_early[0:rows, 0:model]
    first = share_late.shape[1] - proj_at
    for i in range(2):
        low = share_late[:, first + i * half : first + (i + 1) * half]
        high = share_early[:, model + i * half : model + (i + 1) * half]
        for at, both in ((i * model, low), (inner + i * model, high)):
            w_in[:, at : at + half] = both[0:mrows]
            w_in[:, at + half : at + model] = both[mrows : 2 * mrows]

    for d in range(2):
        w_x[d] = share_late[0:rows, d * proj : (d + 1) * proj]
    flipped = share_late[:, 0:first].T
    at = 2 * proj
    for d in range(2):
        w_dt[d] = flipped[at + d * rank : at + (d + 1) * rank, 0:rows]
    flipped = share_late[:, first + model :].T
    for d in range(2):
        conv_w[d] = flipped[d * taps : (d + 1) * taps, 0:rows]
    at = 2 * taps
    conv_b[...] = flipped[at : at + 2, 0:rows]
    dt_bias[...] = flipped[at + 2 : at + 4, 0:rows]
    d_skip[...] = flipped[at + 4 : at + 6, 0:rows]
    at = at + 8
    for d in range(2):
        a_log[d] = flipped[at + d * states : at + (d + 1) * states, 0:rows]

    def picked(total, width):
        source = lax.broadcasted_iota(jnp.int32, (total, width), 0)
        return source == me * width + lax.broadcasted_iota(jnp.int32, (total, width), 1)

    cond = condition[...]
    cond_act = (cond * sigmoid(cond)).astype(BF16)
    my_cond = dot(cond_act, picked(model, mrows).astype(BF16))
    totals = mod[0:seqs, :]
    w_mod[...] = contract_rows(my_cond, totals, HIGHEST)
    bias = jnp.broadcast_to(jnp.sum(totals, axis=0, keepdims=True), (8, 3 * model))
    width = 3 * model // count
    b_mod[...] = dot(bias, picked(3 * model, width).astype(F32), precision=HIGHEST)[0:1]

    norm_grad = norm_wide[RIM : RIM + tokens, :]
    low = jnp.where(me > 0, edges[0:RIM, :], 0.0)
    high = jnp.where(me < count - 1, edges[RIM:, :], 0.0)
    middle = jnp.zeros((tokens - 2 * RIM, model), F32)
    norm_grad = norm_grad + jnp.concatenate([low, middle, high], axis=0)
    scaled = norm_grad * scale1[...]
    normal = normed[RIM : RIM + tokens, :]
    grad_x[...] = grad_out[...].astype(F32) + rescale[:, 0:1] * (
        scaled
        - jnp.mean(scaled, axis=1, keepdims=True)
        - normal * jnp.mean(scaled * normal, axis=1, keepdims=True)
    )


def on_device(
    count,
    hidden,
    condition,
    seq_lengths,
    w_mod,
    b_mod,
    w_in,
    conv_w,
    conv_b,
    w_x,
    w_dt,
    dt_bias,
    a_log,
    d_skip,
    w_out,
    grad_out,
):
    tokens, model = hidden.shape
    inner = w_in.shape[1] // 2
    rank = w_dt.shape[1]
    proj = w_x.shape[2]
    states = a_log.shape[1]
    taps = conv_w.shape[1]
    me = lax.axis_index("seq")
    rows, mrows = inner // count, model // count

    flat_w_x = jnp.swapaxes(w_x, 1, 2)
    given = types.SimpleNamespace(
        lengths=seq_lengths,
        hidden=hidden,
        condition=condition,
        b_mod=b_mod.reshape(-1, LANES),
        conv_w=conv_w,
        conv_b=conv_b,
        dt_bias=dt_bias,
        d_skip=d_skip,
        a_log=a_log,
        grad_out=grad_out,
    )
    h = run_front(count, given, (w_mod, w_in, w_out, flat_w_x, w_dt))
    norm_wide, share_early, share_late, mod, edges = run_back(
        h, count, d_skip, conv_w, flat_w_x, w_dt, w_in
    )
    late = late_columns(model, proj, rank, taps, states)
    results = pl.pallas_call(
        functools.partial(finish_kernel, count, proj, rank, taps, states, sum(late[1:])),
        in_specs=[VMEM] * 11,
        out_specs=[VMEM] * 13,
        out_shape=[
            shaped((tokens, model), BF16),
            shaped((tokens, model)),
            shaped((mrows, 3 * model)),
            shaped((1, 3 * model // count)),
            shaped((mrows, 2 * inner)),
            shaped((2, taps, rows)),
            shaped((2, rows)),
            shaped((2, rows, proj)),
            shaped((2, rank, rows)),
            shaped((2, rows)),
            shaped((2, states, rows)),
            shaped((2, rows)),
            shaped((rows, model)),
        ],
        compiler_params=pltpu.CompilerParams(vmem_limit_bytes=60 * MIB),
        name="finish",
    )(
        share_early,
        share_late,
        mod,
        edges,
        condition,
        norm_wide,
        h.normed,
        h.rescale,
        h.scale1,
        grad_out,
        h.output,
    )
    return tuple(results[:3]) + (results[3].reshape(-1),) + tuple(results[4:])


def solution(mesh):
    in_specs = (P("seq", None),) + (P(),) * 13 + (P("seq", None),)
    out_specs = (
        P("seq", None),
        P("seq", None),
        P("seq", None),
        P("seq"),
        P("seq", None),
        P(None, None, "seq"),
        P(None, "seq"),
        P(None, "seq", None),
        P(None, None, "seq"),
        P(None, "seq"),
        P(None, None, "seq"),
        P(None, "seq"),
        P("seq", None),
    )
    return jax.shard_map(
        functools.partial(on_device, mesh.shape["seq"]),
        mesh=mesh,
        in_specs=in_specs,
        out_specs=out_specs,
        check_vma=False,
    )
```

```python
import functools
import types

import jax
import jax.numpy as jnp
from jax import lax
from jax.experimental import pallas as pl
from jax.experimental.pallas import tpu as pltpu
from jax.sharding import PartitionSpec as P

EPSILON = 1e-06
HIGHEST = lax.Precision.HIGHEST
MESH = pl.DeviceIdType.MESH
LANES = 128
LOG2E = 1.4426950408889634
LN2 = 0.6931471805599453
CUT_STEP = 1e9
PLANE = 8
RIM = 8
CHUNK = 16
XY, YX = (1, 2), (2, 1)
COLS = 256
SCAN = 512
MIB = 1024 * 1024
F32 = jnp.float32
BF16 = jnp.bfloat16
VMEM = pl.BlockSpec(memory_space=pltpu.VMEM)
ANY = pl.BlockSpec(memory_space=pl.ANY)


def shaped(shape, dtype=F32):
    return jax.ShapeDtypeStruct(shape, dtype)


def dot(left, right, dims=((1,), (0,)), precision=None):
    return lax.dot_general(
        left, right, (dims, ((), ())), precision=precision, preferred_element_type=F32
    )


def contract_rows(left, right, precision=None):
    return dot(left, right, ((0,), (0,)), precision)


def contract_cols(left, right):
    return dot(left, right, ((1,), (1,)))


def sigmoid(values):
    return 1.0 / (1.0 + jnp.exp(-values))


def softplus(values):
    return jnp.maximum(values, 0.0) + jnp.log1p(jnp.exp(-jnp.abs(values)))


def tile_at(start):
    return pl.ds(pl.multiple_of(start, LANES), LANES)


def row_of(ref, first, j, lanes):
    eight = pl.ds(pl.multiple_of(first + j // 8 * 8, 8), 8)
    return ref.at[eight, lanes][j % 8 : j % 8 + 1, :]


def segments(positions, bounds):
    total = jnp.full(positions.shape, -1, jnp.int32)
    for bound in bounds:
        total = total + (positions >= bound).astype(jnp.int32)
    return total


def read_bounds(lengths):
    bounds = [jnp.int32(0)]
    for j in range(lengths.shape[0]):
        bounds.append(bounds[-1] + lengths[j])
    return bounds


def rows_iota(rows):
    return lax.broadcasted_iota(jnp.int32, (rows, LANES), 0)


def offset_of(d, k, taps):
    return k - (taps - 1) if d == 0 else taps - 1 - k


def slot_of(o, count, order):
    bits = [o & 1, o >> 1 & 1, o >> 2 & 1]
    return bits[0], (bits[order[0]] * 2 + bits[order[1]]) * (count // PLANE) + o // PLANE


def slot_rows(count, inner):
    rows = inner // count
    return rows + -rows % 16


def stacked_rows(source, stage, o, rows, begin, end):
    middle = (begin + end) // 2
    part = pl.ds(o * rows, rows)
    if rows % 8 == 0:
        return jnp.concatenate([source[part, begin:middle], source[part, middle:end]], axis=0)
    stage[0:rows, :] = source[part, begin:middle]
    stage[rows : 2 * rows, :] = source[part, middle:end]
    return stage[...]


class Refs:
    def __init__(self, names, refs):
        for name, ref in zip(names, refs):
            setattr(self, name, ref)


def token_masks(r, first):
    tokens = r.hidden.shape[0]
    wide = r.normed.shape[0]
    taps = r.conv_w.shape[1]
    bounds = read_bounds(r.lengths)
    position = first + rows_iota(tokens)
    segment = segments(position, bounds)
    for offset in range(1 - taps, taps):
        r.masks[offset + taps - 1] = (segments(position + offset, bounds) == segment).astype(F32)
    wide_segment = segments(first - RIM + rows_iota(wide), bounds)
    lane = lax.broadcasted_iota(jnp.int32, (wide, LANES), 1)
    r.hot[...] = (wide_segment == lane).astype(F32)
    return segment, wide_segment


def normalise(r, below, above):
    tokens = r.hidden.shape[0]
    x = jnp.concatenate([below, r.hidden[...].astype(F32), above], axis=0)
    centered = x - jnp.mean(x, axis=1, keepdims=True)
    scaling = lax.rsqrt(jnp.mean(centered * centered, axis=1, keepdims=True) + EPSILON)
    r.normed[...] = centered * scaling
    r.rescale[...] = jnp.broadcast_to(scaling[RIM : RIM + tokens], (tokens, LANES))


def modulate(r, segment, wide_segment):
    tokens, model = r.hidden.shape
    seqs = r.condition.shape[0]
    for c in range(model // LANES):
        lanes = slice(c * LANES, (c + 1) * LANES)

        def rows_for(part, segs):
            total = jnp.zeros(segs.shape, F32)
            at = part * model + c * LANES
            bias = r.b_mod[at // LANES : at // LANES + 1, :]
            for j in range(seqs):
                row = r.modulation[j : j + 1, at : at + LANES] + bias
                total = jnp.where(segs == j, row, total)
            return total

        one_scale = 1.0 + rows_for(1, wide_segment)
        mixed_in = r.normed[:, lanes] * one_scale + rows_for(0, wide_segment)
        r.mixer[:, lanes] = mixed_in.astype(BF16)
        r.mixer_own[:, lanes] = mixed_in[RIM : RIM + tokens].astype(BF16)
        r.scale1[:, lanes] = one_scale[RIM : RIM + tokens]
        gate = rows_for(2, segment)
        r.gate_rows[:, lanes] = gate
        r.branch_grad[:, lanes] = (r.grad_out[:, lanes].astype(F32) * gate).astype(BF16)


def project(r):
    tokens, inner = r.seed.shape
    r.proj[...] = jnp.zeros_like(r.proj)

    def block(b, none):
        cols = pl.ds(pl.multiple_of(b * COLS, COLS), COLS)
        conv = dot(r.mixer[...], r.w_conv[:, cols]).astype(BF16)
        r.conv_keep[:, cols] = conv
        r.conv_wide[...] = conv.astype(F32)
        gate = dot(r.mixer_own[...], r.w_gate[:, cols])
        r.gate_branch[:, cols] = gate
        back = contract_cols(r.branch_grad[...], r.w_out[cols, :])
        r.gated_grad[:, cols] = back
        r.seed[:, cols] = back * (gate * sigmoid(gate))
        convolve(r, 0, b)
        return none

    lax.fori_loop(0, inner // COLS, block, 0)


def convolve(r, d, b):
    tokens, inner = r.seed.shape
    taps = r.conv_w.shape[1]
    cols = pl.ds(pl.multiple_of(b * COLS, COLS), COLS)
    acts = []
    for c in range(COLS // LANES):
        lanes = tile_at(b * COLS + c * LANES)
        here = slice(c * LANES, (c + 1) * LANES)
        total = jnp.broadcast_to(r.conv_b[d : d + 1, lanes], (tokens, LANES))
        for k in range(taps):
            offset = offset_of(d, k, taps)
            total = total + r.conv_w[d, k : k + 1, lanes] * (
                r.conv_wide[RIM + offset : RIM + offset + tokens, here]
                * r.masks[offset + taps - 1]
            )
        sigma = sigmoid(total)
        r.conv_slope[d, :, lanes] = (sigma * (1.0 + total * (1.0 - sigma))).astype(BF16)
        act = (total * sigma).astype(BF16)
        r.active[d, :, lanes] = act
        acts.append(act)
    r.proj[d] += contract_cols(jnp.concatenate(acts, axis=1), r.w_x[d, :, cols])


def convolve_reverse(r):
    inner = r.seed.shape[1]

    def block(b, none):
        cols = pl.ds(pl.multiple_of(b * COLS, COLS), COLS)
        r.conv_wide[...] = r.conv_keep[:, cols].astype(F32)
        convolve(r, 1, b)
        return none

    lax.fori_loop(0, inner // COLS, block, 0)


def coefficients(r, d):
    tokens = r.seed.shape[0]
    rank = r.w_dt.shape[1]
    states = r.rate.shape[1]
    place = lax.rem(lax.broadcasted_iota(jnp.int32, (tokens, CHUNK * states), 0), CHUNK)
    owner = lax.broadcasted_iota(jnp.int32, (tokens, CHUNK * states), 1) // states
    on_diag = place == owner
    column = lax.rem(lax.broadcasted_iota(jnp.int32, (states, CHUNK * states), 1), states)
    repeat = (column == lax.broadcasted_iota(jnp.int32, (states, CHUNK * states), 0)).astype(BF16)
    whole = r.proj[d]
    r.rank_low[d] = whole[:, :rank].astype(BF16)
    flipped = whole.T
    for start, blk, spread in (
        (rank, r.in_blk, r.in_spread),
        (rank + states, r.out_blk, r.out_spread),
    ):
        coef = whole[:, start : start + states].astype(BF16)
        blk[d] = jnp.where(on_diag, dot(coef, repeat), 0.0).astype(BF16)
        rows = flipped[start : start + states, :]
        for t in range(tokens):
            spread[d, t * states : (t + 1) * states, :] = jnp.broadcast_to(
                rows[:, t : t + 1], (states, LANES)
            )


def step_logits(r, d, cols):
    return dot(r.rank_low[d], r.w_dt[d, :, cols]) + r.dt_bias[d : d + 1, cols]


def stepping(r, d):
    inner = r.seed.shape[1]
    taps = r.conv_w.shape[1]

    def block(b, none):
        cols = pl.ds(pl.multiple_of(b * COLS, COLS), COLS)
        step = softplus(step_logits(r, d, cols))
        keep = r.masks[taps - 2] if d == 0 else r.masks[taps]
        keep = jnp.concatenate([keep] * (COLS // LANES), axis=1)
        r.masked[d, :, cols] = jnp.where(keep > 0.5, step, CUT_STEP)
        r.driven[d, :, cols] = step * r.active[d, :, cols].astype(F32)
        return none

    lax.fori_loop(0, inner // COLS, block, 0)


def state_rows(ref, d, first, j, states):
    return ref[d, pl.ds(pl.multiple_of((first + j) * states, states), states), :]


def summarise(r, d, begin, end):
    tokens, inner = r.seed.shape
    states = r.rate.shape[1]
    tiles = inner // LANES
    per = SCAN // LANES

    def block(b, none):
        lanes = [tile_at(b * SCAN + c * LANES) for c in range(per)]

        def group(i, carry):
            carry = list(carry)
            start = pl.multiple_of((i if d == 0 else tokens // 8 - 1 - i) * 8, 8)
            for k in range(8):
                j = k if d == 0 else 7 - k
                in_row = state_rows(r.in_spread, d, start, j, states)
                out_row = state_rows(r.out_spread, d, start, j, states)
                for c in range(per):
                    state, decay, adj = carry[c]
                    now = jnp.exp2(
                        row_of(r.masked.at[d], start, j, lanes[c]) * r.rate[d, :, lanes[c]]
                    )
                    state = now * state + in_row * row_of(r.driven.at[d], start, j, lanes[c])
                    decay = decay * now
                    adj = adj + decay * (out_row * row_of(r.seed, start, j, lanes[c]))
                    carry[c] = (state, decay, adj)
            return tuple(carry)

        zero = jnp.zeros((states, LANES), F32)
        one = jnp.ones((states, LANES), F32)
        carry = lax.fori_loop(0, tokens // 8, group, tuple((zero, one, zero) for _ in range(per)))
        for c in range(per):
            state, decay, adj = carry[c]
            down, up = (adj, state) if d == 0 else (state, adj)
            at = d * tiles + b * per + c
            r.sums[at, 0] = down.astype(BF16)
            r.sums[at, 1] = three_pieces(
                jnp.sum(r.masked[d, :, lanes[c]], axis=0, keepdims=True), states
            )
            r.sums[at, 2] = up.astype(BF16)
        return none

    lax.fori_loop(begin, end, block, 0)


def three_pieces(row, states):
    high = row.astype(BF16).astype(F32)
    middle = (row - high).astype(BF16).astype(F32)
    lowest = row - high - middle
    at = lax.broadcasted_iota(jnp.int32, (states, row.shape[-1]), 0)
    return jnp.where(
        at == 0, high, jnp.where(at == 1, middle, jnp.where(at == 2, lowest, 0.0))
    ).astype(BF16)


def remote(src, dst, sems, slot, peer, there=None):
    return pltpu.make_async_remote_copy(
        src_ref=src,
        dst_ref=dst,
        send_sem=sems[0].at[slot],
        recv_sem=sems[1].at[slot if there is None else there],
        device_id=(peer,),
        device_id_type=MESH,
    )


class Place:
    def __init__(self, count):
        self.count = count
        self.groups = count // PLANE
        self.me = lax.axis_index("seq")
        self.bits = [lax.rem(self.me, 2), lax.rem(self.me // 2, 2), lax.rem(self.me // 4, 2)]
        self.flips = [self.me + (1 - 2 * self.bits[i]) * (1 << i) for i in range(3)]
        self.level = self.me // PLANE
        self.low = lax.rem(self.me, PLANE)
        self.left = lax.rem(self.me + count - 1, count)
        self.right = lax.rem(self.me + 1, count)
        self.far = [lax.rem(self.level + k, self.groups) for k in range(1, self.groups)]

    def peers(self):
        base = self.level * PLANE
        peers = [base + lax.rem(self.low + k, PLANE) for k in range(1, PLANE)]
        return peers + [self.left, self.right] + [g * PLANE + self.low for g in self.far]


def add_into(into, own, first):
    def one(i, none):
        into[i] = into[i] + own[first + i]
        return none

    lax.fori_loop(0, into.shape[0], one, 0)


class Carries:
    def __init__(self, r, place, sems):
        self.r, self.place, self.sems = r, place, sems
        self.mine = place.low
        self.base = place.level * PLANE
        self.share = r.sums.shape[0] // PLANE

    def rows(self, j):
        return pl.ds(j * self.share, self.share)

    def combiners(self, d):
        return range(d * PLANE // 2, (d + 1) * PLANE // 2)

    def combines(self, d):
        return self.mine // (PLANE // 2) == d

    def out(self, j):
        r = self.r
        src, dst = r.sums.at[self.rows(j)], r.got.at[self.mine]
        return remote(src, dst, self.sems[0], j, self.base + j, self.mine)

    def arrival(self, s):
        r = self.r
        return remote(r.sums.at[self.rows(s)], r.got.at[s], self.sems[0], s, self.base + s)

    def back(self, j):
        r = self.r
        src, dst = r.back.at[j], r.entering.at[self.rows(self.mine)]
        return remote(src, dst, self.sems[2], j, self.base + j, self.mine)

    def entry(self, s):
        r = self.r
        return remote(
            r.back.at[s], r.entering.at[self.rows(s)], self.sems[2], s, self.base + s
        )

    def between(self):
        r, place = self.r, self.place
        copies = []
        for k, other in enumerate(place.far):
            start = jnp.where(other > place.level, 1, 0)
            src, dst = r.total.at[pl.ds(start, 2)], r.others.at[place.level]
            copies.append(remote(src, dst, self.sems[1], k, other * PLANE + self.mine))
        return copies

    def send(self, d):
        for j in self.combiners(d):

            @pl.when(self.mine != j)
            def _():
                self.out(j).start()

    def whole(self, pieces):
        pieces = pieces.astype(F32)
        return pieces[:, 0:1] + pieces[:, 1:2] + pieces[:, 2:3]

    def rates(self):
        r = self.r
        tiles = r.rate.shape[2] // LANES
        parts = []
        for c in range(self.share):
            at = self.mine * self.share + c
            parts.append(r.rate[at // tiles, :, tile_at(lax.rem(at, tiles) * LANES)][None])
        return jnp.concatenate(parts, axis=0)

    def combine(self, d):
        r = self.r

        @pl.when(self.combines(d))
        def _():
            mine, share = self.mine, self.share
            states = r.rate.shape[1]
            r.got[mine] = r.sums[self.rows(mine)]
            r.others[self.place.level] = jnp.zeros(r.others.shape[1:], BF16)
            for s in range(PLANE):

                @pl.when(mine != s)
                def _():
                    self.arrival(s).wait_recv()

            rates = self.rates()
            block = (share, states, LANES)
            up = jnp.zeros(block, F32)
            down = jnp.zeros(block, F32)
            time = jnp.zeros((share, 1, LANES), F32)
            for j in range(PLANE):
                now = self.whole(r.got[j, :, 1])
                up = jnp.exp2(rates * now) * up + r.got[j, :, 2].astype(F32)
                time = time + now
            for j in reversed(range(PLANE)):
                now = jnp.exp2(rates * self.whole(r.got[j, :, 1]))
                down = now * down + r.got[j, :, 0].astype(F32)
            r.total[0] = down.astype(BF16)
            for c in range(share):
                r.total[1, c] = three_pieces(time[c], states)
            r.total[2] = up.astype(BF16)
            for copy in self.between():
                copy.start()

    def spread(self, d):
        r = self.r

        @pl.when(self.combines(d))
        def _():
            mine, share, level = self.mine, self.share, self.place.level
            states = r.rate.shape[1]
            groups = self.place.groups
            for copy in self.between():
                copy.wait_recv()
            rates = self.rates()
            block = (share, states, LANES)
            up = jnp.zeros(block, F32)
            for g in range(groups):
                decay = jnp.exp2(rates * self.whole(r.others[g, 0]))
                up = jnp.where(g < level, decay * up + r.others[g, 1].astype(F32), up)
            down = jnp.zeros(block, F32)
            for g in reversed(range(groups)):
                decay = jnp.exp2(rates * self.whole(r.others[g, 1]))
                down = jnp.where(g > level, decay * down + r.others[g, 0].astype(F32), down)
            decays = [jnp.exp2(rates * self.whole(r.got[j, :, 1])) for j in range(PLANE)]
            for j in range(PLANE):
                r.back[j, :, 0] = up.astype(BF16)
                up = decays[j] * up + r.got[j, :, 2].astype(F32)
            for j in reversed(range(PLANE)):
                r.back[j, :, 1] = down.astype(BF16)
                down = decays[j] * down + r.got[j, :, 0].astype(F32)
            for j in range(PLANE):

                @pl.when(mine != j)
                def _():
                    self.back(j).start()

            r.entering[self.rows(mine)] = r.back[mine]

    def receive(self, d):
        for s in self.combiners(d):

            @pl.when(self.mine != s)
            def _():
                self.entry(s).wait_recv()

    def finish(self):
        for j in range(PLANE):

            @pl.when(self.mine != j)
            def _():
                self.out(j).wait_send()
                self.back(j).wait_send()

        for copy in self.between():
            copy.wait_send()


class Piece:
    def __init__(self, place, order, part, own, refs):
        self.place, self.order, self.part, self.own = place, order, part, own
        self.got1, self.got2, self.got3, self.got4 = refs[:4]
        self.sems = refs[4:]
        self.bits = [place.bits[0], place.bits[order[0]], place.bits[order[1]]]
        self.flips = [place.flips[0], place.flips[order[0]], place.flips[order[1]]]

    def hop(self, i):
        if i == 0:
            src = self.part.at[1 - self.bits[0]]
        else:
            half = 4 * self.place.groups >> i
            held = (self.got1, self.got2)[i - 1]
            src = held.at[pl.ds((1 - self.bits[i]) * half, half)]
        return remote(src, (self.got1, self.got2, self.got3)[i], self.sems, i, self.flips[i])

    def fan(self):
        return [
            remote(
                self.got3.at[g],
                self.got4.at[self.place.level],
                self.sems,
                3 + k,
                g * PLANE + self.place.low,
            )
            for k, g in enumerate(self.place.far)
        ]

    def step(self, i):
        groups = self.place.groups
        if i:
            self.hop(i - 1).wait_recv()
        if i == 1:
            add_into(self.got1, self.own, 0)
        elif i == 2:
            add_into(self.got2, self.got1, self.bits[1] * 2 * groups)
        elif i == 3:
            add_into(self.got3, self.got2, self.bits[2] * groups)
        if i < 3:
            self.hop(i).start()
            return
        for copy in self.fan():
            copy.start()
        self.got4[self.place.level] = self.got3[self.place.level]

    def end(self, share, begin):
        for copy in self.fan():
            copy.wait_recv()
        total = self.got4[0].astype(F32)
        for g in range(1, self.place.groups):
            total = total + self.got4[g].astype(F32)
        share[:, begin : begin + total.shape[1]] = total
        for copy in [self.hop(1), self.hop(2)] + self.fan():
            copy.wait_send()

    def release(self):
        self.hop(0).wait_send()


def piece_scratch(rows, cols, groups):
    return [
        pltpu.VMEM((size, rows, cols), BF16) for size in (4 * groups, 2 * groups, groups, groups)
    ] + [pltpu.SemaphoreType.DMA((2 + groups,))] * 2


def interleaved(chunks, compute, pieces, carry):
    jobs = []
    for i in range(chunks):
        carry = compute(i, i % 2, carry, jobs)
        jobs = pieces(i, i % 2)
    for job in jobs:
        job()
    return carry


def jobs_between(jobs, k):
    every = max(CHUNK // max(len(jobs), 1), 1)
    if jobs and k % every == 0 and k // every < len(jobs):
        jobs[k // every]()


def small_rows(taps):
    return 0, 2 * taps, 2 * taps + 2, 2 * taps + 4, 2 * taps + 8


def forward_scan(r, d):
    tokens, inner = r.seed.shape
    tiles = inner // LANES
    per = SCAN // LANES
    states = r.rate.shape[1]
    chunks = tokens // CHUNK
    rows = (r.rows0, r.rows1)

    def first_of(i):
        return (i if d == 0 else chunks - 1 - i) * CHUNK

    def block(b, none):
        cols = pl.ds(pl.multiple_of(b * SCAN, SCAN), SCAN)
        lanes = [tile_at(b * SCAN + c * LANES) for c in range(per)]
        edge = d * tokens * states
        for c in range(per):
            r.kept[edge : edge + states, lanes[c]] = r.entering[d * tiles + b * per + c, d]

        def compute(i, side, carry, jobs):
            carry = list(carry)
            first = first_of(i)
            for k in range(CHUNK):
                jobs_between(jobs, k)
                j = k if d == 0 else CHUNK - 1 - k
                in_row = state_rows(r.in_spread, d, first, j, states)
                for c in range(per):
                    now = jnp.exp2(
                        row_of(r.masked.at[d], first, j, lanes[c]) * r.rate[d, :, lanes[c]]
                    )
                    state = now * carry[c] + in_row * row_of(r.driven.at[d], first, j, lanes[c])
                    rows[side][
                        j * states : (j + 1) * states, c * LANES : (c + 1) * LANES
                    ] = state.astype(BF16)
                    carry[c] = state
            return tuple(carry)

        def pieces(i, side):
            here = pl.ds(first_of(i), CHUNK)

            def keep(q):
                half = CHUNK * states // 2
                slot = (first_of(i) + 1 - d) * states + q * half
                r.kept[slot : slot + half, cols] = rows[side][q * half : (q + 1) * half, :]

            def mix(q):
                part = pl.ds(pl.multiple_of(b * SCAN + q * COLS, COLS), COLS)
                mixed = dot(r.out_blk[d, here, :], rows[side][:, q * COLS : (q + 1) * COLS])
                if d == 0:
                    r.mixed[here, part] = mixed
                else:
                    r.mixed[here, part] += mixed

            def grad():
                r.out_acc[d, here, :] += contract_cols(
                    r.seed[here, cols].astype(BF16), rows[side][...]
                )

            return [
                functools.partial(mix, 0),
                functools.partial(keep, 0),
                functools.partial(mix, 1),
                functools.partial(keep, 1),
                grad,
            ]

        start = tuple(r.entering[d * tiles + b * per + c, d].astype(F32) for c in range(per))
        interleaved(chunks, compute, pieces, start)
        return none

    lax.fori_loop(0, inner // SCAN, block, 0)


def adjoint_scan(r, d, begin, end):
    tokens, inner = r.seed.shape
    tiles = inner // LANES
    per = SCAN // LANES
    states = r.rate.shape[1]
    taps = r.conv_w.shape[1]
    chunks = tokens // CHUNK
    wide = CHUNK * states
    adjs = (r.rows0, r.rows1)
    slopes = (r.slope0, r.slope1)
    ones = (
        lax.broadcasted_iota(jnp.int32, (CHUNK, wide), 1) // states
        == lax.broadcasted_iota(jnp.int32, (CHUNK, wide), 0)
    ).astype(BF16)

    def first_of(i):
        return (chunks - 1 - i if d == 0 else i) * CHUNK

    def block(b, none):
        cols = pl.ds(pl.multiple_of(b * SCAN, SCAN), SCAN)
        lanes = [tile_at(b * SCAN + c * LANES) for c in range(per)]
        low_rates = [r.rate[d, :, lanes[c]].astype(BF16) for c in range(per)]

        def compute(i, side, carry, jobs):
            carry = list(carry)
            first = first_of(i)
            for k in range(CHUNK):
                jobs_between(jobs, k)
                j = CHUNK - 1 - k if d == 0 else k
                slot = (first + j + d) * states
                out_row = state_rows(r.out_spread, d, first, j, states)
                part = slice(j * states, (j + 1) * states)
                for c in range(per):
                    here = slice(c * LANES, (c + 1) * LANES)
                    coming, total = carry[c]
                    step = row_of(r.masked.at[d], first, j, lanes[c])
                    now = jnp.exp2(step * r.rate[d, :, lanes[c]])
                    adj = out_row * row_of(r.seed, first, j, lanes[c]) + coming
                    coming = now * adj
                    slope = coming.astype(BF16) * r.kept[slot : slot + states, lanes[c]]
                    slope = slope * low_rates[c]
                    total = total + slope.astype(F32) * step
                    adjs[side][part, here] = adj.astype(BF16)
                    slopes[side][part, here] = slope
                    carry[c] = (coming, total)
            return tuple(carry)

        def pieces(i, side):
            here = pl.ds(first_of(i), CHUNK)

            def driven_side(q):
                part = pl.ds(pl.multiple_of(b * SCAN + q * COLS, COLS), COLS)
                r.driven_grad[d][here, part] = dot(
                    r.in_blk[d, here, :], adjs[side][:, q * COLS : (q + 1) * COLS]
                )

            def decay_side(q):
                part = pl.ds(pl.multiple_of(b * SCAN + q * COLS, COLS), COLS)
                r.decay_grad[d][here, part] = (
                    dot(ones, slopes[side][:, q * COLS : (q + 1) * COLS]) * LN2
                )

            def in_side():
                r.in_acc[d, here, :] += contract_cols(
                    r.driven[d, here, cols].astype(BF16), adjs[side][...]
                )

            return [
                functools.partial(driven_side, 0),
                functools.partial(decay_side, 0),
                in_side,
                functools.partial(driven_side, 1),
                functools.partial(decay_side, 1),
            ]

        zero = jnp.zeros((states, LANES), F32)
        start = tuple(
            (r.entering[d * tiles + b * per + c, 1 - d].astype(F32), zero) for c in range(per)
        )
        carry = interleaved(chunks, compute, pieces, start)
        at_rate = small_rows(taps)[4]
        for c in range(per):
            r.small[at_rate + d * states : at_rate + (d + 1) * states, lanes[c]] = (
                carry[c][1] * LN2
            )
        return none

    lax.fori_loop(begin, end, block, 0)


def output_half(r, count, half):
    tokens, inner = r.mixed.shape
    model = r.hidden.shape[1]
    begin = half * inner // COLS // 2

    def block(b, none):
        cols = pl.ds(pl.multiple_of(b * COLS, COLS), COLS)
        mixed = r.mixed[:, cols]
        for d in range(2):
            mixed = mixed + r.d_skip[d : d + 1, cols] * r.active[d, :, cols].astype(F32)
        gate = r.gate_branch[:, cols]
        sigma = sigmoid(gate)
        now = (mixed * (gate * sigma)).astype(BF16)
        r.gated[:, cols] = now
        slope = sigma * (1.0 + gate * (1.0 - sigma))
        back = (r.gated_grad[:, cols] * mixed * slope).astype(BF16)
        r.gate_branch_grad[:, cols] = back
        r.branch[...] += dot(now, r.w_out[cols, :])
        here = pl.ds(pl.multiple_of((b - begin) * COLS, COLS), COLS)
        r.whole[:, here] = contract_rows(r.mixer_own[...], back)
        return none

    lax.fori_loop(begin, begin + inner // COLS // 2, block, 0)
    part = (r.gate0, r.gate1)[half]
    for o in range(count):
        first, later = slot_of(o, count, (XY, YX)[half])
        part[first, later] = stacked_rows(
            r.whole, r.stage, o, model // count, 0, model
        ).astype(BF16)


def output_weights(r, count):
    tokens, inner = r.mixed.shape
    model = r.hidden.shape[1]
    rows = inner // count
    half = model // 2
    chunk = inner // 8
    per = count // 8
    for q in range(8):
        r.whole[0:chunk, :] = contract_rows(
            r.gated[:, q * chunk : (q + 1) * chunk], r.branch_grad[...]
        )
        for i in range(per):
            low = r.whole[i * rows : (i + 1) * rows, :].astype(BF16)
            first, later = slot_of(q * per + i, count, XY)
            r.out0[first, later, 0:rows] = low[:, :half]
            first, later = slot_of(q * per + i, count, YX)
            r.out1[first, later, 0:rows] = low[:, half:]


def column_sum(values):
    return jnp.sum(values, axis=0, keepdims=True)


def through_steps(r):
    tokens, inner = r.seed.shape
    taps = r.conv_w.shape[1]
    rank = r.w_dt.shape[1]
    proj = r.w_x.shape[1]
    states = r.rate.shape[1]
    _, _, at_dt, at_skip, _ = small_rows(taps)
    r.rank_grad[...] = jnp.zeros_like(r.rank_grad)

    def block(b, none):
        cols = pl.ds(pl.multiple_of(b * COLS, COLS), COLS)
        for d in range(2):
            act = r.active[d, :, cols].astype(F32)
            value = step_logits(r, d, cols)
            back = r.driven_grad[d][:, cols]
            grown = r.seed[:, cols]
            grad = (r.decay_grad[d][:, cols] + back * act) * sigmoid(value)
            low = grad.astype(BF16)
            r.driven_grad[d][:, cols] = (
                back * softplus(value) + grown * r.d_skip[d : d + 1, cols]
            )
            r.small[at_dt + d : at_dt + d + 1, cols] = column_sum(grad)
            r.small[at_skip + d : at_skip + d + 1, cols] = column_sum(grown * act)
            r.rank_grad[d] += contract_cols(low, r.w_dt[d, :, cols])
            r.in_spread[d, cols, proj : proj + rank] = contract_rows(low, r.rank_low[d])
        return none

    lax.fori_loop(0, inner // COLS, block, 0)

    place = lax.rem(lax.broadcasted_iota(jnp.int32, (tokens, CHUNK * states), 0), CHUNK)
    owner = lax.broadcasted_iota(jnp.int32, (tokens, CHUNK * states), 1) // states
    on_diag = place == owner
    column = lax.rem(lax.broadcasted_iota(jnp.int32, (CHUNK * states, states), 0), states)
    gather = (column == lax.broadcasted_iota(jnp.int32, (CHUNK * states, states), 1)).astype(BF16)
    for d in range(2):
        r.proj_grad[d, :, 0:rank] = r.rank_grad[d].astype(BF16)
        for start, acc in ((rank, r.in_acc), (rank + states, r.out_acc)):
            kept = jnp.where(on_diag, acc[d], 0.0).astype(BF16)
            r.proj_grad[d, :, start : start + states] = dot(kept, gather).astype(BF16)

    def weights(b, none):
        cols = pl.ds(pl.multiple_of(b * COLS, COLS), COLS)
        for d in range(2):
            r.in_spread[d, cols, 0:proj] = contract_rows(r.active[d, :, cols], r.proj_grad[d])
        return none

    lax.fori_loop(0, inner // COLS, weights, 0)


def through_conv(r, begin, end):
    tokens, inner = r.seed.shape
    taps = r.conv_w.shape[1]
    at_conv, at_bias, _, _, _ = small_rows(taps)

    def block(b, none):
        cols = pl.ds(pl.multiple_of(b * COLS, COLS), COLS)
        r.conv_wide[...] = r.conv_keep[:, cols].astype(F32)
        r.input_wide[...] = jnp.zeros_like(r.input_wide)
        for d in range(2):
            total = r.driven_grad[d][:, cols] + dot(r.proj_grad[d], r.w_x[d, :, cols])
            for c in range(COLS // LANES):
                lanes = tile_at(b * COLS + c * LANES)
                here = slice(c * LANES, (c + 1) * LANES)
                grad = total[:, here] * r.conv_slope[d, :, lanes].astype(F32)
                r.small[at_bias + d : at_bias + d + 1, lanes] = column_sum(grad)
                for k in range(taps):
                    offset = offset_of(d, k, taps)
                    window = slice(RIM + offset, RIM + offset + tokens)
                    part = grad * r.masks[offset + taps - 1]
                    at = at_conv + d * taps + k
                    r.small[at : at + 1, lanes] = column_sum(part * r.conv_wide[window, here])
                    r.input_wide[window, here] += r.conv_w[d, k : k + 1, lanes] * part
        low = r.input_wide[...].astype(BF16)
        here = pl.ds(pl.multiple_of((b - begin) * COLS, COLS), COLS)
        r.whole[:, here] = contract_rows(r.mixer[...], low)
        r.norm_wide[...] += contract_cols(low, r.w_conv[:, cols])
        r.norm_wide[RIM : RIM + tokens, :] += contract_cols(
            r.gate_branch_grad[:, cols], r.w_gate[:, cols]
        )
        r.small_cols[cols, :] = r.small[:, cols].T
        return none

    lax.fori_loop(begin, end, block, 0)


def fill_columns(r, part, count):
    rows = r.seed.shape[1] // count
    for o in range(count):
        first, later = slot_of(o, count, XY)
        for d in range(2):
            part[first, later, 0:rows, d * LANES : (d + 1) * LANES] = r.in_spread[
                d, o * rows : (o + 1) * rows, :
            ].astype(BF16)


def fill_conv(r, parts, count):
    inner = r.seed.shape[1]
    model = r.normed.shape[1]
    rows, mrows = inner // count, model // count
    for o in range(count):
        both = stacked_rows(r.whole, r.stage, o, mrows, 0, model).astype(BF16)
        if len(parts) == 1:
            first, later = slot_of(o, count, YX)
            parts[0][first, later] = both
            continue
        cut = parts[0].shape[3]
        rest = model // 2 - cut
        first, later = slot_of(o, count, XY)
        parts[0][first, later] = both[:, :cut]
        first, later = slot_of(o, count, YX)
        parts[1][first, later, :, 0:rest] = both[:, cut:]
        parts[1][first, later, 0:rows, rest:] = r.small_cols[o * rows : (o + 1) * rows, :].astype(
            BF16
        )


def modulation_shares(r, place):
    seqs, model = r.condition.shape
    mrows = r.w_mod_share.shape[0]
    width = r.b_mod_share.shape[1]

    def picked(total, number):
        source = lax.broadcasted_iota(jnp.int32, (total, number), 0)
        return source == place.me * number + lax.broadcasted_iota(jnp.int32, (total, number), 1)

    cond = r.condition[...]
    cond_act = (cond * sigmoid(cond)).astype(BF16)
    my_cond = dot(cond_act, picked(model, mrows).astype(BF16))
    totals = r.mod[0:seqs, :]
    r.w_mod_share[...] = contract_rows(my_cond, totals, HIGHEST)
    bias = jnp.broadcast_to(jnp.sum(totals, axis=0, keepdims=True), (8, 3 * model))
    r.b_mod_share[...] = dot(bias, picked(3 * model, width).astype(F32), precision=HIGHEST)[0:1]


def input_gradient(r, place):
    tokens, model = r.hidden.shape
    norm_grad = r.norm_wide[RIM : RIM + tokens, :]
    low = jnp.where(place.me > 0, r.edge_got[0:RIM, :], 0.0)
    high = jnp.where(place.me < place.count - 1, r.edge_got[RIM:, :], 0.0)
    middle = jnp.zeros((tokens - 2 * RIM, model), F32)
    norm_grad = norm_grad + jnp.concatenate([low, middle, high], axis=0)
    scaled = norm_grad * r.scale1[...]
    normal = r.normed[RIM : RIM + tokens, :]
    r.grad_x[...] = r.grad_out[...].astype(F32) + r.rescale[:, 0:1] * (
        scaled
        - jnp.mean(scaled, axis=1, keepdims=True)
        - normal * jnp.mean(scaled * normal, axis=1, keepdims=True)
    )


def modulation_sums(r):
    tokens = r.seed.shape[0]
    model = r.normed.shape[1]
    seqs = r.mod_part.shape[1]
    half = r.mod_part.shape[2]
    seq_rows = r.hot[:, 0:seqs]
    grads = r.norm_wide[...]
    sums = [
        contract_rows(seq_rows, grads, HIGHEST),
        contract_rows(seq_rows, grads * r.normed[...], HIGHEST),
        contract_rows(r.hot[RIM : RIM + tokens, 0:seqs], r.branch[...], HIGHEST),
    ]
    whole = jnp.concatenate(sums, axis=1)
    r.mod_part[0] = whole[:, :half].astype(BF16)
    r.mod_part[1] = whole[:, half:].astype(BF16)


class ModSums:
    def __init__(self, place, r, sems):
        self.place, self.r, self.sems = place, r, sems
        self.core = place.bits[0]
        self.chip = place.bits[1] + 2 * place.bits[2]

    def copies(self, i):
        place, r, sems = self.place, self.r, self.sems
        if i == 0:
            return [remote(r.mod_part.at[1 - self.core], r.m1, sems, 0, place.flips[0])]
        if i == 1:
            peers = (place.flips[1], place.flips[2], place.flips[1] + place.flips[2] - place.me)
            return [
                remote(r.m1, r.m2.at[self.chip], sems, 1 + k, peer) for k, peer in enumerate(peers)
            ]
        if i == 2:
            return [
                remote(r.m1, r.m3.at[place.level], sems, 4 + k, g * PLANE + place.low)
                for k, g in enumerate(place.far)
            ]
        slot = 4 + len(place.far)
        return [
            remote(r.m4.at[self.core], r.m4.at[self.core], sems, slot, place.flips[0])
        ]

    def total(self, ref, number):
        total = ref[0].astype(F32)
        for g in range(1, number):
            total = total + ref[g].astype(F32)
        return total.astype(BF16)

    def step(self, i):
        place, r = self.place, self.r
        if i:
            for copy in self.copies(i - 1):
                copy.wait_recv()
        if i == 1:
            r.m1[...] = r.m1[...] + r.mod_part[self.core]
            r.m2[self.chip] = r.m1[...]
        elif i == 2:
            for copy in self.copies(1):
                copy.wait_send()
            summed = self.total(r.m2, 4)
            r.m1[...] = summed
            r.m3[place.level] = summed
        elif i == 3:
            r.m4[self.core] = self.total(r.m3, place.groups)
        for copy in self.copies(i):
            copy.start()

    def end(self, mod):
        half = mod.shape[1] // 2
        self.copies(3)[0].wait_recv()
        for c in range(2):
            mod[:, c * half : (c + 1) * half] = self.r.m4[c].astype(F32)[0 : mod.shape[0]]
        for i in (0, 2, 3):
            for copy in self.copies(i):
                copy.wait_send()


def late_columns(model, proj, rank, taps, states):
    first = proj + rank
    small = 2 * taps + 8 + 2 * states
    half = model // 2
    cut = half // 2 // LANES * LANES + LANES
    return 2 * (first + -first % LANES), half, cut, half - cut + small + -small % LANES


def block_kernel(count, names, lates, *refs):
    refs = list(refs)

    def take(size):
        taken = refs[:size]
        del refs[:size]
        return taken

    in_names, weight_names, out_names, scratch_names = names
    given = take(len(in_names))
    weights_any = take(5)
    outs = take(len(out_names))
    weights = take(len(weight_names))
    scratch = take(len(scratch_names))
    piece_refs = [take(6) for _ in range(8)]
    carry_sems = [take(2) for _ in range(3)]
    mod_sems, edge_sems, halo_sems = take(2), take(2), take(2)
    (load_sems,) = take(1)
    r = Refs(
        in_names + weight_names + out_names + scratch_names, given + weights + outs + scratch
    )
    tokens, inner = r.seed.shape
    blocks = inner // COLS
    scans = inner // SCAN
    r.decay_grad = (r.decay0, r.gate_branch)
    r.driven_grad = (r.driven0, r.gated_grad)

    w_mod_any, w_in_any, w_out_any, w_x_any, w_dt_any = weights_any
    model = r.hidden.shape[1]
    low_mod = r.kept.at[pl.ds(0, model), pl.ds(0, 2 * model)]
    high_mod = r.kept.at[pl.ds(model, model), pl.ds(0, model)]
    sources = (
        w_mod_any.at[:, pl.ds(0, 2 * model)],
        w_mod_any.at[:, pl.ds(2 * model, model)],
        w_in_any.at[:, pl.ds(0, inner)],
        w_in_any.at[:, pl.ds(inner, inner)],
        w_out_any,
        w_x_any,
        w_dt_any,
    )
    loads = [
        pltpu.make_async_copy(src, dst, load_sems.at[i])
        for i, (src, dst) in enumerate(zip(sources, [low_mod, high_mod] + weights))
    ]
    for load in loads:
        load.start()

    place = Place(count)
    barrier = pltpu.get_barrier_semaphore()
    peers = place.peers()
    for peer in peers:
        pl.semaphore_signal(barrier, inc=1, device_id=(peer,), device_id_type=MESH)
    me, core = place.me, place.bits[0]
    carries = Carries(r, place, carry_sems)
    views = (
        r.gate1.at[:, :, :, pl.ds(0, lates[0])],
        r.gate0,
        r.out0.at[:, :, :, pl.ds(0, lates[2])],
        r.out1.at[:, :, :, pl.ds(0, lates[3])],
    )
    parts = (r.gate0, r.gate1, r.out0, r.out1) + views
    pieces = [
        Piece(place, (XY, YX)[p % 2], part, part.at[core], piece_refs[p])
        for p, part in enumerate(parts)
    ]
    early, late = pieces[:4], pieces[4:]

    segment, wide_segment = token_masks(r, me * tokens)
    r.rate[...] = -jnp.exp(r.a_log[...]) * LOG2E
    r.out_acc[...] = jnp.zeros_like(r.out_acc)
    r.in_acc[...] = jnp.zeros_like(r.in_acc)
    r.small[...] = jnp.zeros_like(r.small)
    r.branch[...] = jnp.zeros_like(r.branch)
    r.norm_wide[...] = jnp.zeros_like(r.norm_wide)
    pl.semaphore_wait(barrier, len(peers))
    halos = [
        remote(r.hidden.at[pl.ds(tokens - 16, 16)], r.below, halo_sems, 0, place.right),
        remote(r.hidden.at[pl.ds(0, 16)], r.above, halo_sems, 1, place.left),
    ]
    for halo in halos:
        halo.start()
    cond = r.condition[...]
    cond_act = (cond * sigmoid(cond)).astype(BF16)
    loads[0].wait()
    loads[1].wait()
    seqs = cond.shape[0]
    r.modulation[0:seqs, 0 : 2 * model] = dot(cond_act, low_mod[...])
    r.modulation[0:seqs, 2 * model :] = dot(cond_act, high_mod[...])
    for halo in halos:
        halo.wait_recv()
    below = jnp.where(me > 0, r.below[...].astype(F32), 0.0)[16 - RIM :]
    above = jnp.where(me < count - 1, r.above[...].astype(F32), 0.0)[:RIM]
    normalise(r, below, above)
    modulate(r, segment, wide_segment)
    for load in loads[2:]:
        load.wait()
    project(r)
    coefficients(r, 0)
    stepping(r, 0)

    summarise(r, 0, 0, scans)
    carries.send(0)
    convolve_reverse(r)
    coefficients(r, 1)
    stepping(r, 1)
    carries.combine(0)
    summarise(r, 1, 0, scans - 1)
    carries.spread(0)
    summarise(r, 1, scans - 1, scans)
    carries.send(1)
    carries.receive(0)
    forward_scan(r, 0)
    carries.combine(1)
    adjoint_scan(r, 0, 0, scans - 1)
    carries.spread(1)
    adjoint_scan(r, 0, scans - 1, scans)
    carries.receive(1)
    forward_scan(r, 1)

    output_half(r, count, 0)
    early[0].step(0)
    output_half(r, count, 1)
    early[1].step(0)
    output_weights(r, count)
    early[2].step(0)
    early[3].step(0)
    r.output[...] = (r.hidden[...].astype(F32) + r.gate_rows[...] * r.branch[...]).astype(BF16)
    r.branch[...] = r.grad_out[...].astype(F32) * r.branch[...]
    early[0].step(1)
    early[1].step(1)
    adjoint_scan(r, 1, 0, 1)
    early[2].step(1)
    early[3].step(1)
    adjoint_scan(r, 1, 1, scans)
    through_steps(r)
    early[0].step(2)
    early[1].step(2)
    for piece in early:
        piece.release()
    fill_columns(r, views[0], count)
    late[0].step(0)
    through_conv(r, 0, blocks // 2)
    early[2].step(2)
    early[3].step(2)
    fill_conv(r, views[1:2], count)
    late[1].step(0)
    late[0].step(1)
    early[0].step(3)
    early[1].step(3)
    through_conv(r, blocks // 2, blocks)
    late[1].step(1)
    modulation_sums(r)
    mods = ModSums(place, r, mod_sems)
    mods.step(0)
    fill_conv(r, views[2:], count)
    late[2].step(0)
    late[3].step(0)
    mods.step(1)
    edges = [
        remote(
            r.norm_wide.at[pl.ds(0, RIM)],
            r.edge_got.at[pl.ds(RIM, RIM)],
            edge_sems,
            0,
            place.left,
        ),
        remote(
            r.norm_wide.at[pl.ds(r.norm_wide.shape[0] - RIM, RIM)],
            r.edge_got.at[pl.ds(0, RIM)],
            edge_sems,
            1,
            place.right,
        ),
    ]
    for copy in edges:
        copy.start()
    late[2].step(1)
    late[3].step(1)
    early[2].step(3)
    early[3].step(3)
    late[0].step(2)
    late[1].step(2)
    mods.step(2)
    width = r.share_early.shape[1] // 4
    for p, at in enumerate((2, 3, 0, 1)):
        early[p].end(r.share_early, at * width)
    late[2].step(2)
    late[3].step(2)
    late[0].step(3)
    late[1].step(3)
    mods.step(3)
    for copy in edges:
        copy.wait_recv()
    input_gradient(r, place)
    late[2].step(3)
    late[3].step(3)
    mods.end(r.mod)
    modulation_shares(r, place)
    begin = 0
    for piece, view in zip(late, views):
        piece.end(r.share_late, begin)
        piece.release()
        begin += view.shape[3]
    carries.finish()
    for copy in edges + halos:
        copy.wait_send()


def run_block(count, given, weights):
    w_mod, w_in, w_out, w_x, w_dt = weights
    tokens, model = given.hidden.shape
    inner = w_in.shape[1] // 2
    rank = w_dt.shape[1]
    proj = w_x.shape[1]
    states = given.a_log.shape[1]
    taps = given.conv_w.shape[1]
    groups = count // PLANE
    wide = tokens + 2 * RIM
    tiles = inner // LANES
    share = 2 * tiles // PLANE
    rows = slot_rows(count, inner)
    lates = late_columns(model, proj, rank, taps, states)
    small = lates[3] - (model // 2 - lates[2])
    both = (2, tokens, inner)
    spread = (2, tokens * states, LANES)
    diag = (2, tokens, CHUNK * states)
    mod = (8, 3 * model)
    half_mod = (16, 3 * model // 2)
    slots = pltpu.VMEM((2, count // 2, rows, model // 2), BF16)
    buffer = pltpu.VMEM((CHUNK * states, SCAN), BF16)
    full = pltpu.VMEM((tokens, inner), F32)
    outs = dict(
        output=shaped((tokens, model), BF16),
        grad_x=shaped((tokens, model)),
        w_mod_share=shaped((model // count, 3 * model)),
        b_mod_share=shaped((1, 3 * model // count)),
        share_early=shaped((rows, 2 * model)),
        share_late=shaped((rows, sum(lates))),
    )
    held = dict(
        w_conv=pltpu.VMEM((model, inner), BF16),
        w_gate=pltpu.VMEM((model, inner), BF16),
        w_out=pltpu.VMEM(w_out.shape, BF16),
        w_x=pltpu.VMEM(w_x.shape, BF16),
        w_dt=pltpu.VMEM(w_dt.shape, BF16),
    )
    scratch = dict(
        mixer=pltpu.VMEM((wide, model), BF16),
        mixer_own=pltpu.VMEM((tokens, model), BF16),
        normed=pltpu.VMEM((wide, model), F32),
        rescale=pltpu.VMEM((tokens, LANES), F32),
        scale1=pltpu.VMEM((tokens, model), F32),
        gate_rows=pltpu.VMEM((tokens, model), F32),
        branch_grad=pltpu.VMEM((tokens, model), BF16),
        conv_keep=pltpu.VMEM((wide, inner), BF16),
        conv_wide=pltpu.VMEM((wide, COLS), F32),
        conv_slope=pltpu.VMEM(both, BF16),
        active=pltpu.VMEM(both, BF16),
        gate_branch=full,
        gated_grad=full,
        seed=full,
        proj=pltpu.VMEM((2, tokens, proj), F32),
        rank_low=pltpu.VMEM((2, tokens, rank), BF16),
        masked=pltpu.VMEM(both, F32),
        driven=pltpu.VMEM(both, F32),
        in_spread=pltpu.VMEM(spread, F32),
        out_spread=pltpu.VMEM(spread, F32),
        in_blk=pltpu.VMEM(diag, BF16),
        out_blk=pltpu.VMEM(diag, BF16),
        rate=pltpu.VMEM((2, states, inner), F32),
        masks=pltpu.VMEM((2 * taps - 1, tokens, LANES), F32),
        hot=pltpu.VMEM((wide, LANES), F32),
        below=pltpu.VMEM((16, model), BF16),
        above=pltpu.VMEM((16, model), BF16),
        modulation=pltpu.VMEM((8, w_mod.shape[1]), F32),
        sums=pltpu.VMEM((2 * tiles, 3, states, LANES), BF16),
        got=pltpu.VMEM((PLANE, share, 3, states, LANES), BF16),
        total=pltpu.VMEM((3, share, states, LANES), BF16),
        others=pltpu.VMEM((groups, 2, share, states, LANES), BF16),
        back=pltpu.VMEM((PLANE, share, 2, states, LANES), BF16),
        entering=pltpu.VMEM((2 * tiles, 2, states, LANES), BF16),
        kept=pltpu.VMEM(((tokens + 1) * states, inner), BF16),
        rows0=buffer,
        rows1=buffer,
        slope0=buffer,
        slope1=buffer,
        mixed=full,
        decay0=full,
        driven0=full,
        out_acc=pltpu.VMEM(diag, F32),
        in_acc=pltpu.VMEM(diag, F32),
        gated=pltpu.VMEM((tokens, inner), BF16),
        gate_branch_grad=pltpu.VMEM((tokens, inner), BF16),
        branch=pltpu.VMEM((tokens, model), F32),
        whole=pltpu.VMEM((model, inner // 2), F32),
        stage=pltpu.VMEM((rows, model // 2), F32),
        gate0=slots,
        gate1=slots,
        out0=slots,
        out1=slots,
        small=pltpu.VMEM((small, inner), F32),
        rank_grad=pltpu.VMEM((2, tokens, rank), F32),
        proj_grad=pltpu.VMEM((2, tokens, proj), BF16),
        input_wide=pltpu.VMEM((wide, COLS), F32),
        small_cols=pltpu.VMEM((inner, small), F32),
        norm_wide=pltpu.VMEM((wide, model), F32),
        mod_part=pltpu.VMEM((2,) + half_mod, BF16),
        m1=pltpu.VMEM(half_mod, BF16),
        m2=pltpu.VMEM((4,) + half_mod, BF16),
        m3=pltpu.VMEM((groups,) + half_mod, BF16),
        m4=pltpu.VMEM((2,) + half_mod, BF16),
        mod=pltpu.VMEM(mod, F32),
        edge_got=pltpu.VMEM((2 * RIM, model), F32),
    )
    sems = pltpu.SemaphoreType.DMA
    pieces = []
    for cols in (model // 2,) * 4 + lates:
        pieces += piece_scratch(rows, cols, groups)
    given = vars(given)
    names = tuple(tuple(part) for part in (given, held, outs, scratch))
    return pl.pallas_call(
        functools.partial(block_kernel, count, names, lates),
        in_specs=[pl.BlockSpec(memory_space=pltpu.SMEM)] + [VMEM] * (len(given) - 1) + [ANY] * 5,
        out_specs=[VMEM] * len(outs),
        out_shape=list(outs.values()),
        scratch_shapes=list(held.values())
        + list(scratch.values())
        + pieces
        + [sems((PLANE,))] * 2
        + [sems((groups,))] * 2
        + [sems((PLANE,))] * 2
        + [sems((6 + groups,))] * 2
        + [sems((2,))] * 4
        + [sems((len(held) + 2,))],
        compiler_params=pltpu.CompilerParams(
            collective_id=0, has_side_effects=True, vmem_limit_bytes=63 * MIB
        ),
        name="block",
    )(*given.values(), *weights)


def finish_kernel(
    count,
    proj,
    rank,
    taps,
    states,
    share_early,
    share_late,
    made,
    made_grad,
    made_w_mod,
    made_b_mod,
    output,
    grad_x,
    w_mod,
    b_mod,
    w_in,
    conv_w,
    conv_b,
    w_x,
    w_dt,
    dt_bias,
    a_log,
    d_skip,
    w_out,
):
    tokens, model = output.shape
    mrows, double = w_in.shape
    inner = double // 2
    rows = w_out.shape[0]
    half = model // 2
    first = late_columns(model, proj, rank, taps, states)[0]

    output[...] = made[...]
    grad_x[...] = made_grad[...]
    w_mod[...] = made_w_mod[...]
    b_mod[...] = made_b_mod[...]
    w_out[...] = share_early[0:rows, 0:model]
    for i in range(2):
        low = share_late[:, first + i * half : first + (i + 1) * half]
        high = share_early[:, model + i * half : model + (i + 1) * half]
        for at, both in ((i * model, low), (inner + i * model, high)):
            w_in[:, at : at + half] = both[0:mrows]
            w_in[:, at + half : at + model] = both[mrows : 2 * mrows]

    flipped = share_late[:, 0:first].T
    for d in range(2):
        at = d * first // 2
        w_x[d] = share_late[0:rows, at : at + proj]
        w_dt[d] = flipped[at + proj : at + proj + rank, 0:rows]
    flipped = share_late[:, first + model :].T
    for d in range(2):
        conv_w[d] = flipped[d * taps : (d + 1) * taps, 0:rows]
    at = 2 * taps
    conv_b[...] = flipped[at : at + 2, 0:rows]
    dt_bias[...] = flipped[at + 2 : at + 4, 0:rows]
    d_skip[...] = flipped[at + 4 : at + 6, 0:rows]
    at = at + 8
    for d in range(2):
        a_log[d] = flipped[at + d * states : at + (d + 1) * states, 0:rows]


def on_device(
    count,
    hidden,
    condition,
    seq_lengths,
    w_mod,
    b_mod,
    w_in,
    conv_w,
    conv_b,
    w_x,
    w_dt,
    dt_bias,
    a_log,
    d_skip,
    w_out,
    grad_out,
):
    tokens, model = hidden.shape
    inner = w_in.shape[1] // 2
    rank = w_dt.shape[1]
    proj = w_x.shape[2]
    states = a_log.shape[1]
    taps = conv_w.shape[1]
    rows, mrows = inner // count, model // count
    given = types.SimpleNamespace(
        lengths=seq_lengths,
        hidden=hidden,
        condition=condition,
        b_mod=b_mod.reshape(-1, LANES),
        conv_w=conv_w,
        conv_b=conv_b,
        dt_bias=dt_bias,
        d_skip=d_skip,
        a_log=a_log,
        grad_out=grad_out,
    )
    weights = (w_mod, w_in, w_out, jnp.swapaxes(w_x, 1, 2), w_dt)
    output, grad_x, w_mod_share, b_mod_share, share_early, share_late = run_block(
        count, given, weights
    )
    results = pl.pallas_call(
        functools.partial(finish_kernel, count, proj, rank, taps, states),
        in_specs=[VMEM] * 6,
        out_specs=[VMEM] * 13,
        out_shape=[
            shaped((tokens, model), BF16),
            shaped((tokens, model)),
            shaped((mrows, 3 * model)),
            shaped((1, 3 * model // count)),
            shaped((mrows, 2 * inner)),
            shaped((2, taps, rows)),
            shaped((2, rows)),
            shaped((2, rows, proj)),
            shaped((2, rank, rows)),
            shaped((2, rows)),
            shaped((2, states, rows)),
            shaped((2, rows)),
            shaped((rows, model)),
        ],
        compiler_params=pltpu.CompilerParams(vmem_limit_bytes=60 * MIB),
        name="finish",
    )(share_early, share_late, output, grad_x, w_mod_share, b_mod_share)
    return tuple(results[:3]) + (results[3].reshape(-1),) + tuple(results[4:])


def solution(mesh):
    in_specs = (P("seq", None),) + (P(),) * 13 + (P("seq", None),)
    out_specs = (
        P("seq", None),
        P("seq", None),
        P("seq", None),
        P("seq"),
        P("seq", None),
        P(None, None, "seq"),
        P(None, "seq"),
        P(None, "seq", None),
        P(None, None, "seq"),
        P(None, "seq"),
        P(None, None, "seq"),
        P(None, "seq"),
        P("seq", None),
    )
    return jax.shard_map(
        functools.partial(on_device, mesh.shape["seq"]),
        mesh=mesh,
        in_specs=in_specs,
        out_specs=out_specs,
        check_vma=False,
    )
```

```python
import functools
import types

import jax
import jax.numpy as jnp
from jax import lax
from jax.experimental import pallas as pl
from jax.experimental.pallas import tpu as pltpu
from jax.sharding import PartitionSpec as P

EPSILON = 1e-06
HIGHEST = lax.Precision.HIGHEST
MESH = pl.DeviceIdType.MESH
LANES = 128
LOG2E = 1.4426950408889634
LN2 = 0.6931471805599453
CUT_STEP = 1e9
PLANE = 8
RIM = 8
CHUNK = 16
XY, YX = (1, 2), (2, 1)
COLS = 256
SCAN = 512
MIB = 1024 * 1024
F32 = jnp.float32
BF16 = jnp.bfloat16
VMEM = pl.BlockSpec(memory_space=pltpu.VMEM)
ANY = pl.BlockSpec(memory_space=pl.ANY)


def shaped(shape, dtype=F32):
    return jax.ShapeDtypeStruct(shape, dtype)


def dot(left, right, dims=((1,), (0,)), precision=None):
    return lax.dot_general(
        left, right, (dims, ((), ())), precision=precision, preferred_element_type=F32
    )


def contract_rows(left, right, precision=None):
    return dot(left, right, ((0,), (0,)), precision)


def contract_cols(left, right):
    return dot(left, right, ((1,), (1,)))


def sigmoid(values):
    return 1.0 / (1.0 + jnp.exp(-values))


def softplus(values):
    return jnp.maximum(values, 0.0) + jnp.log1p(jnp.exp(-jnp.abs(values)))


def tile_at(start):
    return pl.ds(pl.multiple_of(start, LANES), LANES)


def row_of(ref, first, j, lanes):
    eight = pl.ds(pl.multiple_of(first + j // 8 * 8, 8), 8)
    return ref.at[eight, lanes][j % 8 : j % 8 + 1, :]


def segments(positions, bounds):
    total = jnp.full(positions.shape, -1, jnp.int32)
    for bound in bounds:
        total = total + (positions >= bound).astype(jnp.int32)
    return total


def read_bounds(lengths):
    bounds = [jnp.int32(0)]
    for j in range(lengths.shape[0]):
        bounds.append(bounds[-1] + lengths[j])
    return bounds


def rows_iota(rows):
    return lax.broadcasted_iota(jnp.int32, (rows, LANES), 0)


def offset_of(d, k, taps):
    return k - (taps - 1) if d == 0 else taps - 1 - k


def slot_of(o, count, order):
    bits = [o & 1, o >> 1 & 1, o >> 2 & 1]
    return bits[0], (bits[order[0]] * 2 + bits[order[1]]) * (count // PLANE) + o // PLANE


def slot_rows(count, inner):
    rows = inner // count
    return rows + -rows % 16


def stacked_rows(source, stage, o, rows, begin, end):
    middle = (begin + end) // 2
    part = pl.ds(o * rows, rows)
    if rows % 8 == 0:
        return jnp.concatenate([source[part, begin:middle], source[part, middle:end]], axis=0)
    stage[0:rows, :] = source[part, begin:middle]
    stage[rows : 2 * rows, :] = source[part, middle:end]
    return stage[...]


class Refs:
    def __init__(self, names, refs):
        for name, ref in zip(names, refs):
            setattr(self, name, ref)


def token_masks(r, first):
    tokens = r.hidden.shape[0]
    wide = r.normed.shape[0]
    taps = r.conv_w.shape[1]
    bounds = read_bounds(r.lengths)
    position = first + rows_iota(tokens)
    segment = segments(position, bounds)
    for offset in range(1 - taps, taps):
        r.masks[offset + taps - 1] = (segments(position + offset, bounds) == segment).astype(F32)
    wide_segment = segments(first - RIM + rows_iota(wide), bounds)
    lane = lax.broadcasted_iota(jnp.int32, (wide, LANES), 1)
    r.hot[...] = (wide_segment == lane).astype(F32)
    return segment, wide_segment


def normalise(r, below, above):
    tokens = r.hidden.shape[0]
    x = jnp.concatenate([below, r.hidden[...].astype(F32), above], axis=0)
    centered = x - jnp.mean(x, axis=1, keepdims=True)
    scaling = lax.rsqrt(jnp.mean(centered * centered, axis=1, keepdims=True) + EPSILON)
    r.normed[...] = centered * scaling
    r.rescale[...] = jnp.broadcast_to(scaling[RIM : RIM + tokens], (tokens, LANES))


def modulate(r, segment, wide_segment):
    tokens, model = r.hidden.shape
    seqs = r.condition.shape[0]
    for c in range(model // LANES):
        lanes = slice(c * LANES, (c + 1) * LANES)

        def rows_for(part, segs):
            total = jnp.zeros(segs.shape, F32)
            at = part * model + c * LANES
            bias = r.b_mod[at // LANES : at // LANES + 1, :]
            for j in range(seqs):
                row = r.modulation[j : j + 1, at : at + LANES] + bias
                total = jnp.where(segs == j, row, total)
            return total

        one_scale = 1.0 + rows_for(1, wide_segment)
        mixed_in = r.normed[:, lanes] * one_scale + rows_for(0, wide_segment)
        r.mixer[:, lanes] = mixed_in.astype(BF16)
        r.mixer_own[:, lanes] = mixed_in[RIM : RIM + tokens].astype(BF16)
        r.scale1[:, lanes] = one_scale[RIM : RIM + tokens]
        gate = rows_for(2, segment)
        r.gate_rows[:, lanes] = gate
        r.branch_grad[:, lanes] = (r.grad_out[:, lanes].astype(F32) * gate).astype(BF16)


def project(r):
    tokens, inner = r.seed.shape
    r.proj[...] = jnp.zeros_like(r.proj)

    def block(b, none):
        cols = pl.ds(pl.multiple_of(b * COLS, COLS), COLS)
        conv = dot(r.mixer[...], r.w_conv[:, cols]).astype(BF16)
        r.conv_keep[:, cols] = conv
        r.conv_wide[...] = conv.astype(F32)
        gate = dot(r.mixer_own[...], r.w_gate[:, cols])
        r.gate_branch[:, cols] = gate
        back = contract_cols(r.branch_grad[...], r.w_out[cols, :])
        r.gated_grad[:, cols] = back
        r.seed[:, cols] = back * (gate * sigmoid(gate))
        convolve(r, 0, b)
        return none

    lax.fori_loop(0, inner // COLS, block, 0)


def convolve(r, d, b):
    tokens, inner = r.seed.shape
    taps = r.conv_w.shape[1]
    cols = pl.ds(pl.multiple_of(b * COLS, COLS), COLS)
    acts = []
    for c in range(COLS // LANES):
        lanes = tile_at(b * COLS + c * LANES)
        here = slice(c * LANES, (c + 1) * LANES)
        total = jnp.broadcast_to(r.conv_b[d : d + 1, lanes], (tokens, LANES))
        for k in range(taps):
            offset = offset_of(d, k, taps)
            tap = r.conv_wide[RIM + offset : RIM + offset + tokens, here]
            if offset:
                tap = tap * r.masks[offset + taps - 1]
            total = total + r.conv_w[d, k : k + 1, lanes] * tap
        sigma = sigmoid(total)
        r.conv_slope[d, :, lanes] = (sigma * (1.0 + total * (1.0 - sigma))).astype(BF16)
        act = (total * sigma).astype(BF16)
        r.active[d, :, lanes] = act
        acts.append(act)
    r.proj[d] += contract_cols(jnp.concatenate(acts, axis=1), r.w_x[d, :, cols])


def convolve_reverse(r):
    inner = r.seed.shape[1]

    def block(b, none):
        cols = pl.ds(pl.multiple_of(b * COLS, COLS), COLS)
        r.conv_wide[...] = r.conv_keep[:, cols].astype(F32)
        convolve(r, 1, b)
        return none

    lax.fori_loop(0, inner // COLS, block, 0)


def coefficients(r, d):
    tokens = r.seed.shape[0]
    rank = r.w_dt.shape[1]
    states = r.rate.shape[1]
    place = lax.rem(lax.broadcasted_iota(jnp.int32, (tokens, CHUNK * states), 0), CHUNK)
    owner = lax.broadcasted_iota(jnp.int32, (tokens, CHUNK * states), 1) // states
    on_diag = place == owner
    column = lax.rem(lax.broadcasted_iota(jnp.int32, (states, CHUNK * states), 1), states)
    repeat = (column == lax.broadcasted_iota(jnp.int32, (states, CHUNK * states), 0)).astype(BF16)
    whole = r.proj[d]
    r.rank_low[d] = whole[:, :rank].astype(BF16)
    flipped = whole.T
    for start, blk, spread in (
        (rank, r.in_blk, r.in_spread),
        (rank + states, r.out_blk, r.out_spread),
    ):
        coef = whole[:, start : start + states].astype(BF16)
        blk[d] = jnp.where(on_diag, dot(coef, repeat), 0.0).astype(BF16)
        rows = flipped[start : start + states, :]
        for t in range(tokens):
            spread[d, t * states : (t + 1) * states, :] = jnp.broadcast_to(
                rows[:, t : t + 1], (states, LANES)
            )


def step_logits(r, d, cols):
    return dot(r.rank_low[d], r.w_dt[d, :, cols]) + r.dt_bias[d : d + 1, cols]


def stepping(r, d):
    inner = r.seed.shape[1]
    taps = r.conv_w.shape[1]

    def block(b, none):
        cols = pl.ds(pl.multiple_of(b * COLS, COLS), COLS)
        step = softplus(step_logits(r, d, cols))
        keep = r.masks[taps - 2] if d == 0 else r.masks[taps]
        keep = jnp.concatenate([keep] * (COLS // LANES), axis=1)
        r.masked[d, :, cols] = jnp.where(keep > 0.5, step, CUT_STEP)
        r.driven[d, :, cols] = step * r.active[d, :, cols].astype(F32)
        return none

    lax.fori_loop(0, inner // COLS, block, 0)


def state_rows(ref, d, first, j, states):
    return ref[d, pl.ds(pl.multiple_of((first + j) * states, states), states), :]


def summarise(r, d, begin, end):
    tokens, inner = r.seed.shape
    states = r.rate.shape[1]
    tiles = inner // LANES
    per = SCAN // LANES

    def block(b, none):
        lanes = [tile_at(b * SCAN + c * LANES) for c in range(per)]

        def group(i, carry):
            carry = list(carry)
            start = pl.multiple_of((i if d == 0 else tokens // 8 - 1 - i) * 8, 8)
            for k in range(8):
                j = k if d == 0 else 7 - k
                in_row = state_rows(r.in_spread, d, start, j, states)
                out_row = state_rows(r.out_spread, d, start, j, states)
                for c in range(per):
                    state, decay, adj = carry[c]
                    now = jnp.exp2(
                        row_of(r.masked.at[d], start, j, lanes[c]) * r.rate[d, :, lanes[c]]
                    )
                    state = now * state + in_row * row_of(r.driven.at[d], start, j, lanes[c])
                    decay = decay * now
                    adj = adj + decay * (out_row * row_of(r.seed, start, j, lanes[c]))
                    carry[c] = (state, decay, adj)
            return tuple(carry)

        zero = jnp.zeros((states, LANES), F32)
        one = jnp.ones((states, LANES), F32)
        carry = lax.fori_loop(0, tokens // 8, group, tuple((zero, one, zero) for _ in range(per)))
        for c in range(per):
            state, decay, adj = carry[c]
            down, up = (adj, state) if d == 0 else (state, adj)
            at = d * tiles + b * per + c
            r.sums[at, 0] = down.astype(BF16)
            r.sums[at, 1] = three_pieces(
                jnp.sum(r.masked[d, :, lanes[c]], axis=0, keepdims=True), states
            )
            r.sums[at, 2] = up.astype(BF16)
        return none

    lax.fori_loop(begin, end, block, 0)


def three_pieces(row, states):
    high = row.astype(BF16).astype(F32)
    middle = (row - high).astype(BF16).astype(F32)
    lowest = row - high - middle
    at = lax.broadcasted_iota(jnp.int32, (states, row.shape[-1]), 0)
    return jnp.where(
        at == 0, high, jnp.where(at == 1, middle, jnp.where(at == 2, lowest, 0.0))
    ).astype(BF16)


def remote(src, dst, sems, slot, peer, there=None):
    return pltpu.make_async_remote_copy(
        src_ref=src,
        dst_ref=dst,
        send_sem=sems[0].at[slot],
        recv_sem=sems[1].at[slot if there is None else there],
        device_id=(peer,),
        device_id_type=MESH,
    )


class Place:
    def __init__(self, count):
        self.count = count
        self.groups = count // PLANE
        self.me = lax.axis_index("seq")
        self.bits = [lax.rem(self.me, 2), lax.rem(self.me // 2, 2), lax.rem(self.me // 4, 2)]
        self.flips = [self.me + (1 - 2 * self.bits[i]) * (1 << i) for i in range(3)]
        self.level = self.me // PLANE
        self.low = lax.rem(self.me, PLANE)
        self.left = lax.rem(self.me + count - 1, count)
        self.right = lax.rem(self.me + 1, count)
        self.far = [lax.rem(self.level + k, self.groups) for k in range(1, self.groups)]

    def peers(self):
        base = self.level * PLANE
        peers = [base + lax.rem(self.low + k, PLANE) for k in range(1, PLANE)]
        return peers + [self.left, self.right] + [g * PLANE + self.low for g in self.far]


def add_into(into, own, first):
    def one(i, none):
        into[i] = into[i] + own[first + i]
        return none

    lax.fori_loop(0, into.shape[0], one, 0)


class Carries:
    def __init__(self, r, place, sems):
        self.r, self.place, self.sems = r, place, sems
        self.mine = place.low
        self.base = place.level * PLANE
        self.share = r.sums.shape[0] // PLANE

    def rows(self, j):
        return pl.ds(j * self.share, self.share)

    def combiners(self, d):
        return range(d * PLANE // 2, (d + 1) * PLANE // 2)

    def combines(self, d):
        return self.mine // (PLANE // 2) == d

    def out(self, j):
        r = self.r
        src, dst = r.sums.at[self.rows(j)], r.got.at[self.mine]
        return remote(src, dst, self.sems[0], j, self.base + j, self.mine)

    def arrival(self, s):
        r = self.r
        return remote(r.sums.at[self.rows(s)], r.got.at[s], self.sems[0], s, self.base + s)

    def back(self, j):
        r = self.r
        src, dst = r.back.at[j], r.entering.at[self.rows(self.mine)]
        return remote(src, dst, self.sems[2], j, self.base + j, self.mine)

    def entry(self, s):
        r = self.r
        return remote(
            r.back.at[s], r.entering.at[self.rows(s)], self.sems[2], s, self.base + s
        )

    def between(self):
        r, place = self.r, self.place
        copies = []
        for k, other in enumerate(place.far):
            start = jnp.where(other > place.level, 1, 0)
            src, dst = r.total.at[pl.ds(start, 2)], r.others.at[place.level]
            copies.append(remote(src, dst, self.sems[1], k, other * PLANE + self.mine))
        return copies

    def send(self, d):
        for j in self.combiners(d):

            @pl.when(self.mine != j)
            def _():
                self.out(j).start()

    def whole(self, pieces):
        pieces = pieces.astype(F32)
        return pieces[:, 0:1] + pieces[:, 1:2] + pieces[:, 2:3]

    def rates(self):
        r = self.r
        tiles = r.rate.shape[2] // LANES
        parts = []
        for c in range(self.share):
            at = self.mine * self.share + c
            parts.append(r.rate[at // tiles, :, tile_at(lax.rem(at, tiles) * LANES)][None])
        return jnp.concatenate(parts, axis=0)

    def combine(self, d):
        r = self.r

        @pl.when(self.combines(d))
        def _():
            mine, share = self.mine, self.share
            states = r.rate.shape[1]
            r.got[mine] = r.sums[self.rows(mine)]
            r.others[self.place.level] = jnp.zeros(r.others.shape[1:], BF16)
            for s in range(PLANE):

                @pl.when(mine != s)
                def _():
                    self.arrival(s).wait_recv()

            rates = self.rates()
            block = (share, states, LANES)
            up = jnp.zeros(block, F32)
            down = jnp.zeros(block, F32)
            time = jnp.zeros((share, 1, LANES), F32)
            for j in range(PLANE):
                now = self.whole(r.got[j, :, 1])
                up = jnp.exp2(rates * now) * up + r.got[j, :, 2].astype(F32)
                time = time + now
            for j in reversed(range(PLANE)):
                now = jnp.exp2(rates * self.whole(r.got[j, :, 1]))
                down = now * down + r.got[j, :, 0].astype(F32)
            r.total[0] = down.astype(BF16)
            for c in range(share):
                r.total[1, c] = three_pieces(time[c], states)
            r.total[2] = up.astype(BF16)
            for copy in self.between():
                copy.start()

    def spread(self, d):
        r = self.r

        @pl.when(self.combines(d))
        def _():
            mine, share, level = self.mine, self.share, self.place.level
            states = r.rate.shape[1]
            groups = self.place.groups
            for copy in self.between():
                copy.wait_recv()
            rates = self.rates()
            block = (share, states, LANES)
            up = jnp.zeros(block, F32)
            for g in range(groups):
                decay = jnp.exp2(rates * self.whole(r.others[g, 0]))
                up = jnp.where(g < level, decay * up + r.others[g, 1].astype(F32), up)
            down = jnp.zeros(block, F32)
            for g in reversed(range(groups)):
                decay = jnp.exp2(rates * self.whole(r.others[g, 1]))
                down = jnp.where(g > level, decay * down + r.others[g, 0].astype(F32), down)
            decays = [jnp.exp2(rates * self.whole(r.got[j, :, 1])) for j in range(PLANE)]
            for j in range(PLANE):
                r.back[j, :, 0] = up.astype(BF16)
                up = decays[j] * up + r.got[j, :, 2].astype(F32)
            for j in reversed(range(PLANE)):
                r.back[j, :, 1] = down.astype(BF16)
                down = decays[j] * down + r.got[j, :, 0].astype(F32)
            for j in range(PLANE):

                @pl.when(mine != j)
                def _():
                    self.back(j).start()

            r.entering[self.rows(mine)] = r.back[mine]

    def receive(self, d):
        for s in self.combiners(d):

            @pl.when(self.mine != s)
            def _():
                self.entry(s).wait_recv()

    def finish(self):
        for j in range(PLANE):

            @pl.when(self.mine != j)
            def _():
                self.out(j).wait_send()
                self.back(j).wait_send()

        for copy in self.between():
            copy.wait_send()


class Piece:
    def __init__(self, place, order, part, own, refs):
        self.place, self.order, self.part, self.own = place, order, part, own
        self.got1, self.got2, self.got3, self.got4 = refs[:4]
        self.sems = refs[4:]
        self.bits = [place.bits[0], place.bits[order[0]], place.bits[order[1]]]
        self.flips = [place.flips[0], place.flips[order[0]], place.flips[order[1]]]

    def hop(self, i):
        if i == 0:
            src = self.part.at[1 - self.bits[0]]
        else:
            half = 4 * self.place.groups >> i
            held = (self.got1, self.got2)[i - 1]
            src = held.at[pl.ds((1 - self.bits[i]) * half, half)]
        return remote(src, (self.got1, self.got2, self.got3)[i], self.sems, i, self.flips[i])

    def fan(self):
        return [
            remote(
                self.got3.at[g],
                self.got4.at[self.place.level],
                self.sems,
                3 + k,
                g * PLANE + self.place.low,
            )
            for k, g in enumerate(self.place.far)
        ]

    def step(self, i):
        groups = self.place.groups
        if i:
            self.hop(i - 1).wait_recv()
        if i == 1:
            add_into(self.got1, self.own, 0)
        elif i == 2:
            add_into(self.got2, self.got1, self.bits[1] * 2 * groups)
        elif i == 3:
            add_into(self.got3, self.got2, self.bits[2] * groups)
        if i < 3:
            self.hop(i).start()
            return
        for copy in self.fan():
            copy.start()
        self.got4[self.place.level] = self.got3[self.place.level]

    def end(self, share, begin):
        for copy in self.fan():
            copy.wait_recv()
        total = self.got4[0].astype(F32)
        for g in range(1, self.place.groups):
            total = total + self.got4[g].astype(F32)
        share[:, begin : begin + total.shape[1]] = total
        for copy in [self.hop(1), self.hop(2)] + self.fan():
            copy.wait_send()

    def release(self):
        self.hop(0).wait_send()


def piece_scratch(rows, cols, groups):
    return [
        pltpu.VMEM((size, rows, cols), BF16) for size in (4 * groups, 2 * groups, groups, groups)
    ] + [pltpu.SemaphoreType.DMA((2 + groups,))] * 2


def interleaved(chunks, compute, pieces, carry):
    jobs = []
    for i in range(chunks):
        carry = compute(i, i % 2, carry, jobs)
        jobs = pieces(i, i % 2)
    for job in jobs:
        job()
    return carry


def jobs_between(jobs, k):
    every = max(CHUNK // max(len(jobs), 1), 1)
    if jobs and k % every == 0 and k // every < len(jobs):
        jobs[k // every]()


def small_rows(taps):
    return 0, 2 * taps, 2 * taps + 2, 2 * taps + 4, 2 * taps + 8


def forward_scan(r, d):
    tokens, inner = r.seed.shape
    tiles = inner // LANES
    per = SCAN // LANES
    states = r.rate.shape[1]
    chunks = tokens // CHUNK
    rows = (r.rows0, r.rows1)

    def first_of(i):
        return (i if d == 0 else chunks - 1 - i) * CHUNK

    def block(b, none):
        cols = pl.ds(pl.multiple_of(b * SCAN, SCAN), SCAN)
        lanes = [tile_at(b * SCAN + c * LANES) for c in range(per)]
        edge = d * tokens * states
        for c in range(per):
            r.kept[edge : edge + states, lanes[c]] = r.entering[d * tiles + b * per + c, d]

        def compute(i, side, carry, jobs):
            carry = list(carry)
            first = first_of(i)
            for k in range(CHUNK):
                jobs_between(jobs, k)
                j = k if d == 0 else CHUNK - 1 - k
                in_row = state_rows(r.in_spread, d, first, j, states)
                for c in range(per):
                    now = jnp.exp2(
                        row_of(r.masked.at[d], first, j, lanes[c]) * r.rate[d, :, lanes[c]]
                    )
                    state = now * carry[c] + in_row * row_of(r.driven.at[d], first, j, lanes[c])
                    rows[side][
                        j * states : (j + 1) * states, c * LANES : (c + 1) * LANES
                    ] = state.astype(BF16)
                    carry[c] = state
            return tuple(carry)

        def pieces(i, side):
            here = pl.ds(first_of(i), CHUNK)

            def keep(q):
                half = CHUNK * states // 2
                slot = (first_of(i) + 1 - d) * states + q * half
                r.kept[slot : slot + half, cols] = rows[side][q * half : (q + 1) * half, :]

            def mix(q):
                part = pl.ds(pl.multiple_of(b * SCAN + q * COLS, COLS), COLS)
                mixed = dot(r.out_blk[d, here, :], rows[side][:, q * COLS : (q + 1) * COLS])
                if d == 0:
                    r.mixed[here, part] = mixed
                else:
                    r.mixed[here, part] += mixed

            def grad():
                r.out_acc[d, here, :] += contract_cols(
                    r.seed[here, cols].astype(BF16), rows[side][...]
                )

            return [
                functools.partial(mix, 0),
                functools.partial(keep, 0),
                functools.partial(mix, 1),
                functools.partial(keep, 1),
                grad,
            ]

        start = tuple(r.entering[d * tiles + b * per + c, d].astype(F32) for c in range(per))
        interleaved(chunks, compute, pieces, start)
        return none

    lax.fori_loop(0, inner // SCAN, block, 0)


def adjoint_scan(r, d, begin, end):
    tokens, inner = r.seed.shape
    tiles = inner // LANES
    per = SCAN // LANES
    states = r.rate.shape[1]
    taps = r.conv_w.shape[1]
    chunks = tokens // CHUNK
    wide = CHUNK * states
    adjs = (r.rows0, r.rows1)
    slopes = (r.slope0, r.slope1)
    ones = (
        lax.broadcasted_iota(jnp.int32, (CHUNK, wide), 1) // states
        == lax.broadcasted_iota(jnp.int32, (CHUNK, wide), 0)
    ).astype(BF16)

    def first_of(i):
        return (chunks - 1 - i if d == 0 else i) * CHUNK

    def block(b, none):
        cols = pl.ds(pl.multiple_of(b * SCAN, SCAN), SCAN)
        lanes = [tile_at(b * SCAN + c * LANES) for c in range(per)]
        low_rates = [r.rate[d, :, lanes[c]].astype(BF16) for c in range(per)]

        def compute(i, side, carry, jobs):
            carry = list(carry)
            first = first_of(i)
            for k in range(CHUNK):
                jobs_between(jobs, k)
                j = CHUNK - 1 - k if d == 0 else k
                slot = (first + j + d) * states
                out_row = state_rows(r.out_spread, d, first, j, states)
                part = slice(j * states, (j + 1) * states)
                for c in range(per):
                    here = slice(c * LANES, (c + 1) * LANES)
                    coming, total = carry[c]
                    step = row_of(r.masked.at[d], first, j, lanes[c])
                    now = jnp.exp2(step * r.rate[d, :, lanes[c]])
                    adj = out_row * row_of(r.seed, first, j, lanes[c]) + coming
                    coming = now * adj
                    slope = coming.astype(BF16) * r.kept[slot : slot + states, lanes[c]]
                    slope = slope * low_rates[c]
                    total = total + slope.astype(F32) * step
                    adjs[side][part, here] = adj.astype(BF16)
                    slopes[side][part, here] = slope
                    carry[c] = (coming, total)
            return tuple(carry)

        def pieces(i, side):
            here = pl.ds(first_of(i), CHUNK)

            def driven_side(q):
                part = pl.ds(pl.multiple_of(b * SCAN + q * COLS, COLS), COLS)
                r.driven_grad[d][here, part] = dot(
                    r.in_blk[d, here, :], adjs[side][:, q * COLS : (q + 1) * COLS]
                )

            def decay_side(q):
                part = pl.ds(pl.multiple_of(b * SCAN + q * COLS, COLS), COLS)
                r.decay_grad[d][here, part] = (
                    dot(ones, slopes[side][:, q * COLS : (q + 1) * COLS]) * LN2
                )

            def in_side():
                r.in_acc[d, here, :] += contract_cols(
                    r.driven[d, here, cols].astype(BF16), adjs[side][...]
                )

            return [
                functools.partial(driven_side, 0),
                functools.partial(decay_side, 0),
                in_side,
                functools.partial(driven_side, 1),
                functools.partial(decay_side, 1),
            ]

        zero = jnp.zeros((states, LANES), F32)
        start = tuple(
            (r.entering[d * tiles + b * per + c, 1 - d].astype(F32), zero) for c in range(per)
        )
        carry = interleaved(chunks, compute, pieces, start)
        at_rate = small_rows(taps)[4]
        for c in range(per):
            r.small[at_rate + d * states : at_rate + (d + 1) * states, lanes[c]] = (
                carry[c][1] * LN2
            )
        return none

    lax.fori_loop(begin, end, block, 0)


def output_half(r, count, half):
    tokens, inner = r.mixed.shape
    model = r.hidden.shape[1]
    begin = half * inner // COLS // 2

    def block(b, none):
        cols = pl.ds(pl.multiple_of(b * COLS, COLS), COLS)
        mixed = r.mixed[:, cols]
        for d in range(2):
            mixed = mixed + r.d_skip[d : d + 1, cols] * r.active[d, :, cols].astype(F32)
        gate = r.gate_branch[:, cols]
        sigma = sigmoid(gate)
        now = (mixed * (gate * sigma)).astype(BF16)
        r.gated[:, cols] = now
        slope = sigma * (1.0 + gate * (1.0 - sigma))
        back = (r.gated_grad[:, cols] * mixed * slope).astype(BF16)
        r.gate_branch_grad[:, cols] = back
        r.branch[...] += dot(now, r.w_out[cols, :])
        here = pl.ds(pl.multiple_of((b - begin) * COLS, COLS), COLS)
        r.whole[:, here] = contract_rows(r.mixer_own[...], back)
        return none

    lax.fori_loop(begin, begin + inner // COLS // 2, block, 0)
    part = (r.gate0, r.gate1)[half]
    for o in range(count):
        first, later = slot_of(o, count, (XY, YX)[half])
        part[first, later] = stacked_rows(
            r.whole, r.stage, o, model // count, 0, model
        ).astype(BF16)


def output_weights(r, count):
    tokens, inner = r.mixed.shape
    model = r.hidden.shape[1]
    rows = inner // count
    half = model // 2
    chunk = inner // 8
    per = count // 8
    for q in range(8):
        r.whole[0:chunk, :] = contract_rows(
            r.gated[:, q * chunk : (q + 1) * chunk], r.branch_grad[...]
        )
        for i in range(per):
            low = r.whole[i * rows : (i + 1) * rows, :].astype(BF16)
            first, later = slot_of(q * per + i, count, XY)
            r.out0[first, later, 0:rows] = low[:, :half]
            first, later = slot_of(q * per + i, count, YX)
            r.out1[first, later, 0:rows] = low[:, half:]


def column_sum(values):
    return jnp.sum(values, axis=0, keepdims=True)


def through_steps(r):
    tokens, inner = r.seed.shape
    taps = r.conv_w.shape[1]
    rank = r.w_dt.shape[1]
    proj = r.w_x.shape[1]
    states = r.rate.shape[1]
    _, _, at_dt, at_skip, _ = small_rows(taps)
    r.rank_grad[...] = jnp.zeros_like(r.rank_grad)

    def block(b, none):
        cols = pl.ds(pl.multiple_of(b * COLS, COLS), COLS)
        for d in range(2):
            act = r.active[d, :, cols].astype(F32)
            value = step_logits(r, d, cols)
            back = r.driven_grad[d][:, cols]
            grown = r.seed[:, cols]
            grad = (r.decay_grad[d][:, cols] + back * act) * sigmoid(value)
            low = grad.astype(BF16)
            r.driven_grad[d][:, cols] = (
                back * softplus(value) + grown * r.d_skip[d : d + 1, cols]
            )
            r.small[at_dt + d : at_dt + d + 1, cols] = column_sum(grad)
            r.small[at_skip + d : at_skip + d + 1, cols] = column_sum(grown * act)
            r.rank_grad[d] += contract_cols(low, r.w_dt[d, :, cols])
            r.in_spread[d, cols, proj : proj + rank] = contract_rows(low, r.rank_low[d])
        return none

    lax.fori_loop(0, inner // COLS, block, 0)

    place = lax.rem(lax.broadcasted_iota(jnp.int32, (tokens, CHUNK * states), 0), CHUNK)
    owner = lax.broadcasted_iota(jnp.int32, (tokens, CHUNK * states), 1) // states
    on_diag = place == owner
    column = lax.rem(lax.broadcasted_iota(jnp.int32, (CHUNK * states, states), 0), states)
    gather = (column == lax.broadcasted_iota(jnp.int32, (CHUNK * states, states), 1)).astype(BF16)
    for d in range(2):
        r.proj_grad[d, :, 0:rank] = r.rank_grad[d].astype(BF16)
        for start, acc in ((rank, r.in_acc), (rank + states, r.out_acc)):
            kept = jnp.where(on_diag, acc[d], 0.0).astype(BF16)
            r.proj_grad[d, :, start : start + states] = dot(kept, gather).astype(BF16)

    def weights(b, none):
        cols = pl.ds(pl.multiple_of(b * COLS, COLS), COLS)
        for d in range(2):
            r.in_spread[d, cols, 0:proj] = contract_rows(r.active[d, :, cols], r.proj_grad[d])
        return none

    lax.fori_loop(0, inner // COLS, weights, 0)


def through_conv(r, begin, end):
    tokens, inner = r.seed.shape
    taps = r.conv_w.shape[1]
    at_conv, at_bias, _, _, _ = small_rows(taps)

    def block(b, none):
        cols = pl.ds(pl.multiple_of(b * COLS, COLS), COLS)
        r.conv_wide[...] = r.conv_keep[:, cols].astype(F32)
        r.input_wide[...] = jnp.zeros_like(r.input_wide)
        for d in range(2):
            total = r.driven_grad[d][:, cols] + dot(r.proj_grad[d], r.w_x[d, :, cols])
            for c in range(COLS // LANES):
                lanes = tile_at(b * COLS + c * LANES)
                here = slice(c * LANES, (c + 1) * LANES)
                grad = total[:, here] * r.conv_slope[d, :, lanes].astype(F32)
                r.small[at_bias + d : at_bias + d + 1, lanes] = column_sum(grad)
                for k in range(taps):
                    offset = offset_of(d, k, taps)
                    window = slice(RIM + offset, RIM + offset + tokens)
                    part = grad * r.masks[offset + taps - 1] if offset else grad
                    at = at_conv + d * taps + k
                    r.small[at : at + 1, lanes] = column_sum(part * r.conv_wide[window, here])
                    r.input_wide[window, here] += r.conv_w[d, k : k + 1, lanes] * part
        low = r.input_wide[...].astype(BF16)
        here = pl.ds(pl.multiple_of((b - begin) * COLS, COLS), COLS)
        r.whole[:, here] = contract_rows(r.mixer[...], low)
        r.norm_wide[...] += contract_cols(low, r.w_conv[:, cols])
        r.norm_wide[RIM : RIM + tokens, :] += contract_cols(
            r.gate_branch_grad[:, cols], r.w_gate[:, cols]
        )
        r.small_cols[cols, :] = r.small[:, cols].T
        return none

    lax.fori_loop(begin, end, block, 0)


def fill_columns(r, part, count):
    rows = r.seed.shape[1] // count
    for o in range(count):
        first, later = slot_of(o, count, XY)
        for d in range(2):
            part[first, later, 0:rows, d * LANES : (d + 1) * LANES] = r.in_spread[
                d, o * rows : (o + 1) * rows, :
            ].astype(BF16)


def fill_conv(r, parts, count):
    inner = r.seed.shape[1]
    model = r.normed.shape[1]
    rows, mrows = inner // count, model // count
    for o in range(count):
        both = stacked_rows(r.whole, r.stage, o, mrows, 0, model).astype(BF16)
        if len(parts) == 1:
            first, later = slot_of(o, count, YX)
            parts[0][first, later] = both
            continue
        cut = parts[0].shape[3]
        rest = model // 2 - cut
        first, later = slot_of(o, count, XY)
        parts[0][first, later] = both[:, :cut]
        first, later = slot_of(o, count, YX)
        parts[1][first, later, :, 0:rest] = both[:, cut:]
        parts[1][first, later, 0:rows, rest:] = r.small_cols[o * rows : (o + 1) * rows, :].astype(
            BF16
        )


def modulation_shares(r, place):
    seqs, model = r.condition.shape
    mrows = r.w_mod_share.shape[0]
    width = r.b_mod_share.shape[1]

    def picked(total, number):
        source = lax.broadcasted_iota(jnp.int32, (total, number), 0)
        return source == place.me * number + lax.broadcasted_iota(jnp.int32, (total, number), 1)

    cond = r.condition[...]
    cond_act = (cond * sigmoid(cond)).astype(BF16)
    my_cond = dot(cond_act, picked(model, mrows).astype(BF16)).astype(BF16)
    totals = r.mod[...].astype(BF16)
    r.w_mod_share[...] = contract_rows(my_cond, totals[0:seqs])
    mine = dot(totals, picked(3 * model, width).astype(BF16))
    r.b_mod_share[...] = jnp.sum(mine[0:seqs], axis=0, keepdims=True)


def input_gradient(r, place):
    tokens, model = r.hidden.shape
    norm_grad = r.norm_wide[RIM : RIM + tokens, :]
    low = jnp.where(place.me > 0, r.edge_got[0:RIM, :], 0.0)
    high = jnp.where(place.me < place.count - 1, r.edge_got[RIM:, :], 0.0)
    middle = jnp.zeros((tokens - 2 * RIM, model), F32)
    norm_grad = norm_grad + jnp.concatenate([low, middle, high], axis=0)
    scaled = norm_grad * r.scale1[...]
    normal = r.normed[RIM : RIM + tokens, :]
    r.grad_x[...] = r.grad_out[...].astype(F32) + r.rescale[:, 0:1] * (
        scaled
        - jnp.mean(scaled, axis=1, keepdims=True)
        - normal * jnp.mean(scaled * normal, axis=1, keepdims=True)
    )


def modulation_sums(r):
    tokens = r.seed.shape[0]
    model = r.normed.shape[1]
    seqs = r.mod_part.shape[1]
    half = r.mod_part.shape[2]
    seq_rows = r.hot[:, 0:seqs]
    grads = r.norm_wide[...]
    sums = [
        contract_rows(seq_rows, grads, HIGHEST),
        contract_rows(seq_rows, grads * r.normed[...], HIGHEST),
        contract_rows(r.hot[RIM : RIM + tokens, 0:seqs], r.branch[...], HIGHEST),
    ]
    whole = jnp.concatenate(sums, axis=1)
    r.mod_part[0] = whole[:, :half].astype(BF16)
    r.mod_part[1] = whole[:, half:].astype(BF16)


class ModSums:
    def __init__(self, place, r, sems):
        self.place, self.r, self.sems = place, r, sems
        self.core = place.bits[0]
        self.chip = place.bits[1] + 2 * place.bits[2]

    def copies(self, i):
        place, r, sems = self.place, self.r, self.sems
        if i == 0:
            return [remote(r.mod_part.at[1 - self.core], r.m1, sems, 0, place.flips[0])]
        if i == 1:
            peers = (place.flips[1], place.flips[2], place.flips[1] + place.flips[2] - place.me)
            return [
                remote(r.m1, r.m2.at[self.chip], sems, 1 + k, peer) for k, peer in enumerate(peers)
            ]
        if i == 2:
            return [
                remote(r.m1, r.m3.at[place.level], sems, 4 + k, g * PLANE + place.low)
                for k, g in enumerate(place.far)
            ]
        slot = 4 + len(place.far)
        return [
            remote(r.m4.at[self.core], r.m4.at[self.core], sems, slot, place.flips[0])
        ]

    def total(self, ref, number):
        total = ref[0].astype(F32)
        for g in range(1, number):
            total = total + ref[g].astype(F32)
        return total.astype(BF16)

    def step(self, i):
        place, r = self.place, self.r
        if i:
            for copy in self.copies(i - 1):
                copy.wait_recv()
        if i == 1:
            r.m1[...] = r.m1[...] + r.mod_part[self.core]
            r.m2[self.chip] = r.m1[...]
        elif i == 2:
            for copy in self.copies(1):
                copy.wait_send()
            summed = self.total(r.m2, 4)
            r.m1[...] = summed
            r.m3[place.level] = summed
        elif i == 3:
            r.m4[self.core] = self.total(r.m3, place.groups)
        for copy in self.copies(i):
            copy.start()

    def end(self, mod):
        half = mod.shape[1] // 2
        self.copies(3)[0].wait_recv()
        for c in range(2):
            mod[:, c * half : (c + 1) * half] = self.r.m4[c].astype(F32)[0 : mod.shape[0]]
        for i in (0, 2, 3):
            for copy in self.copies(i):
                copy.wait_send()


def late_columns(model, proj, rank, taps, states):
    first = proj + rank
    small = 2 * taps + 8 + 2 * states
    half = model // 2
    cut = half // 2 // LANES * LANES + LANES
    return 2 * (first + -first % LANES), half, cut, half - cut + small + -small % LANES


def block_kernel(count, names, lates, *refs):
    refs = list(refs)

    def take(size):
        taken = refs[:size]
        del refs[:size]
        return taken

    in_names, weight_names, out_names, scratch_names = names
    given = take(len(in_names))
    weights_any = take(5)
    outs = take(len(out_names))
    weights = take(len(weight_names))
    scratch = take(len(scratch_names))
    piece_refs = [take(6) for _ in range(8)]
    carry_sems = [take(2) for _ in range(3)]
    mod_sems, edge_sems, halo_sems = take(2), take(2), take(2)
    (load_sems,) = take(1)
    r = Refs(
        in_names + weight_names + out_names + scratch_names, given + weights + outs + scratch
    )
    tokens, inner = r.seed.shape
    blocks = inner // COLS
    scans = inner // SCAN
    r.decay_grad = (r.decay0, r.gate_branch)
    r.driven_grad = (r.driven0, r.gated_grad)

    w_mod_any, w_in_any, w_out_any, w_x_any, w_dt_any = weights_any
    model = r.hidden.shape[1]
    low_mod = r.kept.at[pl.ds(0, model), pl.ds(0, 2 * model)]
    high_mod = r.kept.at[pl.ds(model, model), pl.ds(0, model)]
    sources = (
        w_mod_any.at[:, pl.ds(0, 2 * model)],
        w_mod_any.at[:, pl.ds(2 * model, model)],
        w_in_any.at[:, pl.ds(0, inner)],
        w_in_any.at[:, pl.ds(inner, inner)],
        w_out_any,
        w_x_any,
        w_dt_any,
    )
    loads = [
        pltpu.make_async_copy(src, dst, load_sems.at[i])
        for i, (src, dst) in enumerate(zip(sources, [low_mod, high_mod] + weights))
    ]
    for load in loads:
        load.start()

    place = Place(count)
    barrier = pltpu.get_barrier_semaphore()
    peers = place.peers()
    for peer in peers:
        pl.semaphore_signal(barrier, inc=1, device_id=(peer,), device_id_type=MESH)
    me, core = place.me, place.bits[0]
    carries = Carries(r, place, carry_sems)
    views = (
        r.gate1.at[:, :, :, pl.ds(0, lates[0])],
        r.gate0,
        r.out0.at[:, :, :, pl.ds(0, lates[2])],
        r.out1.at[:, :, :, pl.ds(0, lates[3])],
    )
    parts = (r.gate0, r.gate1, r.out0, r.out1) + views
    pieces = [
        Piece(place, (XY, YX)[p % 2], part, part.at[core], piece_refs[p])
        for p, part in enumerate(parts)
    ]
    early, late = pieces[:4], pieces[4:]

    segment, wide_segment = token_masks(r, me * tokens)
    r.rate[...] = -jnp.exp(r.a_log[...]) * LOG2E
    r.out_acc[...] = jnp.zeros_like(r.out_acc)
    r.in_acc[...] = jnp.zeros_like(r.in_acc)
    r.small[...] = jnp.zeros_like(r.small)
    r.branch[...] = jnp.zeros_like(r.branch)
    r.norm_wide[...] = jnp.zeros_like(r.norm_wide)
    pl.semaphore_wait(barrier, len(peers))
    halos = [
        remote(r.hidden.at[pl.ds(tokens - 16, 16)], r.below, halo_sems, 0, place.right),
        remote(r.hidden.at[pl.ds(0, 16)], r.above, halo_sems, 1, place.left),
    ]
    for halo in halos:
        halo.start()
    cond = r.condition[...]
    cond_act = (cond * sigmoid(cond)).astype(BF16)
    loads[0].wait()
    loads[1].wait()
    seqs = cond.shape[0]
    r.modulation[0:seqs, 0 : 2 * model] = dot(cond_act, low_mod[...])
    r.modulation[0:seqs, 2 * model :] = dot(cond_act, high_mod[...])
    for halo in halos:
        halo.wait_recv()
    below = jnp.where(me > 0, r.below[...].astype(F32), 0.0)[16 - RIM :]
    above = jnp.where(me < count - 1, r.above[...].astype(F32), 0.0)[:RIM]
    normalise(r, below, above)
    modulate(r, segment, wide_segment)
    for load in loads[2:]:
        load.wait()
    project(r)
    coefficients(r, 0)
    stepping(r, 0)

    summarise(r, 0, 0, scans)
    carries.send(0)
    convolve_reverse(r)
    coefficients(r, 1)
    stepping(r, 1)
    carries.combine(0)
    summarise(r, 1, 0, scans - 1)
    carries.spread(0)
    summarise(r, 1, scans - 1, scans)
    carries.send(1)
    carries.receive(0)
    forward_scan(r, 0)
    carries.combine(1)
    adjoint_scan(r, 0, 0, scans - 1)
    carries.spread(1)
    adjoint_scan(r, 0, scans - 1, scans)
    carries.receive(1)
    forward_scan(r, 1)

    output_half(r, count, 0)
    early[0].step(0)
    output_half(r, count, 1)
    early[1].step(0)
    output_weights(r, count)
    early[2].step(0)
    early[3].step(0)
    r.output[...] = (r.hidden[...].astype(F32) + r.gate_rows[...] * r.branch[...]).astype(BF16)
    r.branch[...] = r.grad_out[...].astype(F32) * r.branch[...]
    early[0].step(1)
    early[1].step(1)
    adjoint_scan(r, 1, 0, 1)
    early[2].step(1)
    early[3].step(1)
    adjoint_scan(r, 1, 1, scans)
    through_steps(r)
    early[0].step(2)
    early[1].step(2)
    for piece in early:
        piece.release()
    fill_columns(r, views[0], count)
    late[0].step(0)
    through_conv(r, 0, blocks // 2)
    early[2].step(2)
    early[3].step(2)
    fill_conv(r, views[1:2], count)
    late[1].step(0)
    late[0].step(1)
    early[0].step(3)
    early[1].step(3)
    through_conv(r, blocks // 2, blocks)
    late[1].step(1)
    modulation_sums(r)
    mods = ModSums(place, r, mod_sems)
    mods.step(0)
    fill_conv(r, views[2:], count)
    late[2].step(0)
    late[3].step(0)
    late[2].step(1)
    late[3].step(1)
    mods.step(1)
    edges = [
        remote(
            r.norm_wide.at[pl.ds(0, RIM)],
            r.edge_got.at[pl.ds(RIM, RIM)],
            edge_sems,
            0,
            place.left,
        ),
        remote(
            r.norm_wide.at[pl.ds(r.norm_wide.shape[0] - RIM, RIM)],
            r.edge_got.at[pl.ds(0, RIM)],
            edge_sems,
            1,
            place.right,
        ),
    ]
    for copy in edges:
        copy.start()
    early[2].step(3)
    early[3].step(3)
    late[0].step(2)
    late[1].step(2)
    mods.step(2)
    late[2].step(2)
    late[3].step(2)
    late[0].step(3)
    late[1].step(3)
    mods.step(3)
    for copy in edges:
        copy.wait_recv()
    input_gradient(r, place)
    late[2].step(3)
    late[3].step(3)
    width = r.share_early.shape[1] // 4
    for p, at in enumerate((2, 3, 0, 1)):
        early[p].end(r.share_early, at * width)
    mods.end(r.mod)
    modulation_shares(r, place)
    begin = 0
    for piece, view in zip(late, views):
        piece.end(r.share_late, begin)
        piece.release()
        begin += view.shape[3]
    carries.finish()
    for copy in edges + halos:
        copy.wait_send()


def run_block(count, given, weights):
    w_mod, w_in, w_out, w_x, w_dt = weights
    tokens, model = given.hidden.shape
    inner = w_in.shape[1] // 2
    rank = w_dt.shape[1]
    proj = w_x.shape[1]
    states = given.a_log.shape[1]
    taps = given.conv_w.shape[1]
    groups = count // PLANE
    wide = tokens + 2 * RIM
    tiles = inner // LANES
    share = 2 * tiles // PLANE
    rows = slot_rows(count, inner)
    lates = late_columns(model, proj, rank, taps, states)
    small = lates[3] - (model // 2 - lates[2])
    both = (2, tokens, inner)
    spread = (2, tokens * states, LANES)
    diag = (2, tokens, CHUNK * states)
    mod = (8, 3 * model)
    half_mod = (16, 3 * model // 2)
    slots = pltpu.VMEM((2, count // 2, rows, model // 2), BF16)
    buffer = pltpu.VMEM((CHUNK * states, SCAN), BF16)
    full = pltpu.VMEM((tokens, inner), F32)
    outs = dict(
        output=shaped((tokens, model), BF16),
        grad_x=shaped((tokens, model)),
        w_mod_share=shaped((model // count, 3 * model)),
        b_mod_share=shaped((1, 3 * model // count)),
        share_early=shaped((rows, 2 * model)),
        share_late=shaped((rows, sum(lates))),
    )
    held = dict(
        w_conv=pltpu.VMEM((model, inner), BF16),
        w_gate=pltpu.VMEM((model, inner), BF16),
        w_out=pltpu.VMEM(w_out.shape, BF16),
        w_x=pltpu.VMEM(w_x.shape, BF16),
        w_dt=pltpu.VMEM(w_dt.shape, BF16),
    )
    scratch = dict(
        mixer=pltpu.VMEM((wide, model), BF16),
        mixer_own=pltpu.VMEM((tokens, model), BF16),
        normed=pltpu.VMEM((wide, model), F32),
        rescale=pltpu.VMEM((tokens, LANES), F32),
        scale1=pltpu.VMEM((tokens, model), F32),
        gate_rows=pltpu.VMEM((tokens, model), F32),
        branch_grad=pltpu.VMEM((tokens, model), BF16),
        conv_keep=pltpu.VMEM((wide, inner), BF16),
        conv_wide=pltpu.VMEM((wide, COLS), F32),
        conv_slope=pltpu.VMEM(both, BF16),
        active=pltpu.VMEM(both, BF16),
        gate_branch=full,
        gated_grad=full,
        seed=full,
        proj=pltpu.VMEM((2, tokens, proj), F32),
        rank_low=pltpu.VMEM((2, tokens, rank), BF16),
        masked=pltpu.VMEM(both, F32),
        driven=pltpu.VMEM(both, F32),
        in_spread=pltpu.VMEM(spread, F32),
        out_spread=pltpu.VMEM(spread, F32),
        in_blk=pltpu.VMEM(diag, BF16),
        out_blk=pltpu.VMEM(diag, BF16),
        rate=pltpu.VMEM((2, states, inner), F32),
        masks=pltpu.VMEM((2 * taps - 1, tokens, LANES), F32),
        hot=pltpu.VMEM((wide, LANES), F32),
        below=pltpu.VMEM((16, model), BF16),
        above=pltpu.VMEM((16, model), BF16),
        modulation=pltpu.VMEM((8, w_mod.shape[1]), F32),
        sums=pltpu.VMEM((2 * tiles, 3, states, LANES), BF16),
        got=pltpu.VMEM((PLANE, share, 3, states, LANES), BF16),
        total=pltpu.VMEM((3, share, states, LANES), BF16),
        others=pltpu.VMEM((groups, 2, share, states, LANES), BF16),
        back=pltpu.VMEM((PLANE, share, 2, states, LANES), BF16),
        entering=pltpu.VMEM((2 * tiles, 2, states, LANES), BF16),
        kept=pltpu.VMEM(((tokens + 1) * states, inner), BF16),
        rows0=buffer,
        rows1=buffer,
        slope0=buffer,
        slope1=buffer,
        mixed=full,
        decay0=full,
        driven0=full,
        out_acc=pltpu.VMEM(diag, F32),
        in_acc=pltpu.VMEM(diag, F32),
        gated=pltpu.VMEM((tokens, inner), BF16),
        gate_branch_grad=pltpu.VMEM((tokens, inner), BF16),
        branch=pltpu.VMEM((tokens, model), F32),
        whole=pltpu.VMEM((model, inner // 2), F32),
        stage=pltpu.VMEM((rows, model // 2), F32),
        gate0=slots,
        gate1=slots,
        out0=slots,
        out1=slots,
        small=pltpu.VMEM((small, inner), F32),
        rank_grad=pltpu.VMEM((2, tokens, rank), F32),
        proj_grad=pltpu.VMEM((2, tokens, proj), BF16),
        input_wide=pltpu.VMEM((wide, COLS), F32),
        small_cols=pltpu.VMEM((inner, small), F32),
        norm_wide=pltpu.VMEM((wide, model), F32),
        mod_part=pltpu.VMEM((2,) + half_mod, BF16),
        m1=pltpu.VMEM(half_mod, BF16),
        m2=pltpu.VMEM((4,) + half_mod, BF16),
        m3=pltpu.VMEM((groups,) + half_mod, BF16),
        m4=pltpu.VMEM((2,) + half_mod, BF16),
        mod=pltpu.VMEM(mod, F32),
        edge_got=pltpu.VMEM((2 * RIM, model), F32),
    )
    sems = pltpu.SemaphoreType.DMA
    pieces = []
    for cols in (model // 2,) * 4 + lates:
        pieces += piece_scratch(rows, cols, groups)
    given = vars(given)
    names = tuple(tuple(part) for part in (given, held, outs, scratch))
    return pl.pallas_call(
        functools.partial(block_kernel, count, names, lates),
        in_specs=[pl.BlockSpec(memory_space=pltpu.SMEM)] + [VMEM] * (len(given) - 1) + [ANY] * 5,
        out_specs=[VMEM] * len(outs),
        out_shape=list(outs.values()),
        scratch_shapes=list(held.values())
        + list(scratch.values())
        + pieces
        + [sems((PLANE,))] * 2
        + [sems((groups,))] * 2
        + [sems((PLANE,))] * 2
        + [sems((6 + groups,))] * 2
        + [sems((2,))] * 4
        + [sems((len(held) + 2,))],
        compiler_params=pltpu.CompilerParams(
            collective_id=0, has_side_effects=True, vmem_limit_bytes=63 * MIB
        ),
        name="block",
    )(*given.values(), *weights)


def finish_kernel(
    count,
    proj,
    rank,
    taps,
    states,
    share_early,
    share_late,
    made,
    made_grad,
    made_w_mod,
    made_b_mod,
    output,
    grad_x,
    w_mod,
    b_mod,
    w_in,
    conv_w,
    conv_b,
    w_x,
    w_dt,
    dt_bias,
    a_log,
    d_skip,
    w_out,
):
    tokens, model = output.shape
    mrows, double = w_in.shape
    inner = double // 2
    rows = w_out.shape[0]
    half = model // 2
    first = late_columns(model, proj, rank, taps, states)[0]

    output[...] = made[...]
    grad_x[...] = made_grad[...]
    w_mod[...] = made_w_mod[...]
    b_mod[...] = made_b_mod[...]
    w_out[...] = share_early[0:rows, 0:model]
    for i in range(2):
        low = share_late[:, first + i * half : first + (i + 1) * half]
        high = share_early[:, model + i * half : model + (i + 1) * half]
        for at, both in ((i * model, low), (inner + i * model, high)):
            w_in[:, at : at + half] = both[0:mrows]
            w_in[:, at + half : at + model] = both[mrows : 2 * mrows]

    flipped = share_late[:, 0:first].T
    for d in range(2):
        at = d * first // 2
        w_x[d] = share_late[0:rows, at : at + proj]
        w_dt[d] = flipped[at + proj : at + proj + rank, 0:rows]
    flipped = share_late[:, first + model :].T
    for d in range(2):
        conv_w[d] = flipped[d * taps : (d + 1) * taps, 0:rows]
    at = 2 * taps
    conv_b[...] = flipped[at : at + 2, 0:rows]
    dt_bias[...] = flipped[at + 2 : at + 4, 0:rows]
    d_skip[...] = flipped[at + 4 : at + 6, 0:rows]
    at = at + 8
    for d in range(2):
        a_log[d] = flipped[at + d * states : at + (d + 1) * states, 0:rows]


def on_device(
    count,
    hidden,
    condition,
    seq_lengths,
    w_mod,
    b_mod,
    w_in,
    conv_w,
    conv_b,
    w_x,
    w_dt,
    dt_bias,
    a_log,
    d_skip,
    w_out,
    grad_out,
):
    tokens, model = hidden.shape
    inner = w_in.shape[1] // 2
    rank = w_dt.shape[1]
    proj = w_x.shape[2]
    states = a_log.shape[1]
    taps = conv_w.shape[1]
    rows, mrows = inner // count, model // count
    given = types.SimpleNamespace(
        lengths=seq_lengths,
        hidden=hidden,
        condition=condition,
        b_mod=b_mod.reshape(-1, LANES),
        conv_w=conv_w,
        conv_b=conv_b,
        dt_bias=dt_bias,
        d_skip=d_skip,
        a_log=a_log,
        grad_out=grad_out,
    )
    weights = (w_mod, w_in, w_out, jnp.swapaxes(w_x, 1, 2), w_dt)
    output, grad_x, w_mod_share, b_mod_share, share_early, share_late = run_block(
        count, given, weights
    )
    results = pl.pallas_call(
        functools.partial(finish_kernel, count, proj, rank, taps, states),
        in_specs=[VMEM] * 6,
        out_specs=[VMEM] * 13,
        out_shape=[
            shaped((tokens, model), BF16),
            shaped((tokens, model)),
            shaped((mrows, 3 * model)),
            shaped((1, 3 * model // count)),
            shaped((mrows, 2 * inner)),
            shaped((2, taps, rows)),
            shaped((2, rows)),
            shaped((2, rows, proj)),
            shaped((2, rank, rows)),
            shaped((2, rows)),
            shaped((2, states, rows)),
            shaped((2, rows)),
            shaped((rows, model)),
        ],
        compiler_params=pltpu.CompilerParams(vmem_limit_bytes=60 * MIB),
        name="finish",
    )(share_early, share_late, output, grad_x, w_mod_share, b_mod_share)
    return tuple(results[:3]) + (results[3].reshape(-1),) + tuple(results[4:])


def solution(mesh):
    in_specs = (P("seq", None),) + (P(),) * 13 + (P("seq", None),)
    out_specs = (
        P("seq", None),
        P("seq", None),
        P("seq", None),
        P("seq"),
        P("seq", None),
        P(None, None, "seq"),
        P(None, "seq"),
        P(None, "seq", None),
        P(None, None, "seq"),
        P(None, "seq"),
        P(None, None, "seq"),
        P(None, "seq"),
        P("seq", None),
    )
    return jax.shard_map(
        functools.partial(on_device, mesh.shape["seq"]),
        mesh=mesh,
        in_specs=in_specs,
        out_specs=out_specs,
        check_vma=False,
    )
```
